32 devices in a mesh: section: 2 (over core), dp: 16 (over z, y, x).
Axes of the slice: x: 2, y: 2, z: 4, core: 2. Of those that a mesh axis runs over, the one named last changes fastest.
Arguments:
- canvases: bfloat16 [2, 128, 96, 2048], P('section', 'dp')
- crop_starts: int32 [2, 4], replicated, may hold values from 0 to 95, as said below
- pixel_mask: int32 [2, 128, 96], P(None, 'dp'), may hold values from 0 to 1, as said below
- drop_bits: int32 [2, 128, 96, 2048], P(None, 'dp'), may hold values from 0 to 1023
- reduce_weight: bfloat16 [2, 2048, 512], P('section'), may hold values from -0.125 to 0.125
- spatial_weight: bfloat16 [2, 9, 512, 512], P('section'), may hold values from -0.09375 to 0.09375
- expand_weight: bfloat16 [2, 512, 2048], P('section'), may hold values from -0.25 to 0.25
- inner_gain: float32 [2, 2, 512], P('section'), may hold values from 0.25 to 1.75
- inner_bias: float32 [2, 2, 512], P('section'), may hold values from -3 to 3
- outer_gain: float32 [2, 2048], P('section'), may hold values from 0.25 to 1.75
- outer_bias: float32 [2, 2048], P('section'), may hold values from -3 to 3
- head_weight: bfloat16 [2048, 48], replicated, may hold values from -0.3984375 to 0.3984375
- head_bias: float32 [48], replicated, may hold values from -4 to 4
- head_cotangent: bfloat16 [2, 128, 96, 48], P(None, 'dp'), may hold values from -5 to 5
Outputs:
- heads: float32 [2, 128, 96, 48], P('section', 'dp')
- canvas_grad: bfloat16 [2, 128, 96, 2048], P('section', 'dp')
- reduce_grad: float32 [2, 2048, 512], P('section')
- spatial_grad: float32 [2, 9, 512, 512], P('section')
- expand_grad: float32 [2, 512, 2048], P('section')
- inner_gain_grad: float32 [2, 2, 512], P('section')
- inner_bias_grad: float32 [2, 2, 512], P('section')
- outer_gain_grad: float32 [2, 2048], P('section')
- outer_bias_grad: float32 [2, 2048], P('section')
- head_weight_grad: float32 [2048, 48], P('section')
- head_bias_grad: float32 [48], P('section')
The draws below stay inside these ranges and needn't reach their ends.
Inputs may be any that keep to these rules, and one draw needn't show every extreme that they name: crop_starts[b, 0] is 0 and each row strictly increases; crop k of canvas b spans all 128 rows and the columns from its start up to the next start, or up to 96. `pixel_mask`: column 0 of every canvas row is live.
All inputs are finite; a program needn't handle non-finite values.
Results may differ from the reference program's by a relative error of at most 0.015.
Values may be sent and summed in bfloat16 or wider, within the bound.
A program may use at most 320 MiB of HBM per device.

```python
import jax
import jax.numpy as jnp
from jax import lax

C = 2048
M = 512
TASKS = 3
HEAD_OUT = 16
MB = 2
CANVAS_W = 96
CROPS = 4
LAYERS = 2
CANVAS_H = 128
HEAD_COLS = 48


def draw_canvases(key, part):
    key = jax.random.fold_in(key, 11)
    first_key, second_key, third_key = jax.random.split(key, 3)
    shape = (MB, CANVAS_H, CANVAS_W, C)
    level = jax.random.uniform(second_key, (MB, CANVAS_H, CANVAS_W, 1), jnp.float32)
    offset = 1.2 * jax.random.normal(third_key, (MB, CANVAS_H, 1, C), jnp.float32)
    values = jax.random.normal(first_key, shape, jnp.float32) * 10.0 ** (level - 0.5) + offset
    return values.astype(jnp.bfloat16)


def draw_pixel_mask(key, part):
    key = jax.random.fold_in(key, 23)
    row_index = jnp.arange(CANVAS_H, dtype=jnp.int32)[None, :, None]
    col_index = jnp.arange(CANVAS_W, dtype=jnp.int32)[None, None, :]
    limit = 250 + 700 * row_index // max(CANVAS_H - 1, 1)
    rolled = jax.random.randint(key, (MB, CANVAS_H, CANVAS_W), 0, 1000, dtype=jnp.int32)
    return jnp.logical_or(rolled < limit, col_index == 0).astype(jnp.int32)


def draw_crop_starts(key, part):
    key = jax.random.fold_in(key, 37)
    batch_keys = jax.random.split(key, MB)
    starts = []
    for batch in range(MB):
        if batch == 0:
            order = jax.random.permutation(batch_keys[batch], CANVAS_W - 2).astype(jnp.int32) + 1
            cuts = jnp.sort(order[:CROPS - 2])
            cuts = jnp.concatenate([cuts, jnp.full((1,), CANVAS_W - 1, jnp.int32)])
        else:
            order = jax.random.permutation(batch_keys[batch], CANVAS_W - 1).astype(jnp.int32) + 1
            cuts = jnp.sort(order[:CROPS - 1])
        starts.append(jnp.concatenate([jnp.zeros((1,), jnp.int32), cuts]))
    return jnp.stack(starts)


def set_ends(values, rng, smallest, top_value):
    longest = values.shape.index(max(values.shape))
    spots = []
    for shift in (0, 1):
        where = [jax.random.randint(jax.random.fold_in(rng, axis), (), 0, length) for axis, length in enumerate(values.shape)]
        where[longest] = (where[longest] + shift) % values.shape[longest]
        spots.append(tuple(where))
    return values.at[spots[0]].set(smallest).at[spots[1]].set(top_value)


def steps_of(key, dims, cuts, least, largest):
    def one(dim, shards_of):
        steps = jax.random.uniform(jax.random.fold_in(jax.random.fold_in(key, 6), dim), (shards_of,), jnp.float32, least / len(cuts), largest / len(cuts))
        return jnp.repeat(jnp.exp(steps), dims[dim] // shards_of).reshape((-1,) + (1,) * (len(dims) - dim - 1))

    factor_of = one(*cuts[0])
    for cut in cuts[1:]:
        factor_of = factor_of * one(*cut)
    return factor_of


def normal_values(own_key, dims, deviation, most, pieces=(), kind=jnp.bfloat16):
    loudness = steps_of(own_key, dims, pieces, -0.22, 0.18) if pieces else 1.0
    array = jax.random.normal(own_key, dims, jnp.float32) * deviation * loudness
    return jnp.minimum(jnp.maximum(array, -most), most).astype(kind)


def setup_inputs(seed: int = 0) -> dict:
    splits = jax.random.split(jax.random.key(seed), 15)
    return {
        "canvases": draw_canvases(jax.random.fold_in(splits[14], 71), 0),
        "crop_starts": draw_crop_starts(jax.random.fold_in(splits[14], 71), 0),
        "pixel_mask": draw_pixel_mask(jax.random.fold_in(splits[14], 71), 0),
        "drop_bits": set_ends(jax.random.randint(splits[3], (MB, CANVAS_H, CANVAS_W, C), 0, 1024), jax.random.fold_in(splits[3], 1), 0, 1023).astype(jnp.int32),
        "reduce_weight": normal_values(splits[4], (LAYERS, C, M), C ** -0.5, 0.125, ((0, 2),)),
        "spatial_weight": normal_values(splits[5], (LAYERS, 9, M, M), (9 * M) ** -0.5, 0.09375, ((0, 2),)),
        "expand_weight": normal_values(splits[6], (LAYERS, M, C), M ** -0.5, 0.25, ((0, 2),)),
        "inner_gain": jnp.clip(1.0 + 0.15 * jax.random.normal(splits[7], (LAYERS, 2, M), jnp.float32), 0.25, 1.75),
        "inner_bias": normal_values(splits[8], (LAYERS, 2, M), 0.5, 3.0, ((0, 2),), jnp.float32),
        "outer_gain": jnp.clip(1.0 + 0.15 * jax.random.normal(splits[9], (LAYERS, C), jnp.float32), 0.25, 1.75),
        "outer_bias": normal_values(splits[10], (LAYERS, C), 0.5, 3.0, ((0, 2),), jnp.float32),
        "head_weight": normal_values(splits[11], (C, HEAD_COLS), 0.0625, 0.3984375),
        "head_bias": normal_values(splits[12], (HEAD_COLS,), 1.0, 4.0, (), jnp.float32),
        "head_cotangent": normal_values(splits[13], (MB, CANVAS_H, CANVAS_W, HEAD_COLS), 1.0, 5.0, ((1, 16),)),
    }


EPS = 1e-05
SOFT = 0.05
SHARP = 0.1
LEVELS = 1024.0
HIGH = lax.Precision.HIGHEST

@jax.custom_vjp
def low(v):
    return lax.optimization_barrier(v.astype(jnp.bfloat16)).astype(jnp.float32)

@jax.custom_vjp
def low_back(v):
    return v

def low_keep(v):
    return (low(v), None)

def low_pass(kept, grad):
    return (grad,)

def back_keep(v):
    return (v, None)

def back_low(kept, grad):
    return (low(grad),)
low.defvjp(low_keep, low_pass)
low_back.defvjp(back_keep, back_low)

def column_masks(starts, width):
    columns = jnp.arange(width, dtype=jnp.int32)
    crop = lax.optimization_barrier(jnp.sum((columns[:, None] >= starts[None, :].astype(jnp.int32)).astype(jnp.int32), axis=1))
    outside = jnp.full((1,), -1, jnp.int32)
    before = jnp.concatenate([outside, crop[:-1]])
    after = jnp.concatenate([crop[1:], outside])
    return [(before == crop).astype(jnp.float32), jnp.ones((width,), jnp.float32), (after == crop).astype(jnp.float32)]

def normalize(values, weights, count, gain, bias):
    mean = lax.optimization_barrier(jnp.sum(values * weights, axis=0)) / count
    spread = lax.optimization_barrier(jnp.sum(weights * (values - mean) ** 2, axis=0)) / count
    return gain * ((values - mean) * lax.rsqrt(spread + EPS)) + bias

def spatial(field, kernel, masks):
    height, width, inner = field.shape
    wide = jnp.pad(field, ((1, 1), (1, 1), (0, 0)))
    total = jnp.zeros((height * width, kernel.shape[2]), jnp.float32)
    for row_step in range(3):
        for col_step in range(3):
            piece = wide[row_step:row_step + height, col_step:col_step + width] * masks[col_step][None, :, None]
            total = total + jnp.dot(piece.reshape(height * width, inner), kernel[3 * row_step + col_step], precision=HIGH)
    return total

def block(inputs, kernels, weights, count, masks, height, width):
    reduce_kernel, spatial_kernel, expand_kernel, gain_in, bias_in, gain_out, bias_out = kernels
    inputs = low(low_back(inputs))
    first_map = low_back(jnp.dot(inputs, reduce_kernel, precision=HIGH))
    first_act = low(jax.nn.silu(normalize(first_map, weights, count, gain_in[0], bias_in[0])))
    second_map = low_back(spatial(first_act.reshape(height, width, -1), spatial_kernel, masks))
    second_act = low(jax.nn.silu(normalize(second_map, weights, count, gain_in[1], bias_in[1])))
    third_map = low_back(jnp.dot(second_act, expand_kernel, precision=HIGH))
    return jax.nn.silu(normalize(third_map, weights, count, gain_out, bias_out) + inputs)

def graddrop(task_grads, bits):
    soft = [jnp.sqrt(value * value + SOFT * SOFT) for value in task_grads]
    signed = task_grads[0]
    magnitude = soft[0]
    for index in range(1, len(task_grads)):
        signed = signed + task_grads[index]
        magnitude = magnitude + soft[index]
    purity = 0.5 * (1.0 + signed / magnitude)
    level = (bits.astype(jnp.float32) + 0.5) / LEVELS
    keep = jax.nn.sigmoid((purity - level) / SHARP)
    merged = jnp.zeros_like(purity)
    for value, scale in zip(task_grads, soft):
        upward = 0.5 * (1.0 + value / scale)
        merged = merged + value * (keep * upward + (1.0 - keep) * (1.0 - upward))
    return merged

def reference(canvases, crop_starts, pixel_mask, drop_bits, reduce_weight, spatial_weight, expand_weight, inner_gain, inner_bias, outer_gain, outer_bias, head_weight, head_bias, head_cotangent):
    params = (reduce_weight.astype(jnp.float32), spatial_weight.astype(jnp.float32), expand_weight.astype(jnp.float32), inner_gain, inner_bias, outer_gain, outer_bias)
    head_matrix = head_weight.astype(jnp.float32)
    columns = jnp.arange(HEAD_COLS, dtype=jnp.int32) // HEAD_OUT
    pixels = CANVAS_H * CANVAS_W
    param_grads = jax.tree.map(jnp.zeros_like, params)
    head_w_grad = jnp.zeros_like(head_matrix)
    head_b_grad = jnp.zeros_like(head_bias)
    heads_all = []
    input_grads = []
    for batch in range(MB):
        weights = pixel_mask[batch].reshape(pixels, 1).astype(jnp.float32)
        count = jnp.sum(weights)
        masks = column_masks(crop_starts[batch], CANVAS_W)

        def trunk(inputs, kernels):
            hidden = inputs
            for layer in range(LAYERS):
                hidden = block(hidden, tuple((tensor[layer] for tensor in kernels)), weights, count, masks, CANVAS_H, CANVAS_W)
            return hidden
        feature, trunk_back = jax.vjp(trunk, canvases[batch].reshape(pixels, C).astype(jnp.float32), params)

        def heads_fn(inputs, matrix, bias):
            return jnp.dot(low(inputs), matrix, precision=HIGH) + bias
        heads, heads_back = jax.vjp(heads_fn, feature, head_matrix, head_bias)
        target = head_cotangent[batch].reshape(pixels, HEAD_COLS).astype(jnp.float32) * weights
        unused, weight_part, bias_part = heads_back(target)
        task_grads = [heads_back(target * (columns == task).astype(jnp.float32)[None, :])[0] for task in range(TASKS)]
        merged = graddrop(task_grads, drop_bits[batch].reshape(pixels, C))
        input_grad, kernel_grads = trunk_back(merged)
        param_grads = jax.tree.map(lambda total, part: total + part, param_grads, kernel_grads)
        head_w_grad = head_w_grad + weight_part
        head_b_grad = head_b_grad + bias_part
        heads_all.append(heads.reshape(CANVAS_H, CANVAS_W, HEAD_COLS))
        input_grads.append(input_grad.reshape(CANVAS_H, CANVAS_W, C).astype(jnp.bfloat16))
    return (jnp.stack(heads_all), jnp.stack(input_grads), param_grads[0], param_grads[1], param_grads[2], param_grads[3], param_grads[4], param_grads[5], param_grads[6], head_w_grad, head_b_grad)
```

```python
import functools
import math

import jax
import jax.numpy as jnp
from jax import lax
from jax.experimental import pallas as pl
from jax.experimental.pallas import tpu as pltpu
from jax.sharding import PartitionSpec as P

TASKS = 3
HEAD_OUT = 16

EPS = 1e-05
SOFT = 0.05
SHARP = 0.1
LEVELS = 1024.0
ACROSS = (((0,), (0,)), ((), ()))
BESIDE = (((1,), (1,)), ((), ()))
MESH = pl.DeviceIdType.MESH
TILE = 512
LIMIT = 56 * 2**20


def grid_of(size):
    side = math.isqrt(size // 4)
    assert side * side * 4 == size
    return (4, side, side)


def greet_all(size):
    section, me = lax.axis_index("section"), lax.axis_index("dp")
    barrier = pltpu.get_barrier_semaphore()
    for step in range(1, size):
        pl.semaphore_signal(
            barrier, inc=1, device_id=(section, lax.rem(me + step, size)), device_id_type=MESH
        )
    pl.semaphore_wait(barrier, size - 1)


def gather_kernel(size, x_ref, o_ref, send_sem, recv_sem):
    section, me = lax.axis_index("section"), lax.axis_index("dp")
    greet_all(size)
    o_ref[0] = x_ref[...]
    copies = []
    for step in range(1, size):
        copy = pltpu.make_async_remote_copy(
            src_ref=x_ref,
            dst_ref=o_ref.at[step],
            send_sem=send_sem.at[step],
            recv_sem=recv_sem.at[step],
            device_id=(section, lax.rem(me + step, size)),
            device_id_type=MESH,
        )
        copy.start()
        copies.append(copy)
    for copy in copies:
        copy.wait()


def gather_stats(values, collective):
    size = lax.axis_size("dp")
    return pl.pallas_call(
        functools.partial(gather_kernel, size),
        out_shape=jax.ShapeDtypeStruct((size,) + values.shape, values.dtype),
        in_specs=[pl.BlockSpec(memory_space=pltpu.VMEM)],
        out_specs=pl.BlockSpec(memory_space=pltpu.VMEM),
        scratch_shapes=[
            pltpu.SemaphoreType.DMA((size,)),
            pltpu.SemaphoreType.DMA((size,)),
        ],
        compiler_params=pltpu.CompilerParams(collective_id=collective, has_side_effects=True),
    )(values)


class Reducer:
    STAGES = 9
    RING = 4

    def __init__(self, size, groups):
        self.size = size
        self.groups = groups
        self.nz, self.ny, self.nx = grid_of(size)
        self.half = TILE // 2
        self.cols = TILE // self.nx
        self.yrows = self.half // self.ny
        self.zrows = self.yrows // self.nz

    def scratch(self):
        nx, ny, nz, groups, cols = self.nx, self.ny, self.nz, self.groups, self.cols
        bf16 = jnp.bfloat16
        return [
            pltpu.VMEM((3 * self.RING, nx, self.half, cols), bf16),
            pltpu.VMEM((3 * groups, nx, self.half, cols), bf16),
            pltpu.VMEM((3 * groups, nx, self.half, cols), bf16),
            pltpu.VMEM((2 * groups, nx - 1, self.half, cols), bf16),
            pltpu.VMEM((2 * groups, ny - 1, self.yrows, cols), bf16),
            pltpu.VMEM((2 * groups, nz - 1, self.zrows, cols), bf16),
            pltpu.VMEM((groups, ny - 1, nx, self.yrows, cols), bf16),
            pltpu.VMEM((groups, nz - 1, nx, self.zrows, cols), bf16),
            pltpu.VMEM((groups, nx - 1, self.zrows, cols), bf16),
            pltpu.SemaphoreType.DMA((3 * groups, 2)),
            pltpu.SemaphoreType.DMA((3 * groups, 2)),
            pltpu.SemaphoreType.DMA((3 * groups, 2 * (nx + ny + nz - 3))),
            pltpu.SemaphoreType.DMA((3 * groups, 2 * (nx + ny + nz - 3))),
        ]

    def bind(self, parts, total, scratch):
        self.parts, self.total = parts, total
        (
            self.ring,
            self.res,
            self.sec,
            self.ax,
            self.ay,
            self.az,
            self.by,
            self.bz,
            self.bx,
            self.pair_send,
            self.pair_recv,
            self.send_sem,
            self.recv_sem,
        ) = scratch
        self.section, self.me = lax.axis_index("section"), lax.axis_index("dp")
        plane = self.ny * self.nx
        self.z = self.me // plane
        self.y = (self.me // self.nx) % self.ny
        self.x = self.me % self.nx

    def peers(self):
        found = [(1 - self.section, self.me)]
        for axis in "xyz":
            for step in range(1, self.count(axis)):
                found.append((self.section, self.other(axis, step)[0]))
        return found

    def greet(self):
        barrier = pltpu.get_barrier_semaphore()
        peers = self.peers()
        for peer in peers:
            pl.semaphore_signal(barrier, inc=1, device_id=peer, device_id_type=MESH)
        pl.semaphore_wait(barrier, len(peers))

    def count(self, axis):
        return {"x": self.nx, "y": self.ny, "z": self.nz}[axis]

    def other(self, axis, step):
        plane = self.ny * self.nx
        if axis == "x":
            place = (self.x + step) % self.nx
            return self.z * plane + self.y * self.nx + place, place
        if axis == "y":
            place = (self.y + step) % self.ny
            return self.z * plane + place * self.nx + self.x, place
        place = (self.z + step) % self.nz
        return place * plane + self.y * self.nx + self.x, place

    def sem(self, axis, back, step):
        base = {"x": 0, "y": self.nx - 1, "z": self.nx + self.ny - 2}[axis]
        return base + (step - 1) + (self.nx + self.ny + self.nz - 3 if back else 0)

    def acc(self, tile):
        return self.ring.at[lax.rem(tile, 3 * self.RING)]

    def block(self, base, x, y, z):
        xs = slice(None) if x is None else x
        if y is None:
            return base.at[xs]
        if z is None:
            return base.at[xs, pl.ds(pl.multiple_of(y * self.yrows, 16), self.yrows)]
        start = pl.multiple_of(y * self.yrows + z * self.zrows, 16)
        return base.at[xs, pl.ds(start, self.zrows)]

    def spread(self, tile, axis, back, source, target):
        copies = []
        for step in range(1, self.count(axis)):
            device, place = self.other(axis, step)
            index = self.sem(axis, back, step)
            copies.append(
                pltpu.make_async_remote_copy(
                    src_ref=source(place),
                    dst_ref=target(step),
                    send_sem=self.send_sem.at[tile, index],
                    recv_sem=self.recv_sem.at[tile, index],
                    device_id=(self.section, device),
                    device_id_type=MESH,
                )
            )
        return copies

    def add(self, ref, extra, target=None):
        total = ref[...].astype(jnp.float32)
        for one in extra:
            total = total + one[...].astype(jnp.float32)
        target = ref if target is None else target
        target[...] = total.astype(jnp.bfloat16)

    def order(self, slot):
        return "xyz" if slot < 2 else "yzx"

    def landing(self, group, slot, axis):
        if slot < 2:
            row = 2 * group + slot
            return {"x": self.ax, "y": self.ay, "z": self.az}[axis].at[row]
        return {"x": self.bx, "y": self.by, "z": self.bz}[axis].at[group]

    def where(self, done, extra=None):
        place = {"x": None, "y": None, "z": None}
        for axis in done:
            place[axis] = {"x": self.x, "y": self.y, "z": self.z}[axis]
        place.update(extra or {})
        return place

    def part(self, base, done, extra=None):
        place = self.where(done, extra)
        return self.block(base, place["x"], place["y"], place["z"])

    def half_rows(self, which):
        return pl.ds(pl.multiple_of(which * self.half, 16), self.half)

    def pair(self, tile):
        own = pltpu.make_async_copy(
            self.parts.at[tile, :, self.half_rows(self.section)],
            self.acc(tile),
            self.pair_send.at[tile, 0],
        )
        away = pltpu.make_async_remote_copy(
            src_ref=self.parts.at[tile, :, self.half_rows(1 - self.section)],
            dst_ref=self.sec.at[tile],
            send_sem=self.pair_send.at[tile, 1],
            recv_sem=self.pair_recv.at[tile, 0],
            device_id=(1 - self.section, self.me),
            device_id_type=MESH,
        )
        return own, away

    def scatter(self, group, slot, level):
        tile = 3 * group + slot
        order = self.order(slot)
        axis, done = order[level], order[:level]
        landing = self.landing(group, slot, axis)
        return self.spread(
            tile,
            axis,
            False,
            lambda place: self.part(self.acc(tile), done, {axis: place}),
            lambda step: landing.at[step - 1],
        )

    def scattered(self, group, slot, level):
        tile = 3 * group + slot
        order = self.order(slot)
        axis, done = order[level], order[: level + 1]
        landing = self.landing(group, slot, axis)
        steps = range(1, self.count(axis))
        for copy in self.scatter(group, slot, level):
            copy.wait()
        target = self.part(self.res.at[tile], done) if level == 2 else None
        self.add(self.part(self.acc(tile), done), [landing.at[step - 1] for step in steps], target)

    def gather(self, group, slot, level):
        tile = 3 * group + slot
        order = self.order(slot)
        axis, done = order[level], order[: level + 1]
        ref = self.part(self.res.at[tile], done)
        return self.spread(tile, axis, True, lambda place: ref, lambda step: ref)

    def gathered(self, group, slot, level):
        for copy in self.gather(group, slot, level):
            copy.wait()

    def final(self, group, slot):
        tile = 3 * group + slot
        block = 1 - (tile >= 3 * self.groups // 2).astype(jnp.int32)
        index = tile - (1 - block) * (3 * self.groups // 2)
        target = self.total.at[index, :, self.half_rows(self.section)]
        here = pltpu.make_async_copy(self.res.at[tile], target, self.pair_send.at[tile, 0])
        away = pltpu.make_async_remote_copy(
            src_ref=self.res.at[tile],
            dst_ref=target,
            send_sem=self.pair_send.at[tile, 0],
            recv_sem=self.pair_recv.at[tile, 1],
            device_id=(1 - self.section, self.me),
            device_id_type=MESH,
        )
        return block == self.section, here, away

    def stage(self, number, group):
        for slot in range(3):
            tile = 3 * group + slot
            if number == 0:
                for copy in self.pair(tile):
                    copy.start()
            elif number == 1:
                for copy in self.pair(tile):
                    copy.wait()
                self.add(self.acc(tile), [self.sec.at[tile]])
                for copy in self.scatter(group, slot, 0):
                    copy.start()
            elif number in (2, 3):
                self.scattered(group, slot, number - 2)
                for copy in self.scatter(group, slot, number - 1):
                    copy.start()
            elif number == 4:
                self.scattered(group, slot, 2)
                for copy in self.gather(group, slot, 2):
                    copy.start()
            elif number in (5, 6):
                self.gathered(group, slot, 7 - number)
                for copy in self.gather(group, slot, 6 - number):
                    copy.start()
            elif number == 7:
                self.gathered(group, slot, 0)
                mine, here, away = self.final(group, slot)
                pl.when(mine)(here.start)
                pl.when(jnp.logical_not(mine))(away.start)
            else:
                mine, here, away = self.final(group, slot)

                @pl.when(mine)
                def _():
                    here.wait()
                    away.wait_recv()

                pl.when(jnp.logical_not(mine))(away.wait_send)

    def tick(self, time):
        for number in reversed(range(self.STAGES)):
            group = time - number
            pl.when(jnp.logical_and(group >= 0, group < self.groups))(
                functools.partial(self.stage, number, group)
            )


def reduce_kernel(size, groups, parts, total, *scratch):
    reducer = Reducer(size, groups)
    reducer.bind(parts, total, scratch)
    reducer.greet()

    @pl.loop(0, groups + reducer.STAGES - 1)
    def _(time):
        reducer.tick(time)


def reduce_tiles(parts):
    size = lax.axis_size("dp")
    groups = parts.shape[0] // 3
    reducer = Reducer(size, groups)
    return pl.pallas_call(
        functools.partial(reduce_kernel, size, groups),
        out_shape=jax.ShapeDtypeStruct((parts.shape[0] // 2,) + parts.shape[1:], parts.dtype),
        in_specs=[pl.BlockSpec(memory_space=pl.ANY)],
        out_specs=pl.BlockSpec(memory_space=pl.ANY),
        scratch_shapes=reducer.scratch(),
        compiler_params=pltpu.CompilerParams(
            collective_id=0, has_side_effects=True, vmem_limit_bytes=LIMIT
        ),
    )(parts)


def extended(x):
    size, length = lax.axis_size("dp"), x.shape[0]
    up = [(i, (i + 1) % size) for i in range(size - 1)]
    down = [(j, i) for i, j in up]
    before = lax.ppermute(lax.slice_in_dim(x, length - 1, length), "dp", up)
    after = lax.ppermute(lax.slice_in_dim(x, 0, 1), "dp", down)
    return jnp.concatenate([before, x, after], axis=0)


def silu_slope(values):
    sigma = jax.nn.sigmoid(values)
    return sigma * (1.0 + values * (1.0 - sigma))


def column_masks(starts, width):
    columns = jnp.arange(width, dtype=jnp.int32)
    crop = jnp.sum((columns[:, None] >= starts[None, :]).astype(jnp.int32), axis=1)
    outside = jnp.full((1,), -1, jnp.int32)
    before = jnp.concatenate([outside, crop[:-1]])
    after = jnp.concatenate([crop[1:], outside])
    return [
        (before == crop).astype(jnp.bfloat16),
        jnp.ones((width,), jnp.bfloat16),
        (after == crop).astype(jnp.bfloat16),
    ]


def patches(padded, masks, sign):
    rows = padded.shape[0] - 2
    width = padded.shape[1]
    wide = jnp.pad(padded, ((0, 0), (1, 1), (0, 0)))
    blocks = []
    for row_step in range(3):
        for col_step in range(3):
            top = 1 + sign * (row_step - 1)
            left = 1 + sign * (col_step - 1)
            piece = wide[top : top + rows, left : left + width]
            if col_step != 1:
                piece = piece * masks[1 + sign * (col_step - 1)][None, :, None]
            blocks.append(piece)
    return jnp.concatenate(blocks, axis=2).reshape(rows * width, -1)


def pick(array, index):
    return lax.dynamic_index_in_dim(array, index, 0, keepdims=False)


def norm_forward(values, weights, local_count):
    total = jnp.sum(values * weights, axis=0)
    centered = values - total / local_count
    spread = jnp.sum(weights * centered * centered, axis=0)
    counts = jnp.full_like(total, local_count)
    parts = gather_stats(jnp.stack([total, spread, counts]), 1 if total.shape[0] == TILE else 2)
    totals, spreads, counts = parts[:, 0], parts[:, 1], parts[:, 2]
    count = jnp.sum(counts[:, 0])
    mean = jnp.sum(totals, axis=0) / count
    apart = totals / counts - mean
    variance = (jnp.sum(spreads, axis=0) + jnp.sum(counts * apart * apart, axis=0)) / count
    scale = lax.rsqrt(variance + EPS)
    return ((values - mean) * scale, scale, count)


def norm_backward(upstream, normed, weights, count, gain, scale):
    local = jnp.stack([jnp.sum(upstream, axis=0), jnp.sum(upstream * normed, axis=0)])
    sums = jnp.sum(gather_stats(local, 3 if local.shape[1] == TILE else 4), axis=0)
    bias_sum, gain_sum = sums[0], sums[1]
    result = scale * gain * (upstream - weights * (bias_sum + normed * gain_sum) / count)
    return (result, gain_sum, bias_sum)


def graddrop(task_grads, bits):
    soft = [jnp.sqrt(value * value + SOFT * SOFT) for value in task_grads]
    signed = task_grads[0]
    magnitude = soft[0]
    for index in range(1, len(task_grads)):
        signed = signed + task_grads[index]
        magnitude = magnitude + soft[index]
    purity = 0.5 * (1.0 + signed / magnitude)
    level = (bits.astype(jnp.float32) + 0.5) / LEVELS
    keep = jax.nn.sigmoid((purity - level) / SHARP)
    merged = jnp.zeros_like(purity)
    for value, scale in zip(task_grads, soft):
        upward = 0.5 * (1.0 + value / scale)
        merged = merged + value * (keep * upward + (1.0 - keep) * (1.0 - upward))
    return merged


def layer_forward(layer_in, params, weights, masks):
    reduce_kernel, spatial, expand_kernel, gain_in, bias_in, gain_out, bias_out = params
    rows, width, channels = layer_in.shape
    flat_in = layer_in.reshape(rows * width, channels)
    local_count = jnp.sum(weights)
    first_map = jnp.dot(flat_in, reduce_kernel, preferred_element_type=jnp.float32)
    normed_a, scale_a, count = norm_forward(first_map, weights, local_count)
    act_a = jax.nn.silu(gain_in[0] * normed_a + bias_in[0]).astype(jnp.bfloat16)
    padded = extended(act_a.reshape(rows, width, -1))
    flat = spatial.reshape(-1, spatial.shape[2])
    second_map = jnp.dot(patches(padded, masks, 1), flat, preferred_element_type=jnp.float32)
    normed_b, scale_b, count = norm_forward(second_map, weights, local_count)
    act_b = jax.nn.silu(gain_in[1] * normed_b + bias_in[1]).astype(jnp.bfloat16)
    third_map = jnp.dot(act_b, expand_kernel, preferred_element_type=jnp.float32)
    normed_c, scale_c, count = norm_forward(third_map, weights, local_count)
    output = jax.nn.silu(gain_out * normed_c + bias_out + flat_in.astype(jnp.float32))
    return (
        output,
        (flat_in, normed_a, scale_a, padded, normed_b, scale_b, normed_c, scale_c, count),
    )


def layer_backward(grad_out, kept, params, weights, masks):
    reduce_kernel, spatial, expand_kernel, gain_in, bias_in, gain_out, bias_out = params
    flat_in, normed_a, scale_a, padded, normed_b, scale_b, normed_c, scale_c, count = kept
    rows, width = (padded.shape[0] - 2, padded.shape[1])
    grad_t = grad_out * silu_slope(gain_out * normed_c + bias_out + flat_in.astype(jnp.float32))
    grad_c, gain_c, bias_c = norm_backward(grad_t, normed_c, weights, count, gain_out, scale_c)
    grad_c = grad_c.astype(jnp.bfloat16)
    affine_b = gain_in[1] * normed_b + bias_in[1]
    act_b = jax.nn.silu(affine_b).astype(jnp.bfloat16)
    expand_part = lax.dot_general(act_b, grad_c, ACROSS, preferred_element_type=jnp.float32)
    grad_act_b = lax.dot_general(grad_c, expand_kernel, BESIDE, preferred_element_type=jnp.float32)
    grad_b, gain_b, bias_b = norm_backward(
        grad_act_b * silu_slope(affine_b), normed_b, weights, count, gain_in[1], scale_b
    )
    grad_b = grad_b.astype(jnp.bfloat16)
    spatial_part = lax.dot_general(
        patches(padded, masks, 1), grad_b, ACROSS, preferred_element_type=jnp.float32
    )
    grad_pad = extended(grad_b.reshape(rows, width, -1))
    back = jnp.swapaxes(spatial, 1, 2).reshape(-1, spatial.shape[1])
    grad_act_a = jnp.dot(patches(grad_pad, masks, -1), back, preferred_element_type=jnp.float32)
    affine_a = gain_in[0] * normed_a + bias_in[0]
    grad_a, gain_a, bias_a = norm_backward(
        grad_act_a * silu_slope(affine_a), normed_a, weights, count, gain_in[0], scale_a
    )
    grad_a = grad_a.astype(jnp.bfloat16)
    reduce_part = lax.dot_general(flat_in, grad_a, ACROSS, preferred_element_type=jnp.float32)
    grad_in = (
        lax.dot_general(grad_a, reduce_kernel, BESIDE, preferred_element_type=jnp.float32) + grad_t
    )
    return (
        grad_in.astype(jnp.bfloat16),
        (reduce_part, spatial_part, expand_part),
        (gain_a, gain_b, bias_a, bias_b, gain_c, bias_c),
    )


def heads_step(feature, head_weight, head_bias, cotangent, weights, bits):
    heads = jnp.dot(feature, head_weight, preferred_element_type=jnp.float32) + head_bias
    target = cotangent * weights.astype(jnp.bfloat16)
    weight_part = lax.dot_general(target, feature, ACROSS, preferred_element_type=jnp.float32)
    bias_part = jnp.sum(target.astype(jnp.float32), axis=0)
    task_grads = []
    for task in range(TASKS):
        start = task * HEAD_OUT
        task_grads.append(
            lax.dot_general(
                target[:, start : start + HEAD_OUT],
                head_weight[:, start : start + HEAD_OUT],
                BESIDE,
                preferred_element_type=jnp.float32,
            )
        )
    return (heads, graddrop(task_grads, bits), weight_part, bias_part)


def tiles_of(kernel_parts, small, nx):
    reduce_part, spatial_part, expand_part = kernel_parts
    cols = TILE // nx

    def rows_first(x):
        x = x.astype(jnp.bfloat16).reshape(-1, TILE, nx, cols)
        return jnp.swapaxes(x, 1, 2)

    expand = expand_part.astype(jnp.bfloat16).reshape(TILE, -1, nx, cols)
    return jnp.concatenate(
        [
            jnp.transpose(expand, (1, 2, 0, 3)),
            rows_first(spatial_part),
            rows_first(reduce_part),
            rows_first(small),
        ]
    )


def local(
    canvases,
    crop_starts,
    pixel_mask,
    drop_bits,
    reduce_weight,
    spatial_weight,
    expand_weight,
    inner_gain,
    inner_bias,
    outer_gain,
    outer_bias,
    head_weight,
    head_bias,
    head_cotangent,
):
    section = lax.axis_index("section")
    first = section == 0
    rows, width, channels = canvases.shape[1:]
    inner = reduce_weight.shape[2]
    pixels = rows * width
    head_cols = head_weight.shape[1]
    swap = [(0, 1), (1, 0)]
    own = (
        reduce_weight[0],
        spatial_weight[0],
        expand_weight[0],
        inner_gain[0],
        inner_bias[0],
        outer_gain[0],
        outer_bias[0],
    )
    came = [lax.ppermute(x, "section", swap) for x in own]
    params = [
        [jnp.where(first, x, y) for x, y in zip(own, came)],
        [jnp.where(first, y, x) for x, y in zip(own, came)],
    ]
    weights = pick(pixel_mask, section).reshape(pixels, 1).astype(jnp.float32)
    masks = column_masks(pick(crop_starts, section), width)
    layer_in = canvases[0]
    saved = []
    for layer in range(2):
        output, kept = layer_forward(layer_in, params[layer], weights, masks)
        saved.append(kept)
        feature = output.astype(jnp.bfloat16)
        layer_in = feature.reshape(rows, width, channels)
    cotangent = pick(head_cotangent, section).reshape(pixels, head_cols)
    bits = pick(drop_bits, section).reshape(pixels, channels)
    heads, grad, head_part, head_bias_part = heads_step(
        feature, head_weight, head_bias, cotangent, weights, bits
    )
    only = lax.axis_index("dp") == 0
    nx = grid_of(lax.axis_size("dp"))[2]
    half = channels // 2
    tiles = []
    for layer in (1, 0):
        grad, kernel_parts, norm_parts = layer_backward(
            grad.astype(jnp.float32), saved[layer], params[layer], weights, masks
        )
        mine = head_part[:, layer * half : (layer + 1) * half].reshape(-1, inner)
        row = jnp.pad(head_bias_part, (0, inner - head_cols))[None]
        norms = jnp.concatenate([x.reshape(-1, inner) for x in norm_parts])
        small = jnp.concatenate([mine, row, jnp.where(only, norms, 0.0)])
        small = jnp.pad(small, ((0, TILE - small.shape[0]), (0, 0)))
        tiles.append(tiles_of(kernel_parts, small, nx))
    total = reduce_tiles(jnp.concatenate(tiles))
    total = jnp.swapaxes(total, 1, 2).reshape(-1, TILE, TILE).astype(jnp.float32)
    across = channels // TILE
    taps = spatial_weight.shape[1]
    expand_total = jnp.swapaxes(total[:across], 0, 1).reshape(inner, channels)
    spatial_total = total[across : across + taps]
    reduce_total = total[across + taps : 2 * across + taps].reshape(channels, inner)
    small = total[-1]
    count = head_cols * half // inner
    head_w_out = small[:count].reshape(head_cols, half).T
    cut = head_cols // 2
    head_b_out = jnp.where(first, small[count, :cut], small[count, cut:head_cols])
    norms = small[count + 1 :]
    return (
        heads.reshape(1, rows, width, head_cols),
        grad.reshape(1, rows, width, channels),
        reduce_total[None],
        spatial_total[None],
        expand_total[None],
        norms[0:2][None],
        norms[2:4][None],
        norms[4 : 4 + across].reshape(1, channels),
        norms[4 + across : 4 + 2 * across].reshape(1, channels),
        head_w_out,
        head_b_out,
    )


def solution(mesh):
    placed = (
        P("section", "dp", None, None),
        P(),
        P(None, "dp", None),
        P(None, "dp", None, None),
        P("section", None, None),
        P("section", None, None, None),
        P("section", None, None),
        P("section", None, None),
        P("section", None, None),
        P("section", None),
        P("section", None),
        P(),
        P(),
        P(None, "dp", None, None),
    )
    return jax.shard_map(
        local,
        mesh=mesh,
        in_specs=placed,
        out_specs=(
            P("section", "dp", None, None),
            P("section", "dp", None, None),
            P("section", None, None),
            P("section", None, None, None),
            P("section", None, None),
            P("section", None, None),
            P("section", None, None),
            P("section", None),
            P("section", None),
            P("section", None),
            P("section"),
        ),
        check_vma=False,
    )
```

```python
import functools
import math

import jax
import jax.numpy as jnp
from jax import lax
from jax.experimental import pallas as pl
from jax.experimental.pallas import tpu as pltpu
from jax.sharding import PartitionSpec as P

TASKS = 3
HEAD_OUT = 16

EPS = 1e-05
SOFT = 0.05
SHARP = 0.1
LEVELS = 1024.0
ACROSS = (((0,), (0,)), ((), ()))
BESIDE = (((1,), (1,)), ((), ()))
MESH = pl.DeviceIdType.MESH
TILE = 512
LIMIT = 56 * 2**20


def grid_of(size):
    side = math.isqrt(size // 4)
    assert side * side * 4 == size
    return (4, side, side)


class Reducer:
    STAGES = 9
    RING = 4

    def __init__(self, size, groups):
        self.size = size
        self.groups = groups
        self.nz, self.ny, self.nx = grid_of(size)
        self.half = TILE // 2
        self.cols = TILE // self.nx
        self.yrows = self.half // self.ny
        self.zrows = self.yrows // self.nz

    def scratch(self):
        nx, ny, nz, groups, cols = self.nx, self.ny, self.nz, self.groups, self.cols
        bf16 = jnp.bfloat16
        return [
            pltpu.VMEM((3 * self.RING, self.half, TILE), bf16),
            pltpu.VMEM((3 * groups, self.half, TILE), bf16),
            pltpu.VMEM((3 * groups, self.half, TILE), bf16),
            pltpu.VMEM((2 * groups, nx - 1, self.half, cols), bf16),
            pltpu.VMEM((2 * groups, ny - 1, self.yrows, cols), bf16),
            pltpu.VMEM((2 * groups, nz - 1, self.zrows, cols), bf16),
            pltpu.VMEM((groups, ny - 1, self.yrows, TILE), bf16),
            pltpu.VMEM((groups, nz - 1, self.zrows, TILE), bf16),
            pltpu.VMEM((groups, nx - 1, self.zrows, cols), bf16),
            pltpu.SemaphoreType.DMA((3 * groups, 2)),
            pltpu.SemaphoreType.DMA((3 * groups, 2)),
            pltpu.SemaphoreType.DMA((3 * groups, 2 * (nx + ny + nz - 3))),
            pltpu.SemaphoreType.DMA((3 * groups, 2 * (nx + ny + nz - 3))),
        ]

    def bind(self, parts, total, scratch):
        self.parts, self.total = parts, total
        (
            self.ring,
            self.res,
            self.sec,
            self.ax,
            self.ay,
            self.az,
            self.by,
            self.bz,
            self.bx,
            self.pair_send,
            self.pair_recv,
            self.send_sem,
            self.recv_sem,
        ) = scratch
        self.section, self.me = lax.axis_index("section"), lax.axis_index("dp")
        plane = self.ny * self.nx
        self.z = self.me // plane
        self.y = (self.me // self.nx) % self.ny
        self.x = self.me % self.nx

    def peers(self):
        found = [(1 - self.section, self.me)]
        for axis in "xyz":
            for step in range(1, self.count(axis)):
                found.append((self.section, self.other(axis, step)[0]))
        return found

    def greet(self):
        barrier = pltpu.get_barrier_semaphore()
        peers = self.peers()
        for peer in peers:
            pl.semaphore_signal(barrier, inc=1, device_id=peer, device_id_type=MESH)
        pl.semaphore_wait(barrier, len(peers))

    def count(self, axis):
        return {"x": self.nx, "y": self.ny, "z": self.nz}[axis]

    def other(self, axis, step):
        plane = self.ny * self.nx
        if axis == "x":
            place = (self.x + step) % self.nx
            return self.z * plane + self.y * self.nx + place, place
        if axis == "y":
            place = (self.y + step) % self.ny
            return self.z * plane + place * self.nx + self.x, place
        place = (self.z + step) % self.nz
        return place * plane + self.y * self.nx + self.x, place

    def sem(self, axis, back, step):
        base = {"x": 0, "y": self.nx - 1, "z": self.nx + self.ny - 2}[axis]
        return base + (step - 1) + (self.nx + self.ny + self.nz - 3 if back else 0)

    def acc(self, tile):
        return self.ring.at[lax.rem(tile, 3 * self.RING)]

    def block(self, base, x, y, z):
        if y is None:
            lines = slice(None)
        elif z is None:
            lines = pl.ds(pl.multiple_of(y * self.yrows, 16), self.yrows)
        else:
            lines = pl.ds(pl.multiple_of(y * self.yrows + z * self.zrows, 16), self.zrows)
        if x is None:
            return base.at[lines]
        return base.at[lines, pl.ds(pl.multiple_of(x * self.cols, self.cols), self.cols)]

    def spread(self, tile, axis, back, source, target):
        copies = []
        for step in range(1, self.count(axis)):
            device, place = self.other(axis, step)
            index = self.sem(axis, back, step)
            copies.append(
                pltpu.make_async_remote_copy(
                    src_ref=source(place),
                    dst_ref=target(step),
                    send_sem=self.send_sem.at[tile, index],
                    recv_sem=self.recv_sem.at[tile, index],
                    device_id=(self.section, device),
                    device_id_type=MESH,
                )
            )
        return copies

    def add(self, ref, extra, target=None):
        total = ref[...].astype(jnp.float32)
        for one in extra:
            total = total + one[...].astype(jnp.float32)
        target = ref if target is None else target
        target[...] = total.astype(jnp.bfloat16)

    def order(self, slot):
        return "xyz" if slot < 2 else "yzx"

    def landing(self, group, slot, axis):
        if slot < 2:
            row = 2 * group + slot
            return {"x": self.ax, "y": self.ay, "z": self.az}[axis].at[row]
        return {"x": self.bx, "y": self.by, "z": self.bz}[axis].at[group]

    def where(self, done, extra=None):
        place = {"x": None, "y": None, "z": None}
        for axis in done:
            place[axis] = {"x": self.x, "y": self.y, "z": self.z}[axis]
        place.update(extra or {})
        return place

    def part(self, base, done, extra=None):
        place = self.where(done, extra)
        return self.block(base, place["x"], place["y"], place["z"])

    def half_rows(self, which):
        return pl.ds(pl.multiple_of(which * self.half, 16), self.half)

    def pair(self, tile):
        own = pltpu.make_async_copy(
            self.parts.at[tile, self.half_rows(self.section)],
            self.acc(tile),
            self.pair_send.at[tile, 0],
        )
        away = pltpu.make_async_remote_copy(
            src_ref=self.parts.at[tile, self.half_rows(1 - self.section)],
            dst_ref=self.sec.at[tile],
            send_sem=self.pair_send.at[tile, 1],
            recv_sem=self.pair_recv.at[tile, 0],
            device_id=(1 - self.section, self.me),
            device_id_type=MESH,
        )
        return own, away

    def scatter(self, group, slot, level):
        tile = 3 * group + slot
        order = self.order(slot)
        axis, done = order[level], order[:level]
        landing = self.landing(group, slot, axis)
        return self.spread(
            tile,
            axis,
            False,
            lambda place: self.part(self.acc(tile), done, {axis: place}),
            lambda step: landing.at[step - 1],
        )

    def scattered(self, group, slot, level):
        tile = 3 * group + slot
        order = self.order(slot)
        axis, done = order[level], order[: level + 1]
        landing = self.landing(group, slot, axis)
        steps = range(1, self.count(axis))
        for copy in self.scatter(group, slot, level):
            copy.wait()
        target = self.part(self.res.at[tile], done) if level == 2 else None
        self.add(self.part(self.acc(tile), done), [landing.at[step - 1] for step in steps], target)

    def gather(self, group, slot, level):
        tile = 3 * group + slot
        order = self.order(slot)
        axis, done = order[level], order[: level + 1]
        ref = self.part(self.res.at[tile], done)
        return self.spread(tile, axis, True, lambda place: ref, lambda step: ref)

    def gathered(self, group, slot, level):
        for copy in self.gather(group, slot, level):
            copy.wait()

    def places(self, index):
        expand, spatial, reduce, small = self.total
        across = expand.shape[1] // TILE
        half = self.half_rows(self.section)
        taps = spatial.shape[0]
        tile = index - across - taps
        lines = pl.multiple_of(tile * TILE + self.section * self.half, 16)
        return [
            (index < across, lambda: expand.at[half, pl.ds(pl.multiple_of(index * TILE, TILE), TILE)]),
            (
                jnp.logical_and(index >= across, index < across + taps),
                lambda: spatial.at[index - across, half],
            ),
            (
                jnp.logical_and(index >= across + taps, index < 2 * across + taps),
                lambda: reduce.at[pl.ds(lines, self.half)],
            ),
            (index == 2 * across + taps, lambda: small.at[half]),
        ]

    def final(self, tile, target):
        here = pltpu.make_async_copy(self.res.at[tile], target, self.pair_send.at[tile, 0])
        away = pltpu.make_async_remote_copy(
            src_ref=self.res.at[tile],
            dst_ref=target,
            send_sem=self.pair_send.at[tile, 0],
            recv_sem=self.pair_recv.at[tile, 1],
            device_id=(1 - self.section, self.me),
            device_id_type=MESH,
        )
        return here, away

    def finish(self, tile):
        later = (tile >= 3 * self.groups // 2).astype(jnp.int32)
        mine = self.section == 1 - later
        index = tile - later * (3 * self.groups // 2)
        for wanted, place in self.places(index):

            @pl.when(jnp.logical_and(wanted, mine))
            def _():
                self.final(tile, place())[0].start()

            @pl.when(jnp.logical_and(wanted, jnp.logical_not(mine)))
            def _():
                self.final(tile, place())[1].start()

    def finished(self, tile):
        later = (tile >= 3 * self.groups // 2).astype(jnp.int32)
        mine = self.section == 1 - later
        here, away = self.final(tile, self.total[3].at[self.half_rows(self.section)])

        @pl.when(mine)
        def _():
            here.wait()
            away.wait_recv()

        pl.when(jnp.logical_not(mine))(away.wait_send)

    def stage(self, number, group):
        for slot in range(3):
            tile = 3 * group + slot
            if number == 0:
                for copy in self.pair(tile):
                    copy.start()
            elif number == 1:
                for copy in self.pair(tile):
                    copy.wait()
                self.add(self.acc(tile), [self.sec.at[tile]])
                for copy in self.scatter(group, slot, 0):
                    copy.start()
            elif number in (2, 3):
                self.scattered(group, slot, number - 2)
                for copy in self.scatter(group, slot, number - 1):
                    copy.start()
            elif number == 4:
                self.scattered(group, slot, 2)
                for copy in self.gather(group, slot, 2):
                    copy.start()
            elif number in (5, 6):
                self.gathered(group, slot, 7 - number)
                for copy in self.gather(group, slot, 6 - number):
                    copy.start()
            elif number == 7:
                self.gathered(group, slot, 0)
                self.finish(tile)
            else:
                self.finished(tile)

    def tick(self, time):
        for number in reversed(range(self.STAGES)):
            group = time - number
            pl.when(jnp.logical_and(group >= 0, group < self.groups))(
                functools.partial(self.stage, number, group)
            )


def reduce_kernel(size, groups, parts, expand, spatial, reduce, small, *scratch):
    reducer = Reducer(size, groups)
    reducer.bind(parts, (expand, spatial, reduce, small), scratch)
    reducer.greet()

    @pl.loop(0, groups + reducer.STAGES - 1)
    def _(time):
        reducer.tick(time)


def reduce_tiles(parts, channels, taps):
    size = lax.axis_size("dp")
    groups = parts.shape[0] // 3
    reducer = Reducer(size, groups)
    shapes = [(TILE, channels), (taps, TILE, TILE), (channels, TILE), (TILE, TILE)]
    return pl.pallas_call(
        functools.partial(reduce_kernel, size, groups),
        out_shape=[jax.ShapeDtypeStruct(shape, parts.dtype) for shape in shapes],
        in_specs=[pl.BlockSpec(memory_space=pl.ANY)],
        out_specs=[pl.BlockSpec(memory_space=pl.ANY)] * 4,
        scratch_shapes=reducer.scratch(),
        compiler_params=pltpu.CompilerParams(
            collective_id=0, has_side_effects=True, vmem_limit_bytes=LIMIT
        ),
    )(parts)


def silu_parts(v):
    sigma = 1.0 / (1.0 + jnp.exp(-v))
    return v * sigma, sigma * (1.0 + v * (1.0 - sigma))


def folded(x):
    return jnp.sum(x.reshape(x.shape[0] // 8, 8, x.shape[1]), axis=0)


class Exchange:
    def __init__(self, size, send_sem, recv_sem, edge_send, edge_recv):
        self.size = size
        self.section, self.me = lax.axis_index("section"), lax.axis_index("dp")
        self.send_sem, self.recv_sem = send_sem, recv_sem
        self.edge_send, self.edge_recv = edge_send, edge_recv

    def greet(self):
        barrier = pltpu.get_barrier_semaphore()
        for step in range(1, self.size):
            peer = (self.section, lax.rem(self.me + step, self.size))
            pl.semaphore_signal(barrier, inc=1, device_id=peer, device_id_type=MESH)
        other = (1 - self.section, self.me)
        pl.semaphore_signal(barrier, inc=1, device_id=other, device_id_type=MESH)
        pl.semaphore_wait(barrier, self.size)

    def copies(self, number, slots):
        return [
            pltpu.make_async_remote_copy(
                src_ref=slots.at[0],
                dst_ref=slots.at[step],
                send_sem=self.send_sem.at[number, step],
                recv_sem=self.recv_sem.at[number, step],
                device_id=(self.section, lax.rem(self.me + step, self.size)),
                device_id_type=MESH,
            )
            for step in range(1, self.size)
        ]

    def edges(self, number, first, last, landing):
        made = []
        for way, (ref, step) in enumerate(((first, self.size - 1), (last, 1))):
            made.append(
                pltpu.make_async_remote_copy(
                    src_ref=ref,
                    dst_ref=landing.at[1 - way],
                    send_sem=self.edge_send.at[number, way],
                    recv_sem=self.edge_recv.at[number, 1 - way],
                    device_id=(self.section, lax.rem(self.me + step, self.size)),
                    device_id_type=MESH,
                )
            )
        return made

    def start_edges(self, number, first, last, landing):
        up, down = self.edges(number, first, last, landing)
        pl.when(self.me > 0)(up.start)
        pl.when(self.me < self.size - 1)(down.start)

    def wait_edges(self, number, first, last, landing):
        up, down = self.edges(number, first, last, landing)
        pl.when(self.me > 0)(up.wait_send)
        pl.when(self.me > 0)(down.wait_recv)
        pl.when(self.me < self.size - 1)(down.wait_send)
        pl.when(self.me < self.size - 1)(up.wait_recv)


def forward_kernel(
    size,
    u_hbm,
    bits_hbm,
    cot_hbm,
    wr_hbm,
    ws_hbm,
    we_hbm,
    ig_ref,
    ib_ref,
    og_ref,
    ob_ref,
    hwt_ref,
    hb_ref,
    info_ref,
    heads_ref,
    hwg_ref,
    hbg_ref,
    igs,
    ibs,
    ogs,
    obs,
    rs_ref,
    rc_ref,
    merged_hbm,
    u1_hbm,
    zc_hbm,
    za_hbm,
    zb_hbm,
    r1_hbm,
    wr_all,
    ws_all,
    we_all,
    wr,
    ws,
    we,
    u0,
    u1,
    a_ref,
    b_ref,
    e_ref,
    cat,
    r2,
    za,
    zb,
    zc,
    merged,
    bits,
    cot,
    halo,
    msg,
    msg_c,
    first_msg,
    stat,
    stat_c,
    send_sem,
    recv_sem,
    edge_send,
    edge_recv,
    w_load,
    w_send,
    w_recv,
    w_out,
    in_sem,
    bit_sem,
    out_sem,
):
    link = Exchange(size, send_sem, recv_sem, edge_send, edge_recv)
    section, me = link.section, link.me
    pixels, channels = u0.shape
    inner = a_ref.shape[1]
    rows, width = bits_hbm.shape[1], bits_hbm.shape[2]
    f32, bf16 = jnp.float32, jnp.bfloat16

    load_u = pltpu.make_async_copy(u_hbm, u0, in_sem.at[0])
    load_cot = pltpu.make_async_copy(cot_hbm.at[section], cot, in_sem.at[1])

    def load_bits(chunk):
        return pltpu.make_async_copy(
            bits_hbm.at[section, chunk], bits.at[chunk % 2], bit_sem.at[chunk % 2]
        )

    load_u.start()
    load_cot.start()
    load_bits(0).start()
    load_bits(1).start()

    weights = ((wr_hbm, wr, wr_all), (ws_hbm, ws, ws_all), (we_hbm, we, we_all))

    def local_load(kind):
        source, target, _ = weights[kind]
        return pltpu.make_async_copy(source, target.at[section], w_load.at[kind])

    def pushed(kind):
        source, target, _ = weights[kind]
        return pltpu.make_async_remote_copy(
            src_ref=source,
            dst_ref=target.at[section],
            send_sem=w_send.at[kind],
            recv_sem=w_recv.at[kind],
            device_id=(1 - section, me),
            device_id_type=MESH,
        )

    vectors = ((ig_ref, igs), (ib_ref, ibs), (og_ref, ogs), (ob_ref, obs))

    def pushed_vector(kind):
        source, target = vectors[kind]
        return pltpu.make_async_remote_copy(
            src_ref=source,
            dst_ref=target.at[section],
            send_sem=w_send.at[3 + kind],
            recv_sem=w_recv.at[3 + kind],
            device_id=(1 - section, me),
            device_id_type=MESH,
        )

    def save_weight(kind, layer):
        _, target, saved = weights[kind]
        return pltpu.make_async_copy(target.at[layer], saved.at[layer], w_out.at[kind, layer])

    for kind in range(3):
        local_load(kind).start()
    link.greet()
    for kind in range(4):
        pushed_vector(kind).start()
    for kind in range(3):
        pushed(kind).start()
    for source, target in vectors:
        target[section] = source[...]

    def need_weight(kind, layer):
        pl.when(section == layer)(local_load(kind).wait)
        pl.when(section != layer)(pushed(kind).wait_recv)
        save_weight(kind, layer).start()

    own = pl.ds(width, pixels)

    def live_at(start, count):
        return info_ref[pl.ds(start, count), 0:1]

    def drop_chunk(chunk):
        load_bits(chunk).wait()
        start = pl.multiple_of(chunk * width, 16)
        target = cot[chunk].astype(f32) * live_at(width + start, width)
        task = lax.broadcasted_iota(jnp.int32, target.shape, 1) // HEAD_OUT
        parts = [jnp.where(task == k, target, 0.0).astype(bf16) for k in range(TASKS)]

        @pl.loop(0, channels // TILE)
        def _(tile):
            cols = pl.ds(pl.multiple_of(tile * TILE, TILE), TILE)
            table = hwt_ref[:, cols]
            signed = magnitude = weighted = None
            for part in parts:
                value = jnp.dot(part, table, preferred_element_type=f32)
                square = value * value
                whole = square + SOFT * SOFT
                inverse = lax.rsqrt(whole)
                if signed is None:
                    signed, magnitude, weighted = value, whole * inverse, square * inverse
                else:
                    signed = signed + value
                    magnitude = magnitude + whole * inverse
                    weighted = weighted + square * inverse
            level = bits[chunk % 2, :, cols].astype(f32)
            reach = 0.25 / SHARP
            inside = reach * (signed / magnitude) + (
                reach * (1.0 - 1.0 / LEVELS) - (2.0 * reach / LEVELS) * level
            )
            value = 0.5 * signed + (0.5 * jnp.tanh(inside)) * weighted
            merged[pl.ds(start, width), cols] = value.astype(bf16)

        if chunk + 2 < rows:
            load_bits(chunk + 2).start()

    live_all = info_ref[own, 0:1]
    count_here = jnp.sum(live_all, axis=0, keepdims=True)
    share = 1.0 / count_here

    def column_stats(values):
        mean = jnp.sum(values * live_all, axis=0, keepdims=True) * share
        apart = values - mean
        return mean, jnp.sum(live_all * apart * apart, axis=0, keepdims=True)

    def counts(step):
        return first_msg[step, 2:3, 0:1]

    def combine(slots):
        number = counts(0)
        mean = slots[0, 0:1] * counts(0)
        spread = slots[0, 1:2]
        for step in range(1, size):
            number = number + counts(step)
            mean = mean + slots[step, 0:1] * counts(step)
            spread = spread + slots[step, 1:2]
        mean = mean / number
        for step in range(size):
            apart = slots[step, 0:1] - mean
            spread = spread + counts(step) * apart * apart
        return mean, lax.rsqrt(spread / number + EPS), number

    load_u.wait()
    load_cot.wait()
    drop_chunk(0)
    first_msg[0, 2:3] = jnp.broadcast_to(count_here, (1, inner))
    first_msg[0, 3:4] = jnp.zeros((1, inner), f32)
    zc_out = za_out = zb_out = r1_out = None
    u1_out = pltpu.make_async_copy(u1, u1_hbm, out_sem.at[0])
    for layer in range(2):
        x_ref = (u0, u1)[layer]
        need_weight(0, layer)
        slots = first_msg if layer == 0 else msg.at[0]

        @pl.loop(0, inner // 256)
        def _(tile):
            cols = pl.ds(pl.multiple_of(tile * 256, 256), 256)
            values = jnp.dot(x_ref[...], wr[layer, :, cols], preferred_element_type=f32)
            a_ref[:, cols] = values
            mean, spread = column_stats(values)
            slots[0, 0:1, cols] = mean
            slots[0, 1:2, cols] = spread

        if layer == 1:
            for copy in (za_out, zb_out, r1_out, zc_out):
                copy.wait()
            u1_out.start()
        sends = link.copies(3 * layer, slots)
        for copy in sends:
            copy.start()
        a_edges = (a_ref.at[pl.ds(0, width)], a_ref.at[pl.ds(pixels - width, width)])
        a_halo = halo.at[2 * layer]
        link.start_edges(2 * layer, *a_edges, a_halo)
        if layer == 0:
            for kind in range(4):
                pushed_vector(kind).wait()
        drop_chunk(1 + 3 * layer)
        for copy in sends:
            copy.wait()
        mean, inverse, number = combine(slots)
        stat[layer, 0:1], stat[layer, 1:2] = mean, inverse
        rs_ref[layer, 0:1] = inverse
        rs_ref[layer, 2:3] = jnp.broadcast_to(number, (1, inner))
        link.wait_edges(2 * layer, *a_edges, a_halo)

        def first_act(row, values, inside):
            normed = (values - stat[layer, 0:1]) * stat[layer, 1:2]
            affine = normed * igs[layer, 0:1] + ibs[layer, 0:1]
            act = affine * (1.0 / (1.0 + jnp.exp(-affine)))
            if inside is not None:
                act = jnp.where(inside, act, 0.0)
            here = pl.ds(pl.multiple_of(row * width, 16), width)
            masks = info_ref[pl.ds(width, width), :]
            cat[here, 0:inner] = (pltpu.roll(act, 1, 0) * masks[:, 1:2]).astype(bf16)
            cat[here, inner : 2 * inner] = act.astype(bf16)
            cat[here, 2 * inner : 3 * inner] = (
                pltpu.roll(act, width - 1, 0) * masks[:, 2:3]
            ).astype(bf16)
            return normed

        first_act(0, a_halo[0], me > 0)
        first_act(rows + 1, a_halo[1], me < size - 1)

        @pl.loop(0, rows)
        def _(row):
            here = pl.ds(pl.multiple_of(row * width, 16), width)
            za[here] = first_act(row + 1, a_ref[here], None).astype(bf16)

        za_out = pltpu.make_async_copy(za, za_hbm.at[layer], out_sem.at[1])
        r1_out = pltpu.make_async_copy(
            cat.at[:, pl.ds(inner, inner)], r1_hbm.at[layer], out_sem.at[2]
        )
        za_out.start()
        r1_out.start()
        need_weight(1, layer)
        slots = msg.at[1 + 2 * layer]

        @pl.loop(0, inner // 256)
        def _(tile):
            cols = pl.ds(pl.multiple_of(tile * 256, 256), 256)
            values = None
            for tap in range(3):
                table = ws[layer, 3 * tap : 3 * tap + 3, :, cols].reshape(3 * inner, 256)
                value = jnp.dot(
                    cat[tap * width : tap * width + pixels], table, preferred_element_type=f32
                )
                values = value if values is None else values + value
            b_ref[:, cols] = values
            mean, spread = column_stats(values)
            slots[0, 0:1, cols] = mean
            slots[0, 1:2, cols] = spread

        sends = link.copies(3 * layer + 1, slots)
        for copy in sends:
            copy.start()
        b_edges = (b_ref.at[pl.ds(0, width)], b_ref.at[pl.ds(pixels - width, width)])
        b_halo = halo.at[2 * layer + 1]
        link.start_edges(2 * layer + 1, *b_edges, b_halo)
        drop_chunk(2 + 3 * layer)
        for copy in sends:
            copy.wait()
        mean, inverse, _ = combine(slots)
        stat[layer, 2:3], stat[layer, 3:4] = mean, inverse
        rs_ref[layer, 1:2] = inverse

        @pl.loop(0, rows)
        def _(row):
            here = pl.ds(pl.multiple_of(row * width, 16), width)
            normed = (b_ref[here] - stat[layer, 2:3]) * stat[layer, 3:4]
            zb[pl.ds(pl.multiple_of((row + 1) * width, 16), width)] = normed.astype(bf16)
            affine = normed * igs[layer, 1:2] + ibs[layer, 1:2]
            r2[here] = (affine * (1.0 / (1.0 + jnp.exp(-affine)))).astype(bf16)

        need_weight(2, layer)
        slots = msg_c.at[layer]

        @pl.loop(0, channels // 256)
        def _(tile):
            cols = pl.ds(pl.multiple_of(tile * 256, 256), 256)
            values = jnp.dot(r2[...], we[layer, :, cols], preferred_element_type=f32)
            e_ref[:, cols] = values
            mean, spread = column_stats(values)
            slots[0, 0:1, cols] = mean
            slots[0, 1:2, cols] = spread

        sends = link.copies(3 * layer + 2, slots)
        for copy in sends:
            copy.start()
        link.wait_edges(2 * layer + 1, *b_edges, b_halo)
        for side, row in ((0, 0), (1, rows + 1)):
            normed = (b_halo[side] - stat[layer, 2:3]) * stat[layer, 3:4]
            zb[row * width : (row + 1) * width] = normed.astype(bf16)
        zb_out = pltpu.make_async_copy(zb, zb_hbm.at[layer], out_sem.at[3])
        zb_out.start()
        drop_chunk(3 + 3 * layer)
        if layer == 1:
            drop_chunk(7)
            pltpu.make_async_copy(merged, merged_hbm, out_sem.at[4]).start()
        for copy in sends:
            copy.wait()
        mean, inverse, _ = combine(slots)
        stat_c[0:1], stat_c[1:2] = mean, inverse
        rc_ref[layer] = inverse
        out_ref = (u1, u0)[layer]

        @pl.loop(0, rows * (channels // TILE))
        def _(chunk):
            row, tile = chunk // (channels // TILE), chunk % (channels // TILE)
            here = pl.ds(pl.multiple_of(row * width, 16), width)
            cols = pl.ds(pl.multiple_of(tile * TILE, TILE), TILE)
            normed = (e_ref[here, cols] - stat_c[0:1, cols]) * stat_c[1:2, cols]
            zc[here, cols] = normed.astype(bf16)
            total = normed * ogs[layer, :, cols] + obs[layer, :, cols] + x_ref[here, cols].astype(f32)
            out_ref[here, cols] = (total * (1.0 / (1.0 + jnp.exp(-total)))).astype(bf16)

        zc_out = pltpu.make_async_copy(zc, zc_hbm.at[layer], out_sem.at[5])
        zc_out.start()

    heads_ref[...] = (
        lax.dot_general(u0[...], hwt_ref[...], BESIDE, preferred_element_type=f32) + hb_ref[...]
    )
    target = cot[...].astype(f32).reshape(pixels, -1) * live_all
    hbg_ref[...] = jnp.sum(target, axis=0, keepdims=True)
    target = target.astype(bf16)

    @pl.loop(0, channels // 256)
    def _(tile):
        cols = pl.ds(pl.multiple_of(tile * 256, 256), 256)
        hwg_ref[:, cols] = lax.dot_general(target, u0[:, cols], ACROSS, preferred_element_type=f32)

    for copy in (za_out, zb_out, r1_out, zc_out, u1_out):
        copy.wait()
    pltpu.make_async_copy(merged, merged_hbm, out_sem.at[4]).wait()
    for kind in range(3):
        pushed(kind).wait_send()
        for layer in range(2):
            save_weight(kind, layer).wait()


def forward(u, bits, cot, wr, ws, we, ig, ib, og, ob, hwt, hb, info):
    size = lax.axis_size("dp")
    pixels, channels = u.shape
    inner = wr.shape[1]
    _, rows, width, head_cols = cot.shape
    f32, bf16 = jnp.float32, jnp.bfloat16
    padded = pixels + 2 * width
    anywhere = pl.BlockSpec(memory_space=pl.ANY)
    vmem = pl.BlockSpec(memory_space=pltpu.VMEM)

    def out(kind, *shape):
        return jax.ShapeDtypeStruct(shape, kind)

    return pl.pallas_call(
        functools.partial(forward_kernel, size),
        out_shape=[
            out(f32, pixels, head_cols),
            out(f32, head_cols, channels),
            out(f32, 1, head_cols),
            out(f32, 2, 2, inner),
            out(f32, 2, 2, inner),
            out(f32, 2, 1, channels),
            out(f32, 2, 1, channels),
            out(f32, 2, 8, inner),
            out(f32, 2, 1, channels),
            out(bf16, pixels, channels),
            out(bf16, pixels, channels),
            out(bf16, 2, pixels, channels),
            out(bf16, 2, pixels, inner),
            out(bf16, 2, padded, inner),
            out(bf16, 2, padded, inner),
            out(bf16, 2, channels, inner),
            out(bf16, 2, 9, inner, inner),
            out(bf16, 2, inner, channels),
        ],
        in_specs=[anywhere] * 6 + [vmem] * 7,
        out_specs=[vmem] * 9 + [anywhere] * 9,
        scratch_shapes=[
            pltpu.VMEM((2, channels, inner), bf16),
            pltpu.VMEM((2, 9, inner, inner), bf16),
            pltpu.VMEM((2, inner, channels), bf16),
            pltpu.VMEM((pixels, channels), bf16),
            pltpu.VMEM((pixels, channels), bf16),
            pltpu.VMEM((pixels, inner), f32),
            pltpu.VMEM((pixels, inner), f32),
            pltpu.VMEM((pixels, channels), f32),
            pltpu.VMEM((padded, 3 * inner), bf16),
            pltpu.VMEM((pixels, inner), bf16),
            pltpu.VMEM((pixels, inner), bf16),
            pltpu.VMEM((padded, inner), bf16),
            pltpu.VMEM((pixels, channels), bf16),
            pltpu.VMEM((pixels, channels), bf16),
            pltpu.VMEM((2, width, channels), jnp.int32),
            pltpu.VMEM((rows, width, head_cols), bf16),
            pltpu.VMEM((4, 2, width, inner), f32),
            pltpu.VMEM((4, size, 2, inner), f32),
            pltpu.VMEM((2, size, 2, channels), f32),
            pltpu.VMEM((size, 4, inner), f32),
            pltpu.VMEM((2, 8, inner), f32),
            pltpu.VMEM((2, channels), f32),
            pltpu.SemaphoreType.DMA((6, size)),
            pltpu.SemaphoreType.DMA((6, size)),
            pltpu.SemaphoreType.DMA((4, 2)),
            pltpu.SemaphoreType.DMA((4, 2)),
            pltpu.SemaphoreType.DMA((3,)),
            pltpu.SemaphoreType.DMA((7,)),
            pltpu.SemaphoreType.DMA((7,)),
            pltpu.SemaphoreType.DMA((3, 2)),
            pltpu.SemaphoreType.DMA((2,)),
            pltpu.SemaphoreType.DMA((2,)),
            pltpu.SemaphoreType.DMA((6,)),
        ],
        compiler_params=pltpu.CompilerParams(
            collective_id=1, has_side_effects=True, vmem_limit_bytes=LIMIT
        ),
    )(u, bits, cot, wr, ws, we, ig, ib, og, ob, hwt, hb, info)


def backward_kernel(
    size,
    u0_hbm,
    u1_hbm,
    merged_hbm,
    zc_hbm,
    za_hbm,
    zb_hbm,
    r1_hbm,
    wr_all,
    ws_all,
    we_all,
    igs,
    ibs,
    ogs,
    obs,
    rs_ref,
    rc_ref,
    hwg_ref,
    hbg_ref,
    info_ref,
    grad_hbm,
    parts,
    wr,
    ws,
    we,
    u_ref,
    d_ref,
    de,
    zc,
    za,
    zb,
    r1,
    r2,
    cat,
    dzb,
    dza,
    da,
    stage,
    small,
    halo,
    msg,
    msg_c,
    part_sum,
    sums,
    sums_c,
    send_sem,
    recv_sem,
    edge_send,
    edge_recv,
    in_sem,
    tile_sem,
    out_sem,
):
    link = Exchange(size, send_sem, recv_sem, edge_send, edge_recv)
    section, me = link.section, link.me
    pixels, channels = d_ref.shape
    inner = da.shape[1]
    width = halo.shape[2]
    rows = pixels // width
    across = channels // TILE
    f32, bf16 = jnp.float32, jnp.bfloat16
    own = pl.ds(width, pixels)

    def loads(layer):
        return {
            "zc": pltpu.make_async_copy(zc_hbm.at[layer], zc, in_sem.at[0]),
            "za": pltpu.make_async_copy(za_hbm.at[layer], za, in_sem.at[1]),
            "zb": pltpu.make_async_copy(zb_hbm.at[layer], zb, in_sem.at[2]),
            "r1": pltpu.make_async_copy(r1_hbm.at[layer], r1, in_sem.at[3]),
            "wr": pltpu.make_async_copy(wr_all.at[layer], wr, in_sem.at[4]),
            "ws": pltpu.make_async_copy(ws_all.at[layer], ws, in_sem.at[5]),
            "we": pltpu.make_async_copy(we_all.at[layer], we, in_sem.at[6]),
            "u": pltpu.make_async_copy((u0_hbm, u1_hbm)[layer], u_ref.at[layer], in_sem.at[7 + layer]),
        }

    load_d = pltpu.make_async_copy(merged_hbm, d_ref, in_sem.at[9])
    first, second = loads(1), loads(0)
    load_d.start()
    for name in ("u", "zc", "we", "zb", "ws", "za", "r1", "wr"):
        first[name].start()
    second["u"].start()
    link.greet()
    live_all = info_ref[own, 0:1]

    def stage_copy(slot, tile):
        return pltpu.make_async_copy(stage.at[slot], parts.at[tile], tile_sem.at[slot])

    def put_tile(base, index, make):
        slot = lax.rem(index, 2)
        pl.when(base + index >= 2)(lambda: stage_copy(slot, 0).wait())

        @pl.loop(0, 2)
        def _(side):
            cols = pl.ds(pl.multiple_of(side * 256, 256), 256)
            stage[slot, :, cols] = make(side).astype(bf16)

        stage_copy(slot, base + index).start()

    def column_sums(values):
        return jnp.sum(values, axis=0, keepdims=True)

    def total_of(slots):
        found = slots[0]
        for step in range(1, size):
            found = found + slots[step]
        return found

    def expand_tiles(base):
        @pl.loop(0, across)
        def _(tile):
            def make(side):
                cols = pl.ds(pl.multiple_of(tile * TILE + side * 256, 256), 256)
                return lax.dot_general(r2[...], de[:, cols], ACROSS, preferred_element_type=f32)

            put_tile(base, tile, make)

    def spatial_tiles(base):
        @pl.loop(0, 9)
        def _(tap):
            shift, side_step = tap // 3, tap % 3

            def make(side):
                at = pl.ds(pl.multiple_of(shift * width, 16), pixels)
                cols = pl.ds(pl.multiple_of(side_step * inner + side * 256, 256), 256)
                return lax.dot_general(r1[at], cat[own, cols], ACROSS, preferred_element_type=f32)

            put_tile(base, across + tap, make)

    def reduce_tiles_of(base, layer):
        @pl.loop(0, across)
        def _(tile):
            def make(side):
                cols = pl.ds(pl.multiple_of(side * 256, 256), 256)
                lines = pl.ds(pl.multiple_of(tile * TILE, TILE), TILE)
                return lax.dot_general(
                    u_ref[layer, :, lines], da[:, cols], ACROSS, preferred_element_type=f32
                )

            put_tile(base, across + 9 + tile, make)

    def small_tile(base, layer):
        last = 2 * across + 9
        half = channels // 2
        head_cols = hwg_ref.shape[0]
        slot = last % 2
        stage_copy(slot, 0).wait()
        small[...] = jnp.zeros_like(small)
        for k in range(2):
            at = layer * half + k * TILE
            small[k * head_cols : (k + 1) * head_cols] = hwg_ref[:, at : at + TILE]
        row = 2 * head_cols
        small[row : row + 1, 0:head_cols] = hbg_ref[...]
        only = (me == 0).astype(f32)
        small[row + 8 : row + 9] = sums[0, 1:2] * only
        small[row + 9 : row + 10] = sums[1, 1:2] * only
        small[row + 10 : row + 11] = sums[0, 0:1] * only
        small[row + 11 : row + 12] = sums[1, 0:1] * only
        for k in range(across):
            cols = slice(k * TILE, (k + 1) * TILE)
            small[row + 12 + k : row + 13 + k] = sums_c[1:2, cols] * only
            small[row + 12 + across + k : row + 13 + across + k] = sums_c[0:1, cols] * only
        stage[slot] = jnp.zeros_like(stage[slot])
        stage[slot, 0 : small.shape[0]] = small[...].astype(bf16)
        stage_copy(slot, base + last).start()

    load_d.wait()
    for layer in (1, 0):
        base = (1 - layer) * (2 * across + 10)
        now = (second, first)[layer]
        now["u"].wait()
        now["zc"].wait()
        part_sum[...] = jnp.zeros_like(part_sum)

        @pl.loop(0, rows * across)
        def _(chunk):
            row, tile = chunk // across, chunk % across
            here = pl.ds(pl.multiple_of(row * width, 16), width)
            cols = pl.ds(pl.multiple_of(tile * TILE, TILE), TILE)
            normed = zc[here, cols].astype(f32)
            total = (
                normed * ogs[layer, :, cols]
                + obs[layer, :, cols]
                + u_ref[layer, here, cols].astype(f32)
            )
            _, slope = silu_parts(total)
            dt = d_ref[here, cols].astype(f32) * slope
            d_ref[here, cols] = dt.astype(bf16)
            part_sum[0, :, cols] += folded(dt)
            part_sum[1, :, cols] += folded(dt * normed)

        slots = msg_c.at[1 - layer]
        slots[0, 0:1] = column_sums(part_sum[0])
        slots[0, 1:2] = column_sums(part_sum[1])
        sends = link.copies(3 * layer, slots)
        for copy in sends:
            copy.start()
        if layer == 0:
            reduce_tiles_of(0, 1)
            small_tile(0, 1)
        for copy in sends:
            copy.wait()
        sums_c[...] = total_of(slots)
        number = rs_ref[layer, 2:3, 0:1]
        share = 1.0 / number

        @pl.loop(0, rows * across)
        def _(chunk):
            row, tile = chunk // across, chunk % across
            here = pl.ds(pl.multiple_of(row * width, 16), width)
            cols = pl.ds(pl.multiple_of(tile * TILE, TILE), TILE)
            live = info_ref[pl.ds(pl.multiple_of((row + 1) * width, 16), width), 0:1]
            normed = zc[here, cols].astype(f32)
            away = (sums_c[0:1, cols] + normed * sums_c[1:2, cols]) * share
            scale = rc_ref[layer, :, cols] * ogs[layer, :, cols]
            value = scale * (d_ref[here, cols].astype(f32) - live * away)
            de[here, cols] = value.astype(bf16)

        now["we"].wait()
        now["zb"].wait()
        slots = msg.at[2 * layer]

        @pl.loop(0, inner // 256)
        def _(tile):
            cols = pl.ds(pl.multiple_of(tile * 256, 256), 256)
            dr2 = lax.dot_general(de[...], we[cols], BESIDE, preferred_element_type=f32)
            normed = zb[own, cols].astype(f32)
            act, slope = silu_parts(normed * igs[layer, 1:2, cols] + ibs[layer, 1:2, cols])
            r2[:, cols] = act.astype(bf16)
            dz = dr2 * slope
            dzb[:, cols] = dz
            slots[0, 0:1, cols] = column_sums(dz)
            slots[0, 1:2, cols] = column_sums(dz * normed)

        sends = link.copies(3 * layer + 1, slots)
        for copy in sends:
            copy.start()
        edges = (dzb.at[pl.ds(0, width)], dzb.at[pl.ds(pixels - width, width)])
        landing = halo.at[layer]
        link.start_edges(layer, *edges, landing)
        if layer == 1:
            second["zc"].start()
            second["we"].start()
        expand_tiles(base)
        for copy in sends:
            copy.wait()
        sums[1] = total_of(slots)
        link.wait_edges(layer, *edges, landing)

        def db_row(row, dz, inside):
            here = pl.ds(pl.multiple_of(row * width, 16), width)
            live = info_ref[here, 0:1]
            normed = zb[here].astype(f32)
            away = (sums[1, 0:1] + normed * sums[1, 1:2]) * share
            value = (rs_ref[layer, 1:2] * igs[layer, 1:2]) * (dz - live * away)
            if inside is not None:
                value = jnp.where(inside, value, 0.0)
            masks = info_ref[pl.ds(width, width), :]
            cat[here, 0:inner] = (pltpu.roll(value, width - 1, 0) * masks[:, 2:3]).astype(bf16)
            cat[here, inner : 2 * inner] = value.astype(bf16)
            cat[here, 2 * inner : 3 * inner] = (
                pltpu.roll(value, 1, 0) * masks[:, 1:2]
            ).astype(bf16)

        db_row(0, landing[0], me > 0)
        db_row(rows + 1, landing[1], me < size - 1)

        @pl.loop(0, rows)
        def _(row):
            db_row(row + 1, dzb[pl.ds(pl.multiple_of(row * width, 16), width)], None)

        if layer == 1:
            second["zb"].start()
        now["ws"].wait()
        now["za"].wait()
        slots = msg.at[2 * layer + 1]

        @pl.loop(0, inner // 256)
        def _(tile):
            cols = pl.ds(pl.multiple_of(tile * 256, 256), 256)
            dr1 = None
            for tap in range(9):
                start = (2 - tap // 3) * width
                block = cat[start : start + pixels, (tap % 3) * inner : (tap % 3 + 1) * inner]
                value = lax.dot_general(block, ws[tap, cols], BESIDE, preferred_element_type=f32)
                dr1 = value if dr1 is None else dr1 + value
            normed = za[:, cols].astype(f32)
            _, slope = silu_parts(normed * igs[layer, 0:1, cols] + ibs[layer, 0:1, cols])
            dz = dr1 * slope
            dza[:, cols] = dz
            slots[0, 0:1, cols] = column_sums(dz)
            slots[0, 1:2, cols] = column_sums(dz * normed)

        sends = link.copies(3 * layer + 2, slots)
        for copy in sends:
            copy.start()
        if layer == 1:
            second["ws"].start()
        now["r1"].wait()
        spatial_tiles(base)
        for copy in sends:
            copy.wait()
        sums[0] = total_of(slots)
        if layer == 1:
            second["r1"].start()

        @pl.loop(0, rows)
        def _(row):
            here = pl.ds(pl.multiple_of(row * width, 16), width)
            live = info_ref[pl.ds(pl.multiple_of((row + 1) * width, 16), width), 0:1]
            away = (sums[0, 0:1] + za[here].astype(f32) * sums[0, 1:2]) * share
            value = (rs_ref[layer, 0:1] * igs[layer, 0:1]) * (dza[here] - live * away)
            da[here] = value.astype(bf16)

        if layer == 1:
            second["za"].start()
        now["wr"].wait()

        @pl.loop(0, channels // 256)
        def _(tile):
            cols = pl.ds(pl.multiple_of(tile * 256, 256), 256)
            du = lax.dot_general(da[...], wr[cols], BESIDE, preferred_element_type=f32)
            d_ref[:, cols] = (du + d_ref[:, cols].astype(f32)).astype(bf16)

        if layer == 1:
            second["wr"].start()
    out = pltpu.make_async_copy(d_ref, grad_hbm, out_sem)
    out.start()
    reduce_tiles_of(2 * across + 10, 0)
    small_tile(2 * across + 10, 0)
    stage_copy(0, 0).wait()
    stage_copy(1, 0).wait()
    out.wait()


def backward(u0, u1, merged, zc, za, zb, r1, wr, ws, we, igs, ibs, ogs, obs, rs, rc, hwg, hbg, info):
    size = lax.axis_size("dp")
    pixels, channels = u0.shape
    inner = za.shape[2]
    padded = zb.shape[1]
    width = (padded - pixels) // 2
    f32, bf16 = jnp.float32, jnp.bfloat16
    anywhere = pl.BlockSpec(memory_space=pl.ANY)
    vmem = pl.BlockSpec(memory_space=pltpu.VMEM)
    count = 2 * (2 * (channels // TILE) + 10)
    return pl.pallas_call(
        functools.partial(backward_kernel, size),
        out_shape=[
            jax.ShapeDtypeStruct((pixels, channels), bf16),
            jax.ShapeDtypeStruct((count, TILE, TILE), bf16),
        ],
        in_specs=[anywhere] * 10 + [vmem] * 9,
        out_specs=[anywhere] * 2,
        scratch_shapes=[
            pltpu.VMEM((channels, inner), bf16),
            pltpu.VMEM((9, inner, inner), bf16),
            pltpu.VMEM((inner, channels), bf16),
            pltpu.VMEM((2, pixels, channels), bf16),
            pltpu.VMEM((pixels, channels), bf16),
            pltpu.VMEM((pixels, channels), bf16),
            pltpu.VMEM((pixels, channels), bf16),
            pltpu.VMEM((pixels, inner), bf16),
            pltpu.VMEM((padded, inner), bf16),
            pltpu.VMEM((padded, inner), bf16),
            pltpu.VMEM((pixels, inner), bf16),
            pltpu.VMEM((padded, 3 * inner), bf16),
            pltpu.VMEM((pixels, inner), f32),
            pltpu.VMEM((pixels, inner), f32),
            pltpu.VMEM((pixels, inner), bf16),
            pltpu.VMEM((2, TILE, TILE), bf16),
            pltpu.VMEM((128, TILE), f32),
            pltpu.VMEM((2, 2, width, inner), f32),
            pltpu.VMEM((4, size, 2, inner), f32),
            pltpu.VMEM((2, size, 2, channels), f32),
            pltpu.VMEM((2, 8, channels), f32),
            pltpu.VMEM((2, 2, inner), f32),
            pltpu.VMEM((2, channels), f32),
            pltpu.SemaphoreType.DMA((6, size)),
            pltpu.SemaphoreType.DMA((6, size)),
            pltpu.SemaphoreType.DMA((2, 2)),
            pltpu.SemaphoreType.DMA((2, 2)),
            pltpu.SemaphoreType.DMA((10,)),
            pltpu.SemaphoreType.DMA((2,)),
            pltpu.SemaphoreType.DMA,
        ],
        compiler_params=pltpu.CompilerParams(
            collective_id=2, has_side_effects=True, vmem_limit_bytes=LIMIT
        ),
    )(u0, u1, merged, zc, za, zb, r1, wr, ws, we, igs, ibs, ogs, obs, rs, rc, hwg, hbg, info)


def pixel_info(pixel_mask, starts):
    size = lax.axis_size("dp")
    rows, width = pixel_mask.shape
    up = [(i, i + 1) for i in range(size - 1)]
    down = [(j, i) for i, j in up]
    before = lax.ppermute(pixel_mask[rows - 1 :], "dp", up)
    after = lax.ppermute(pixel_mask[:1], "dp", down)
    live = jnp.concatenate([before, pixel_mask, after])
    columns = jnp.arange(width, dtype=jnp.int32)
    crop = jnp.sum((columns[:, None] >= starts[None, :]).astype(jnp.int32), axis=1)
    outside = jnp.full((1,), -1, jnp.int32)
    left = jnp.concatenate([outside, crop[:-1]]) == crop
    right = jnp.concatenate([crop[1:], outside]) == crop
    lane = jnp.arange(128, dtype=jnp.int32)
    first = jnp.where(lane == 0, live[:, :, None], 0)
    links = jnp.where(lane == 1, left[:, None].astype(jnp.int32), 0)
    links = links + jnp.where(lane == 2, right[:, None].astype(jnp.int32), 0)
    return (first + links[None]).astype(jnp.float32).reshape(-1, 128)


def pick(array, index):
    return lax.dynamic_index_in_dim(array, index, 0, keepdims=False)


def local(
    canvases,
    crop_starts,
    pixel_mask,
    drop_bits,
    reduce_weight,
    spatial_weight,
    expand_weight,
    inner_gain,
    inner_bias,
    outer_gain,
    outer_bias,
    head_weight,
    head_bias,
    head_cotangent,
):
    section = lax.axis_index("section")
    first = section == 0
    rows, width, channels = canvases.shape[1:]
    taps = spatial_weight.shape[1]
    head_cols = head_weight.shape[1]
    pixels = rows * width
    flat = canvases.reshape(pixels, channels)
    info = pixel_info(pick(pixel_mask, section), pick(crop_starts, section))
    heads, hwg, hbg, igs, ibs, ogs, obs, rs, rc, merged, u1, zc, za, zb, r1, wr, ws, we = forward(
        flat,
        drop_bits,
        head_cotangent,
        reduce_weight[0],
        spatial_weight[0],
        expand_weight[0],
        inner_gain[0],
        inner_bias[0],
        outer_gain,
        outer_bias,
        head_weight.T,
        head_bias[None],
        info,
    )
    grad, parts = backward(
        flat, u1, merged, zc, za, zb, r1, wr, ws, we, igs, ibs, ogs, obs, rs, rc, hwg, hbg, info
    )
    expand_total, spatial_total, reduce_total, small = reduce_tiles(parts, channels, taps)
    small = small.astype(jnp.float32)
    half = channels // 2
    across = channels // TILE
    head_w_out = jnp.concatenate([small[:head_cols].T, small[head_cols : 2 * head_cols].T])
    row = 2 * head_cols
    cut = head_cols // 2
    head_b_out = jnp.where(first, small[row, :cut], small[row, cut:head_cols])
    norms = small[row + 8 :]
    return (
        heads.reshape(1, rows, width, head_cols),
        grad.reshape(1, rows, width, channels),
        reduce_total.astype(jnp.float32)[None],
        spatial_total.astype(jnp.float32)[None],
        expand_total.astype(jnp.float32)[None],
        norms[0:2][None],
        norms[2:4][None],
        norms[4 : 4 + across].reshape(1, channels),
        norms[4 + across : 4 + 2 * across].reshape(1, channels),
        head_w_out,
        head_b_out,
    )


def solution(mesh):
    placed = (
        P("section", "dp", None, None),
        P(),
        P(None, "dp", None),
        P(None, "dp", None, None),
        P("section", None, None),
        P("section", None, None, None),
        P("section", None, None),
        P("section", None, None),
        P("section", None, None),
        P("section", None),
        P("section", None),
        P(),
        P(),
        P(None, "dp", None, None),
    )
    return jax.shard_map(
        local,
        mesh=mesh,
        in_specs=placed,
        out_specs=(
            P("section", "dp", None, None),
            P("section", "dp", None, None),
            P("section", None, None),
            P("section", None, None, None),
            P("section", None, None),
            P("section", None, None),
            P("section", None, None),
            P("section", None),
            P("section", None),
            P("section", None),
            P("section"),
        ),
        check_vma=False,
    )
```

```python
import functools
import math

import jax
import jax.numpy as jnp
from jax import lax
from jax.experimental import pallas as pl
from jax.experimental.pallas import tpu as pltpu
from jax.sharding import PartitionSpec as P

TASKS = 3
HEAD_OUT = 16

EPS = 1e-05
SOFT = 0.05
SHARP = 0.1
LEVELS = 1024.0
ACROSS = (((0,), (0,)), ((), ()))
BESIDE = (((1,), (1,)), ((), ()))
MESH = pl.DeviceIdType.MESH
TILE = 512
LIMIT = 56 * 2**20


def grid_of(size):
    side = math.isqrt(size // 4)
    assert side * side * 4 == size
    return (4, side, side)


class Reducer:
    STAGES = 9

    def __init__(self, size, tiles):
        self.size = size
        self.nz, self.ny, self.nx = grid_of(size)
        self.zrows = 16
        self.yrows = self.zrows * self.nz
        self.half = self.yrows * self.ny
        self.lines = 2 * self.half
        self.cols = TILE // self.nx
        self.per_tile = TILE // self.lines
        self.lag = 2 if self.per_tile > 1 else 1
        self.slots = 4 * self.lag + 2
        self.real = tiles * self.per_tile + 1
        self.block_groups = -(-self.real // 3)
        self.groups = 2 * self.block_groups

    def scratch(self):
        nx, ny, nz, groups, cols = self.nx, self.ny, self.nz, self.groups, self.cols
        bf16 = jnp.bfloat16
        return [
            pltpu.VMEM((3 * self.slots, self.lines, TILE), bf16),
            pltpu.VMEM((3 * groups, self.half, TILE), bf16),
            pltpu.VMEM((2 * groups, nx - 1, self.half, cols), bf16),
            pltpu.VMEM((2 * groups, ny - 1, self.yrows, cols), bf16),
            pltpu.VMEM((2 * groups, nz - 1, self.zrows, cols), bf16),
            pltpu.VMEM((groups, ny - 1, self.yrows, TILE), bf16),
            pltpu.VMEM((groups, nz - 1, self.zrows, TILE), bf16),
            pltpu.VMEM((groups, nx - 1, self.zrows, cols), bf16),
            pltpu.SemaphoreType.DMA((3 * groups, 2)),
            pltpu.SemaphoreType.DMA((3 * groups, 2)),
            pltpu.SemaphoreType.DMA((3 * groups, 2 * (nx + ny + nz - 3))),
            pltpu.SemaphoreType.DMA((3 * groups, 2 * (nx + ny + nz - 3))),
        ]

    def bind(self, total, scratch):
        self.total = total
        (
            self.ring,
            self.res,
            self.ax,
            self.ay,
            self.az,
            self.by,
            self.bz,
            self.bx,
            self.pair_send,
            self.pair_recv,
            self.send_sem,
            self.recv_sem,
        ) = scratch
        self.section, self.me = lax.axis_index("section"), lax.axis_index("dp")
        plane = self.ny * self.nx
        self.z = self.me // plane
        self.y = (self.me // self.nx) % self.ny
        self.x = self.me % self.nx

    def count(self, axis):
        return {"x": self.nx, "y": self.ny, "z": self.nz}[axis]

    def other(self, axis, step):
        plane = self.ny * self.nx
        if axis == "x":
            place = (self.x + step) % self.nx
            return self.z * plane + self.y * self.nx + place, place
        if axis == "y":
            place = (self.y + step) % self.ny
            return self.z * plane + place * self.nx + self.x, place
        place = (self.z + step) % self.nz
        return place * plane + self.y * self.nx + self.x, place

    def sem(self, axis, back, step):
        base = {"x": 0, "y": self.nx - 1, "z": self.nx + self.ny - 2}[axis]
        return base + (step - 1) + (self.nx + self.ny + self.nz - 3 if back else 0)

    def slot(self, unit):
        return self.ring.at[lax.rem(unit, 3 * self.slots)]

    def acc(self, unit):
        return self.slot(unit).at[self.half_rows(self.section)]

    def block(self, base, x, y, z):
        if y is None:
            lines = slice(None)
        elif z is None:
            lines = pl.ds(pl.multiple_of(y * self.yrows, 16), self.yrows)
        else:
            lines = pl.ds(pl.multiple_of(y * self.yrows + z * self.zrows, 16), self.zrows)
        if x is None:
            return base.at[lines]
        return base.at[lines, pl.ds(pl.multiple_of(x * self.cols, self.cols), self.cols)]

    def spread(self, tile, axis, back, source, target):
        copies = []
        for step in range(1, self.count(axis)):
            device, place = self.other(axis, step)
            index = self.sem(axis, back, step)
            copies.append(
                pltpu.make_async_remote_copy(
                    src_ref=source(place),
                    dst_ref=target(step),
                    send_sem=self.send_sem.at[tile, index],
                    recv_sem=self.recv_sem.at[tile, index],
                    device_id=(self.section, device),
                    device_id_type=MESH,
                )
            )
        return copies

    def add(self, ref, extra, target=None):
        total = ref[...].astype(jnp.float32)
        for one in extra:
            total = total + one[...].astype(jnp.float32)
        target = ref if target is None else target
        target[...] = total.astype(jnp.bfloat16)

    def order(self, slot):
        return "xyz" if slot < 2 else "yzx"

    def landing(self, group, slot, axis):
        if slot < 2:
            row = 2 * group + slot
            return {"x": self.ax, "y": self.ay, "z": self.az}[axis].at[row]
        return {"x": self.bx, "y": self.by, "z": self.bz}[axis].at[group]

    def where(self, done, extra=None):
        place = {"x": None, "y": None, "z": None}
        for axis in done:
            place[axis] = {"x": self.x, "y": self.y, "z": self.z}[axis]
        place.update(extra or {})
        return place

    def part(self, base, done, extra=None):
        place = self.where(done, extra)
        return self.block(base, place["x"], place["y"], place["z"])

    def half_rows(self, which):
        return pl.ds(pl.multiple_of(which * self.half, 16), self.half)

    def pair(self, unit):
        return pltpu.make_async_remote_copy(
            src_ref=self.slot(unit).at[self.half_rows(1 - self.section)],
            dst_ref=self.res.at[unit],
            send_sem=self.pair_send.at[unit, 1],
            recv_sem=self.pair_recv.at[unit, 0],
            device_id=(1 - self.section, self.me),
            device_id_type=MESH,
        )

    def scatter(self, group, slot, level):
        tile = 3 * group + slot
        order = self.order(slot)
        axis, done = order[level], order[:level]
        landing = self.landing(group, slot, axis)
        return self.spread(
            tile,
            axis,
            False,
            lambda place: self.part(self.acc(tile), done, {axis: place}),
            lambda step: landing.at[step - 1],
        )

    def scattered(self, group, slot, level):
        tile = 3 * group + slot
        order = self.order(slot)
        axis, done = order[level], order[: level + 1]
        landing = self.landing(group, slot, axis)
        steps = range(1, self.count(axis))
        for copy in self.scatter(group, slot, level):
            copy.wait()
        target = self.part(self.res.at[tile], done) if level == 2 else None
        self.add(self.part(self.acc(tile), done), [landing.at[step - 1] for step in steps], target)

    def gather(self, group, slot, level):
        tile = 3 * group + slot
        order = self.order(slot)
        axis, done = order[level], order[: level + 1]
        ref = self.part(self.res.at[tile], done)
        return self.spread(tile, axis, True, lambda place: ref, lambda step: ref)

    def gathered(self, group, slot, level):
        for copy in self.gather(group, slot, level):
            copy.wait()

    def places(self, index):
        expand, spatial, reduce, small = self.total
        across = expand.shape[1] // TILE
        taps = spatial.shape[0]
        tile, part = index // self.per_tile, index % self.per_tile
        inside = part * self.lines + self.section * self.half
        lines = pl.ds(pl.multiple_of(inside, 16), self.half)
        further = pl.ds(pl.multiple_of((tile - across - taps) * TILE + inside, 16), self.half)
        return [
            (tile < across, lambda: expand.at[lines, pl.ds(pl.multiple_of(tile * TILE, TILE), TILE)]),
            (
                jnp.logical_and(tile >= across, tile < across + taps),
                lambda: spatial.at[tile - across, lines],
            ),
            (
                jnp.logical_and(tile >= across + taps, tile < 2 * across + taps),
                lambda: reduce.at[further],
            ),
            (index == self.real - 1, lambda: small.at[self.half_rows(self.section)]),
        ]

    def final(self, tile, target):
        here = pltpu.make_async_copy(self.res.at[tile], target, self.pair_send.at[tile, 0])
        away = pltpu.make_async_remote_copy(
            src_ref=self.res.at[tile],
            dst_ref=target,
            send_sem=self.pair_send.at[tile, 0],
            recv_sem=self.pair_recv.at[tile, 1],
            device_id=(1 - self.section, self.me),
            device_id_type=MESH,
        )
        return here, away

    def finish(self, tile):
        later = (tile >= 3 * self.block_groups).astype(jnp.int32)
        mine = self.section == 1 - later
        index = tile - later * (3 * self.block_groups)
        for wanted, place in self.places(index):

            @pl.when(jnp.logical_and(wanted, mine))
            def _():
                self.final(tile, place())[0].start()

            @pl.when(jnp.logical_and(wanted, jnp.logical_not(mine)))
            def _():
                self.final(tile, place())[1].start()

    def finished(self, tile):
        later = (tile >= 3 * self.block_groups).astype(jnp.int32)
        mine = self.section == 1 - later
        here, away = self.final(tile, self.total[3].at[self.half_rows(self.section)])

        @pl.when(mine)
        def _():
            here.wait()
            away.wait_recv()

        pl.when(jnp.logical_not(mine))(away.wait_send)

    def stage(self, number, group):
        for slot in range(3):
            if slot == 2 and self.real < 3 * self.block_groups:
                last = lax.rem(group, self.block_groups) == self.block_groups - 1
                pl.when(jnp.logical_not(last))(functools.partial(self.step, number, group, slot))
            else:
                self.step(number, group, slot)

    def step(self, number, group, slot):
        unit = 3 * group + slot
        if number == 0:
            self.pair(unit).start()
        elif number == 1:
            self.pair(unit).wait()
            self.add(self.acc(unit), [self.res.at[unit]])
            for copy in self.scatter(group, slot, 0):
                copy.start()
        elif number in (2, 3):
            self.scattered(group, slot, number - 2)
            for copy in self.scatter(group, slot, number - 1):
                copy.start()
        elif number == 4:
            self.scattered(group, slot, 2)
            for copy in self.gather(group, slot, 2):
                copy.start()
        elif number in (5, 6):
            self.gathered(group, slot, 7 - number)
            for copy in self.gather(group, slot, 6 - number):
                copy.start()
        elif number == 7:
            self.gathered(group, slot, 0)
            self.finish(unit)
        else:
            self.finished(unit)

    def tick(self, time):
        time = jnp.asarray(time, jnp.int32)
        for number in reversed(range(self.STAGES)):
            group = time - self.lag * number
            pl.when(jnp.logical_and(group >= 0, group < self.groups))(
                functools.partial(self.stage, number, group)
            )

    def after_tile(self, layer, tile):
        before = (tile * self.per_tile) // 3
        after = ((tile + 1) * self.per_tile) // 3
        pl.when(after > before)(lambda: self.tick((1 - layer) * self.block_groups + before))

    def drain(self):
        @pl.loop(self.groups, self.groups + self.lag * (self.STAGES - 1))
        def _(time):
            self.tick(time)


def silu_parts(v):
    sigma = 1.0 / (1.0 + jnp.exp(-v))
    return v * sigma, sigma * (1.0 + v * (1.0 - sigma))


def folded(x):
    return jnp.sum(x.reshape(x.shape[0] // 8, 8, x.shape[1]), axis=0)


class Exchange:
    def __init__(self, size, send_sem, recv_sem, edge_send, edge_recv):
        self.size = size
        self.section, self.me = lax.axis_index("section"), lax.axis_index("dp")
        self.send_sem, self.recv_sem = send_sem, recv_sem
        self.edge_send, self.edge_recv = edge_send, edge_recv

    def greet(self):
        barrier = pltpu.get_barrier_semaphore()
        for step in range(1, self.size):
            peer = (self.section, lax.rem(self.me + step, self.size))
            pl.semaphore_signal(barrier, inc=1, device_id=peer, device_id_type=MESH)
        other = (1 - self.section, self.me)
        pl.semaphore_signal(barrier, inc=1, device_id=other, device_id_type=MESH)
        pl.semaphore_wait(barrier, self.size)

    def copies(self, number, slots):
        return [
            pltpu.make_async_remote_copy(
                src_ref=slots.at[0],
                dst_ref=slots.at[step],
                send_sem=self.send_sem.at[number, step],
                recv_sem=self.recv_sem.at[number, step],
                device_id=(self.section, lax.rem(self.me + step, self.size)),
                device_id_type=MESH,
            )
            for step in range(1, self.size)
        ]

    def edges(self, number, first, last, landing):
        made = []
        for way, (ref, step) in enumerate(((first, self.size - 1), (last, 1))):
            made.append(
                pltpu.make_async_remote_copy(
                    src_ref=ref,
                    dst_ref=landing.at[1 - way],
                    send_sem=self.edge_send.at[number, way],
                    recv_sem=self.edge_recv.at[number, 1 - way],
                    device_id=(self.section, lax.rem(self.me + step, self.size)),
                    device_id_type=MESH,
                )
            )
        return made

    def start_edges(self, number, first, last, landing):
        up, down = self.edges(number, first, last, landing)
        pl.when(self.me > 0)(up.start)
        pl.when(self.me < self.size - 1)(down.start)

    def wait_edges(self, number, first, last, landing):
        up, down = self.edges(number, first, last, landing)
        pl.when(self.me > 0)(up.wait_send)
        pl.when(self.me > 0)(down.wait_recv)
        pl.when(self.me < self.size - 1)(down.wait_send)
        pl.when(self.me < self.size - 1)(up.wait_recv)


def forward_kernel(
    size,
    u_hbm,
    bits_hbm,
    cot_hbm,
    wr_hbm,
    ws_hbm,
    we_hbm,
    ig_ref,
    ib_ref,
    og_ref,
    ob_ref,
    hwt_ref,
    hb_ref,
    info_ref,
    heads_ref,
    hwg_ref,
    hbg_ref,
    igs,
    ibs,
    ogs,
    obs,
    rs_ref,
    rc_ref,
    merged_hbm,
    u1_hbm,
    zc_hbm,
    za_hbm,
    zb_hbm,
    r1_hbm,
    wr_all,
    ws_all,
    we_all,
    wr,
    ws,
    we,
    u0,
    u1,
    a_ref,
    b_ref,
    e_ref,
    cat,
    r2,
    za,
    zb,
    zc,
    merged,
    bits,
    cot,
    halo,
    msg,
    msg_c,
    first_msg,
    stat,
    stat_c,
    send_sem,
    recv_sem,
    edge_send,
    edge_recv,
    w_load,
    w_send,
    w_recv,
    w_out,
    in_sem,
    bit_sem,
    out_sem,
):
    link = Exchange(size, send_sem, recv_sem, edge_send, edge_recv)
    section, me = link.section, link.me
    pixels, channels = u0.shape
    inner = a_ref.shape[1]
    rows, width = bits_hbm.shape[1], bits_hbm.shape[2]
    f32, bf16 = jnp.float32, jnp.bfloat16

    load_u = pltpu.make_async_copy(u_hbm, u0, in_sem.at[0])
    load_cot = pltpu.make_async_copy(cot_hbm.at[section], cot, in_sem.at[1])

    def load_bits(chunk):
        return pltpu.make_async_copy(
            bits_hbm.at[section, chunk], bits.at[chunk % 2], bit_sem.at[chunk % 2]
        )

    load_u.start()
    load_cot.start()
    load_bits(0).start()
    load_bits(1).start()

    weights = ((wr_hbm, wr, wr_all), (ws_hbm, ws, ws_all), (we_hbm, we, we_all))

    def local_load(kind):
        source, target, _ = weights[kind]
        return pltpu.make_async_copy(source, target.at[section], w_load.at[kind])

    def pushed(kind):
        source, target, _ = weights[kind]
        return pltpu.make_async_remote_copy(
            src_ref=source,
            dst_ref=target.at[section],
            send_sem=w_send.at[kind],
            recv_sem=w_recv.at[kind],
            device_id=(1 - section, me),
            device_id_type=MESH,
        )

    vectors = ((ig_ref, igs), (ib_ref, ibs), (og_ref, ogs), (ob_ref, obs))

    def pushed_vector(kind):
        source, target = vectors[kind]
        return pltpu.make_async_remote_copy(
            src_ref=source,
            dst_ref=target.at[section],
            send_sem=w_send.at[3 + kind],
            recv_sem=w_recv.at[3 + kind],
            device_id=(1 - section, me),
            device_id_type=MESH,
        )

    def save_weight(kind, layer):
        _, target, saved = weights[kind]
        return pltpu.make_async_copy(target.at[layer], saved.at[layer], w_out.at[kind, layer])

    for kind in range(3):
        local_load(kind).start()
    link.greet()
    for kind in range(4):
        pushed_vector(kind).start()
    for kind in range(3):
        pushed(kind).start()
    for source, target in vectors:
        target[section] = source[...]

    def need_weight(kind, layer):
        pl.when(section == layer)(local_load(kind).wait)
        pl.when(section != layer)(pushed(kind).wait_recv)
        save_weight(kind, layer).start()

    own = pl.ds(width, pixels)

    def live_at(start, count):
        return info_ref[pl.ds(start, count), 0:1]

    def drop_chunk(chunk):
        load_bits(chunk).wait()
        start = pl.multiple_of(chunk * width, 16)
        target = cot[chunk].astype(f32) * live_at(width + start, width)
        task = lax.broadcasted_iota(jnp.int32, target.shape, 1) // HEAD_OUT
        parts = [jnp.where(task == k, target, 0.0).astype(bf16) for k in range(TASKS)]

        @pl.loop(0, channels // TILE)
        def _(tile):
            cols = pl.ds(pl.multiple_of(tile * TILE, TILE), TILE)
            table = hwt_ref[:, cols]
            signed = magnitude = weighted = None
            for part in parts:
                value = jnp.dot(part, table, preferred_element_type=f32)
                square = value * value
                whole = square + SOFT * SOFT
                inverse = lax.rsqrt(whole)
                if signed is None:
                    signed, magnitude, weighted = value, whole * inverse, square * inverse
                else:
                    signed = signed + value
                    magnitude = magnitude + whole * inverse
                    weighted = weighted + square * inverse
            level = bits[chunk % 2, :, cols].astype(f32)
            reach = 0.25 / SHARP
            inside = reach * (signed / magnitude) + (
                reach * (1.0 - 1.0 / LEVELS) - (2.0 * reach / LEVELS) * level
            )
            value = 0.5 * signed + (0.5 * jnp.tanh(inside)) * weighted
            merged[pl.ds(start, width), cols] = value.astype(bf16)

        if chunk + 2 < rows:
            load_bits(chunk + 2).start()

    live_all = info_ref[own, 0:1]
    count_here = jnp.sum(live_all, axis=0, keepdims=True)
    share = 1.0 / count_here

    def column_stats(values):
        mean = jnp.sum(values * live_all, axis=0, keepdims=True) * share
        apart = values - mean
        return mean, jnp.sum(live_all * apart * apart, axis=0, keepdims=True)

    def counts(step):
        return first_msg[step, 2:3, 0:1]

    def combine(slots):
        number = counts(0)
        mean = slots[0, 0:1] * counts(0)
        spread = slots[0, 1:2]
        for step in range(1, size):
            number = number + counts(step)
            mean = mean + slots[step, 0:1] * counts(step)
            spread = spread + slots[step, 1:2]
        mean = mean / number
        for step in range(size):
            apart = slots[step, 0:1] - mean
            spread = spread + counts(step) * apart * apart
        return mean, lax.rsqrt(spread / number + EPS), number

    load_u.wait()
    load_cot.wait()
    drop_chunk(0)
    first_msg[0, 2:3] = jnp.broadcast_to(count_here, (1, inner))
    first_msg[0, 3:4] = jnp.zeros((1, inner), f32)
    zc_out = za_out = zb_out = r1_out = None
    u1_out = pltpu.make_async_copy(u1, u1_hbm, out_sem.at[0])
    for layer in range(2):
        x_ref = (u0, u1)[layer]
        need_weight(0, layer)
        slots = first_msg if layer == 0 else msg.at[0]

        @pl.loop(0, inner // 256)
        def _(tile):
            cols = pl.ds(pl.multiple_of(tile * 256, 256), 256)
            values = jnp.dot(x_ref[...], wr[layer, :, cols], preferred_element_type=f32)
            a_ref[:, cols] = values
            mean, spread = column_stats(values)
            slots[0, 0:1, cols] = mean
            slots[0, 1:2, cols] = spread

        if layer == 1:
            for copy in (za_out, zb_out, r1_out, zc_out):
                copy.wait()
            u1_out.start()
        sends = link.copies(3 * layer, slots)
        for copy in sends:
            copy.start()
        a_edges = (a_ref.at[pl.ds(0, width)], a_ref.at[pl.ds(pixels - width, width)])
        a_halo = halo.at[2 * layer]
        link.start_edges(2 * layer, *a_edges, a_halo)
        if layer == 0:
            for kind in range(4):
                pushed_vector(kind).wait()
        drop_chunk(1 + 3 * layer)
        for copy in sends:
            copy.wait()
        mean, inverse, number = combine(slots)
        stat[layer, 0:1], stat[layer, 1:2] = mean, inverse
        rs_ref[layer, 0:1] = inverse
        rs_ref[layer, 2:3] = jnp.broadcast_to(number, (1, inner))
        link.wait_edges(2 * layer, *a_edges, a_halo)

        def first_act(row, values, inside):
            normed = (values - stat[layer, 0:1]) * stat[layer, 1:2]
            affine = normed * igs[layer, 0:1] + ibs[layer, 0:1]
            act = affine * (1.0 / (1.0 + jnp.exp(-affine)))
            if inside is not None:
                act = jnp.where(inside, act, 0.0)
            here = pl.ds(pl.multiple_of(row * width, 16), width)
            masks = info_ref[pl.ds(width, width), :]
            cat[here, 0:inner] = (pltpu.roll(act, 1, 0) * masks[:, 1:2]).astype(bf16)
            cat[here, inner : 2 * inner] = act.astype(bf16)
            cat[here, 2 * inner : 3 * inner] = (
                pltpu.roll(act, width - 1, 0) * masks[:, 2:3]
            ).astype(bf16)
            return normed

        first_act(0, a_halo[0], me > 0)
        first_act(rows + 1, a_halo[1], me < size - 1)

        @pl.loop(0, rows)
        def _(row):
            here = pl.ds(pl.multiple_of(row * width, 16), width)
            za[here] = first_act(row + 1, a_ref[here], None).astype(bf16)

        za_out = pltpu.make_async_copy(za, za_hbm.at[layer], out_sem.at[1])
        r1_out = pltpu.make_async_copy(
            cat.at[:, pl.ds(inner, inner)], r1_hbm.at[layer], out_sem.at[2]
        )
        za_out.start()
        r1_out.start()
        need_weight(1, layer)
        slots = msg.at[1 + 2 * layer]

        @pl.loop(0, inner // 256)
        def _(tile):
            cols = pl.ds(pl.multiple_of(tile * 256, 256), 256)
            values = None
            for tap in range(3):
                table = ws[layer, 3 * tap : 3 * tap + 3, :, cols].reshape(3 * inner, 256)
                value = jnp.dot(
                    cat[tap * width : tap * width + pixels], table, preferred_element_type=f32
                )
                values = value if values is None else values + value
            b_ref[:, cols] = values
            mean, spread = column_stats(values)
            slots[0, 0:1, cols] = mean
            slots[0, 1:2, cols] = spread

        sends = link.copies(3 * layer + 1, slots)
        for copy in sends:
            copy.start()
        b_edges = (b_ref.at[pl.ds(0, width)], b_ref.at[pl.ds(pixels - width, width)])
        b_halo = halo.at[2 * layer + 1]
        link.start_edges(2 * layer + 1, *b_edges, b_halo)
        drop_chunk(2 + 3 * layer)
        for copy in sends:
            copy.wait()
        mean, inverse, _ = combine(slots)
        stat[layer, 2:3], stat[layer, 3:4] = mean, inverse
        rs_ref[layer, 1:2] = inverse

        @pl.loop(0, rows)
        def _(row):
            here = pl.ds(pl.multiple_of(row * width, 16), width)
            normed = (b_ref[here] - stat[layer, 2:3]) * stat[layer, 3:4]
            zb[pl.ds(pl.multiple_of((row + 1) * width, 16), width)] = normed.astype(bf16)
            affine = normed * igs[layer, 1:2] + ibs[layer, 1:2]
            r2[here] = (affine * (1.0 / (1.0 + jnp.exp(-affine)))).astype(bf16)

        need_weight(2, layer)
        slots = msg_c.at[layer]

        @pl.loop(0, channels // 256)
        def _(tile):
            cols = pl.ds(pl.multiple_of(tile * 256, 256), 256)
            values = jnp.dot(r2[...], we[layer, :, cols], preferred_element_type=f32)
            e_ref[:, cols] = values
            mean, spread = column_stats(values)
            slots[0, 0:1, cols] = mean
            slots[0, 1:2, cols] = spread

        sends = link.copies(3 * layer + 2, slots)
        for copy in sends:
            copy.start()
        link.wait_edges(2 * layer + 1, *b_edges, b_halo)
        for side, row in ((0, 0), (1, rows + 1)):
            normed = (b_halo[side] - stat[layer, 2:3]) * stat[layer, 3:4]
            zb[row * width : (row + 1) * width] = normed.astype(bf16)
        zb_out = pltpu.make_async_copy(zb, zb_hbm.at[layer], out_sem.at[3])
        zb_out.start()
        drop_chunk(3 + 3 * layer)
        if layer == 1:
            drop_chunk(7)
            pltpu.make_async_copy(merged, merged_hbm, out_sem.at[4]).start()
        for copy in sends:
            copy.wait()
        mean, inverse, _ = combine(slots)
        stat_c[0:1], stat_c[1:2] = mean, inverse
        rc_ref[layer] = inverse
        out_ref = (u1, u0)[layer]

        @pl.loop(0, rows * (channels // TILE))
        def _(chunk):
            row, tile = chunk // (channels // TILE), chunk % (channels // TILE)
            here = pl.ds(pl.multiple_of(row * width, 16), width)
            cols = pl.ds(pl.multiple_of(tile * TILE, TILE), TILE)
            normed = (e_ref[here, cols] - stat_c[0:1, cols]) * stat_c[1:2, cols]
            zc[here, cols] = normed.astype(bf16)
            total = normed * ogs[layer, :, cols] + obs[layer, :, cols] + x_ref[here, cols].astype(f32)
            out_ref[here, cols] = (total * (1.0 / (1.0 + jnp.exp(-total)))).astype(bf16)

        zc_out = pltpu.make_async_copy(zc, zc_hbm.at[layer], out_sem.at[5])
        zc_out.start()

    heads_ref[...] = (
        lax.dot_general(u0[...], hwt_ref[...], BESIDE, preferred_element_type=f32) + hb_ref[...]
    )
    target = cot[...].astype(f32).reshape(pixels, -1) * live_all
    hbg_ref[...] = jnp.sum(target, axis=0, keepdims=True)
    target = target.astype(bf16)

    @pl.loop(0, channels // 256)
    def _(tile):
        cols = pl.ds(pl.multiple_of(tile * 256, 256), 256)
        hwg_ref[:, cols] = lax.dot_general(target, u0[:, cols], ACROSS, preferred_element_type=f32)

    for copy in (za_out, zb_out, r1_out, zc_out, u1_out):
        copy.wait()
    pltpu.make_async_copy(merged, merged_hbm, out_sem.at[4]).wait()
    for kind in range(3):
        pushed(kind).wait_send()
        for layer in range(2):
            save_weight(kind, layer).wait()


def forward(u, bits, cot, wr, ws, we, ig, ib, og, ob, hwt, hb, info):
    size = lax.axis_size("dp")
    pixels, channels = u.shape
    inner = wr.shape[1]
    _, rows, width, head_cols = cot.shape
    f32, bf16 = jnp.float32, jnp.bfloat16
    padded = pixels + 2 * width
    anywhere = pl.BlockSpec(memory_space=pl.ANY)
    vmem = pl.BlockSpec(memory_space=pltpu.VMEM)

    def out(kind, *shape):
        return jax.ShapeDtypeStruct(shape, kind)

    return pl.pallas_call(
        functools.partial(forward_kernel, size),
        out_shape=[
            out(f32, pixels, head_cols),
            out(f32, head_cols, channels),
            out(f32, 1, head_cols),
            out(f32, 2, 2, inner),
            out(f32, 2, 2, inner),
            out(f32, 2, 1, channels),
            out(f32, 2, 1, channels),
            out(f32, 2, 8, inner),
            out(f32, 2, 1, channels),
            out(bf16, pixels, channels),
            out(bf16, pixels, channels),
            out(bf16, 2, pixels, channels),
            out(bf16, 2, pixels, inner),
            out(bf16, 2, padded, inner),
            out(bf16, 2, padded, inner),
            out(bf16, 2, channels, inner),
            out(bf16, 2, 9, inner, inner),
            out(bf16, 2, inner, channels),
        ],
        in_specs=[anywhere] * 6 + [vmem] * 7,
        out_specs=[vmem] * 9 + [anywhere] * 9,
        scratch_shapes=[
            pltpu.VMEM((2, channels, inner), bf16),
            pltpu.VMEM((2, 9, inner, inner), bf16),
            pltpu.VMEM((2, inner, channels), bf16),
            pltpu.VMEM((pixels, channels), bf16),
            pltpu.VMEM((pixels, channels), bf16),
            pltpu.VMEM((pixels, inner), f32),
            pltpu.VMEM((pixels, inner), f32),
            pltpu.VMEM((pixels, channels), f32),
            pltpu.VMEM((padded, 3 * inner), bf16),
            pltpu.VMEM((pixels, inner), bf16),
            pltpu.VMEM((pixels, inner), bf16),
            pltpu.VMEM((padded, inner), bf16),
            pltpu.VMEM((pixels, channels), bf16),
            pltpu.VMEM((pixels, channels), bf16),
            pltpu.VMEM((2, width, channels), jnp.int32),
            pltpu.VMEM((rows, width, head_cols), bf16),
            pltpu.VMEM((4, 2, width, inner), f32),
            pltpu.VMEM((4, size, 2, inner), f32),
            pltpu.VMEM((2, size, 2, channels), f32),
            pltpu.VMEM((size, 4, inner), f32),
            pltpu.VMEM((2, 8, inner), f32),
            pltpu.VMEM((2, channels), f32),
            pltpu.SemaphoreType.DMA((6, size)),
            pltpu.SemaphoreType.DMA((6, size)),
            pltpu.SemaphoreType.DMA((4, 2)),
            pltpu.SemaphoreType.DMA((4, 2)),
            pltpu.SemaphoreType.DMA((3,)),
            pltpu.SemaphoreType.DMA((7,)),
            pltpu.SemaphoreType.DMA((7,)),
            pltpu.SemaphoreType.DMA((3, 2)),
            pltpu.SemaphoreType.DMA((2,)),
            pltpu.SemaphoreType.DMA((2,)),
            pltpu.SemaphoreType.DMA((6,)),
        ],
        compiler_params=pltpu.CompilerParams(
            collective_id=1, has_side_effects=True, vmem_limit_bytes=LIMIT
        ),
    )(u, bits, cot, wr, ws, we, ig, ib, og, ob, hwt, hb, info)


def backward_kernel(
    size,
    reducer,
    u0_hbm,
    u1_hbm,
    merged_hbm,
    zc_hbm,
    za_hbm,
    zb_hbm,
    r1_hbm,
    wr_all,
    ws_all,
    we_all,
    igs,
    ibs,
    ogs,
    obs,
    rs_ref,
    rc_ref,
    hwg_ref,
    hbg_ref,
    info_ref,
    grad_hbm,
    expand_hbm,
    spatial_hbm,
    reduce_hbm,
    small_hbm,
    wr,
    ws,
    we,
    u_ref,
    d_ref,
    zc,
    za,
    zb,
    r1,
    r2,
    wide,
    dz_ref,
    da,
    small,
    halo,
    msg,
    msg_c,
    part_sum,
    sums,
    sums_c,
    send_sem,
    recv_sem,
    edge_send,
    edge_recv,
    in_sem,
    out_sem,
    *scratch,
):
    reducer.bind((expand_hbm, spatial_hbm, reduce_hbm, small_hbm), scratch)
    link = Exchange(size, send_sem, recv_sem, edge_send, edge_recv)
    section, me = link.section, link.me
    pixels, channels = d_ref.shape
    inner = da.shape[1]
    width = halo.shape[2]
    rows = pixels // width
    across = channels // TILE
    f32, bf16 = jnp.float32, jnp.bfloat16
    own = pl.ds(width, pixels)
    de, cat = wide.at[pl.ds(0, pixels)], wide.at[:, pl.ds(0, 3 * inner)]

    def loads(layer):
        return {
            "zc": pltpu.make_async_copy(zc_hbm.at[layer], zc, in_sem.at[0]),
            "za": pltpu.make_async_copy(za_hbm.at[layer], za, in_sem.at[1]),
            "zb": pltpu.make_async_copy(zb_hbm.at[layer], zb, in_sem.at[2]),
            "r1": pltpu.make_async_copy(r1_hbm.at[layer], r1, in_sem.at[3]),
            "wr": pltpu.make_async_copy(wr_all.at[layer], wr, in_sem.at[4]),
            "ws": pltpu.make_async_copy(ws_all.at[layer], ws, in_sem.at[5]),
            "we": pltpu.make_async_copy(we_all.at[layer], we, in_sem.at[6]),
            "u": pltpu.make_async_copy((u0_hbm, u1_hbm)[layer], u_ref.at[layer], in_sem.at[7 + layer]),
        }

    load_d = pltpu.make_async_copy(merged_hbm, d_ref, in_sem.at[9])
    first, second = loads(1), loads(0)
    load_d.start()
    for name in ("u", "zc", "we", "zb", "ws", "za", "r1", "wr"):
        first[name].start()
    second["u"].start()
    link.greet()
    live_all = info_ref[own, 0:1]

    def put_tile(layer, tile, make):
        unit = (1 - layer) * 3 * reducer.block_groups + tile * reducer.per_tile

        @pl.loop(0, 2)
        def _(side):
            cols = pl.ds(pl.multiple_of(side * 256, 256), 256)
            value = make(side).astype(bf16)
            for part in range(reducer.per_tile):
                lines = slice(part * reducer.lines, (part + 1) * reducer.lines)
                reducer.slot(unit + part)[:, cols] = value[lines]

        reducer.after_tile(layer, tile)

    def column_sums(values):
        return jnp.sum(values, axis=0, keepdims=True)

    def total_of(slots):
        found = slots[0]
        for step in range(1, size):
            found = found + slots[step]
        return found

    def expand_tiles(layer):
        @pl.loop(0, across)
        def _(tile):
            def make(side):
                cols = pl.ds(pl.multiple_of(tile * TILE + side * 256, 256), 256)
                return lax.dot_general(r2[...], de[:, cols], ACROSS, preferred_element_type=f32)

            put_tile(layer, tile, make)

    def spatial_tiles(layer):
        @pl.loop(0, 9)
        def _(tap):
            shift, side_step = tap // 3, tap % 3

            def make(side):
                at = pl.ds(pl.multiple_of(shift * width, 16), pixels)
                cols = pl.ds(pl.multiple_of(side_step * inner + side * 256, 256), 256)
                return lax.dot_general(r1[at], cat[own, cols], ACROSS, preferred_element_type=f32)

            put_tile(layer, across + tap, make)

    def reduce_tiles_of(layer):
        @pl.loop(0, across)
        def _(tile):
            def make(side):
                cols = pl.ds(pl.multiple_of(side * 256, 256), 256)
                lines = pl.ds(pl.multiple_of(tile * TILE, TILE), TILE)
                return lax.dot_general(
                    u_ref[layer, :, lines], da[:, cols], ACROSS, preferred_element_type=f32
                )

            put_tile(layer, across + 9 + tile, make)

    def small_unit(layer):
        half = channels // 2
        head_cols = hwg_ref.shape[0]
        small[...] = jnp.zeros_like(small)
        for k in range(2):
            at = layer * half + k * TILE
            small[k * head_cols : (k + 1) * head_cols] = hwg_ref[:, at : at + TILE]
        row = 2 * head_cols
        small[row : row + 1, 0:head_cols] = hbg_ref[...]
        only = (me == 0).astype(f32)
        small[row + 8 : row + 9] = sums[0, 1:2] * only
        small[row + 9 : row + 10] = sums[1, 1:2] * only
        small[row + 10 : row + 11] = sums[0, 0:1] * only
        small[row + 11 : row + 12] = sums[1, 0:1] * only
        for k in range(across):
            cols = slice(k * TILE, (k + 1) * TILE)
            small[row + 12 + k : row + 13 + k] = sums_c[1:2, cols] * only
            small[row + 12 + across + k : row + 13 + across + k] = sums_c[0:1, cols] * only
        unit = (1 - layer) * 3 * reducer.block_groups + reducer.real - 1
        target = reducer.slot(unit)
        target[...] = jnp.zeros(target.shape, bf16)
        target[0 : small.shape[0]] = small[...].astype(bf16)
        reducer.tick((2 - layer) * reducer.block_groups - 1)

    load_d.wait()
    for layer in (1, 0):
        now = (second, first)[layer]
        now["u"].wait()
        now["zc"].wait()
        part_sum[...] = jnp.zeros_like(part_sum)

        @pl.loop(0, rows * across)
        def _(chunk):
            row, tile = chunk // across, chunk % across
            here = pl.ds(pl.multiple_of(row * width, 16), width)
            cols = pl.ds(pl.multiple_of(tile * TILE, TILE), TILE)
            normed = zc[here, cols].astype(f32)
            total = (
                normed * ogs[layer, :, cols]
                + obs[layer, :, cols]
                + u_ref[layer, here, cols].astype(f32)
            )
            _, slope = silu_parts(total)
            dt = d_ref[here, cols].astype(f32) * slope
            d_ref[here, cols] = dt.astype(bf16)
            part_sum[0, :, cols] += folded(dt)
            part_sum[1, :, cols] += folded(dt * normed)

        slots = msg_c.at[1 - layer]
        slots[0, 0:1] = column_sums(part_sum[0])
        slots[0, 1:2] = column_sums(part_sum[1])
        sends = link.copies(3 * layer, slots)
        for copy in sends:
            copy.start()
        if layer == 0:
            reduce_tiles_of(1)
            small_unit(1)
        for copy in sends:
            copy.wait()
        sums_c[...] = total_of(slots)
        number = rs_ref[layer, 2:3, 0:1]
        share = 1.0 / number

        @pl.loop(0, rows * across)
        def _(chunk):
            row, tile = chunk // across, chunk % across
            here = pl.ds(pl.multiple_of(row * width, 16), width)
            cols = pl.ds(pl.multiple_of(tile * TILE, TILE), TILE)
            live = info_ref[pl.ds(pl.multiple_of((row + 1) * width, 16), width), 0:1]
            normed = zc[here, cols].astype(f32)
            away = (sums_c[0:1, cols] + normed * sums_c[1:2, cols]) * share
            scale = rc_ref[layer, :, cols] * ogs[layer, :, cols]
            value = scale * (d_ref[here, cols].astype(f32) - live * away)
            de[here, cols] = value.astype(bf16)

        now["we"].wait()
        now["zb"].wait()
        slots = msg.at[2 * layer]

        @pl.loop(0, inner // 256)
        def _(tile):
            cols = pl.ds(pl.multiple_of(tile * 256, 256), 256)
            dr2 = lax.dot_general(de[...], we[cols], BESIDE, preferred_element_type=f32)
            normed = zb[own, cols].astype(f32)
            act, slope = silu_parts(normed * igs[layer, 1:2, cols] + ibs[layer, 1:2, cols])
            r2[:, cols] = act.astype(bf16)
            dz = dr2 * slope
            dz_ref[:, cols] = dz
            slots[0, 0:1, cols] = column_sums(dz)
            slots[0, 1:2, cols] = column_sums(dz * normed)

        sends = link.copies(3 * layer + 1, slots)
        for copy in sends:
            copy.start()
        edges = (dz_ref.at[pl.ds(0, width)], dz_ref.at[pl.ds(pixels - width, width)])
        landing = halo.at[layer]
        link.start_edges(layer, *edges, landing)
        if layer == 1:
            second["zc"].start()
            second["we"].start()
        expand_tiles(layer)
        for copy in sends:
            copy.wait()
        sums[1] = total_of(slots)
        link.wait_edges(layer, *edges, landing)

        def db_row(row, dz, inside):
            here = pl.ds(pl.multiple_of(row * width, 16), width)
            live = info_ref[here, 0:1]
            normed = zb[here].astype(f32)
            away = (sums[1, 0:1] + normed * sums[1, 1:2]) * share
            value = (rs_ref[layer, 1:2] * igs[layer, 1:2]) * (dz - live * away)
            if inside is not None:
                value = jnp.where(inside, value, 0.0)
            masks = info_ref[pl.ds(width, width), :]
            cat[here, 0:inner] = (pltpu.roll(value, width - 1, 0) * masks[:, 2:3]).astype(bf16)
            cat[here, inner : 2 * inner] = value.astype(bf16)
            cat[here, 2 * inner : 3 * inner] = (
                pltpu.roll(value, 1, 0) * masks[:, 1:2]
            ).astype(bf16)

        db_row(0, landing[0], me > 0)
        db_row(rows + 1, landing[1], me < size - 1)

        @pl.loop(0, rows)
        def _(row):
            db_row(row + 1, dz_ref[pl.ds(pl.multiple_of(row * width, 16), width)], None)

        if layer == 1:
            second["zb"].start()
        now["ws"].wait()
        now["za"].wait()
        slots = msg.at[2 * layer + 1]

        @pl.loop(0, inner // 256)
        def _(tile):
            cols = pl.ds(pl.multiple_of(tile * 256, 256), 256)
            dr1 = None
            for tap in range(9):
                start = (2 - tap // 3) * width
                block = cat[start : start + pixels, (tap % 3) * inner : (tap % 3 + 1) * inner]
                value = lax.dot_general(block, ws[tap, cols], BESIDE, preferred_element_type=f32)
                dr1 = value if dr1 is None else dr1 + value
            normed = za[:, cols].astype(f32)
            _, slope = silu_parts(normed * igs[layer, 0:1, cols] + ibs[layer, 0:1, cols])
            dz = dr1 * slope
            dz_ref[:, cols] = dz
            slots[0, 0:1, cols] = column_sums(dz)
            slots[0, 1:2, cols] = column_sums(dz * normed)

        sends = link.copies(3 * layer + 2, slots)
        for copy in sends:
            copy.start()
        if layer == 1:
            second["ws"].start()
        now["r1"].wait()
        spatial_tiles(layer)
        for copy in sends:
            copy.wait()
        sums[0] = total_of(slots)
        if layer == 1:
            second["r1"].start()

        @pl.loop(0, rows)
        def _(row):
            here = pl.ds(pl.multiple_of(row * width, 16), width)
            live = info_ref[pl.ds(pl.multiple_of((row + 1) * width, 16), width), 0:1]
            away = (sums[0, 0:1] + za[here].astype(f32) * sums[0, 1:2]) * share
            value = (rs_ref[layer, 0:1] * igs[layer, 0:1]) * (dz_ref[here] - live * away)
            da[here] = value.astype(bf16)

        if layer == 1:
            second["za"].start()
        now["wr"].wait()

        @pl.loop(0, channels // 256)
        def _(tile):
            cols = pl.ds(pl.multiple_of(tile * 256, 256), 256)
            du = lax.dot_general(da[...], wr[cols], BESIDE, preferred_element_type=f32)
            d_ref[:, cols] = (du + d_ref[:, cols].astype(f32)).astype(bf16)

        if layer == 1:
            second["wr"].start()
    out = pltpu.make_async_copy(d_ref, grad_hbm, out_sem)
    out.start()
    reduce_tiles_of(0)
    small_unit(0)
    reducer.drain()
    out.wait()


def backward(u0, u1, merged, zc, za, zb, r1, wr, ws, we, igs, ibs, ogs, obs, rs, rc, hwg, hbg, info):
    size = lax.axis_size("dp")
    pixels, channels = u0.shape
    inner = za.shape[2]
    padded = zb.shape[1]
    width = (padded - pixels) // 2
    f32, bf16 = jnp.float32, jnp.bfloat16
    anywhere = pl.BlockSpec(memory_space=pl.ANY)
    vmem = pl.BlockSpec(memory_space=pltpu.VMEM)
    taps = ws.shape[1]
    reducer = Reducer(size, 2 * (channels // TILE) + taps)
    totals = [(TILE, channels), (taps, TILE, TILE), (channels, TILE), (reducer.lines, TILE)]
    return pl.pallas_call(
        functools.partial(backward_kernel, size, reducer),
        out_shape=[
            jax.ShapeDtypeStruct((pixels, channels), bf16),
        ]
        + [jax.ShapeDtypeStruct(shape, bf16) for shape in totals],
        in_specs=[anywhere] * 10 + [vmem] * 9,
        out_specs=[anywhere] * 5,
        scratch_shapes=[
            pltpu.VMEM((channels, inner), bf16),
            pltpu.VMEM((9, inner, inner), bf16),
            pltpu.VMEM((inner, channels), bf16),
            pltpu.VMEM((2, pixels, channels), bf16),
            pltpu.VMEM((pixels, channels), bf16),
            pltpu.VMEM((pixels, channels), bf16),
            pltpu.VMEM((pixels, inner), bf16),
            pltpu.VMEM((padded, inner), bf16),
            pltpu.VMEM((padded, inner), bf16),
            pltpu.VMEM((pixels, inner), bf16),
            pltpu.VMEM((padded, channels), bf16),
            pltpu.VMEM((pixels, inner), f32),
            pltpu.VMEM((pixels, inner), bf16),
            pltpu.VMEM((128, TILE), f32),
            pltpu.VMEM((2, 2, width, inner), f32),
            pltpu.VMEM((4, size, 2, inner), f32),
            pltpu.VMEM((2, size, 2, channels), f32),
            pltpu.VMEM((2, 8, channels), f32),
            pltpu.VMEM((2, 2, inner), f32),
            pltpu.VMEM((2, channels), f32),
            pltpu.SemaphoreType.DMA((6, size)),
            pltpu.SemaphoreType.DMA((6, size)),
            pltpu.SemaphoreType.DMA((2, 2)),
            pltpu.SemaphoreType.DMA((2, 2)),
            pltpu.SemaphoreType.DMA((10,)),
            pltpu.SemaphoreType.DMA,
        ]
        + reducer.scratch(),
        compiler_params=pltpu.CompilerParams(
            collective_id=2, has_side_effects=True, vmem_limit_bytes=63 * 2**20
        ),
    )(u0, u1, merged, zc, za, zb, r1, wr, ws, we, igs, ibs, ogs, obs, rs, rc, hwg, hbg, info)


def pixel_info(pixel_mask, starts):
    size = lax.axis_size("dp")
    rows, width = pixel_mask.shape
    up = [(i, i + 1) for i in range(size - 1)]
    down = [(j, i) for i, j in up]
    before = lax.ppermute(pixel_mask[rows - 1 :], "dp", up)
    after = lax.ppermute(pixel_mask[:1], "dp", down)
    live = jnp.concatenate([before, pixel_mask, after])
    columns = jnp.arange(width, dtype=jnp.int32)
    crop = jnp.sum((columns[:, None] >= starts[None, :]).astype(jnp.int32), axis=1)
    outside = jnp.full((1,), -1, jnp.int32)
    left = jnp.concatenate([outside, crop[:-1]]) == crop
    right = jnp.concatenate([crop[1:], outside]) == crop
    lane = jnp.arange(128, dtype=jnp.int32)
    first = jnp.where(lane == 0, live[:, :, None], 0)
    links = jnp.where(lane == 1, left[:, None].astype(jnp.int32), 0)
    links = links + jnp.where(lane == 2, right[:, None].astype(jnp.int32), 0)
    return (first + links[None]).astype(jnp.float32).reshape(-1, 128)


def pick(array, index):
    return lax.dynamic_index_in_dim(array, index, 0, keepdims=False)


def local(
    canvases,
    crop_starts,
    pixel_mask,
    drop_bits,
    reduce_weight,
    spatial_weight,
    expand_weight,
    inner_gain,
    inner_bias,
    outer_gain,
    outer_bias,
    head_weight,
    head_bias,
    head_cotangent,
):
    section = lax.axis_index("section")
    first = section == 0
    rows, width, channels = canvases.shape[1:]
    head_cols = head_weight.shape[1]
    pixels = rows * width
    flat = canvases.reshape(pixels, channels)
    info = pixel_info(pick(pixel_mask, section), pick(crop_starts, section))
    heads, hwg, hbg, igs, ibs, ogs, obs, rs, rc, merged, u1, zc, za, zb, r1, wr, ws, we = forward(
        flat,
        drop_bits,
        head_cotangent,
        reduce_weight[0],
        spatial_weight[0],
        expand_weight[0],
        inner_gain[0],
        inner_bias[0],
        outer_gain,
        outer_bias,
        head_weight.T,
        head_bias[None],
        info,
    )
    grad, expand_total, spatial_total, reduce_total, small = backward(
        flat, u1, merged, zc, za, zb, r1, wr, ws, we, igs, ibs, ogs, obs, rs, rc, hwg, hbg, info
    )
    small = small.astype(jnp.float32)
    half = channels // 2
    across = channels // TILE
    head_w_out = jnp.concatenate([small[:head_cols].T, small[head_cols : 2 * head_cols].T])
    row = 2 * head_cols
    cut = head_cols // 2
    head_b_out = jnp.where(first, small[row, :cut], small[row, cut:head_cols])
    norms = small[row + 8 :]
    return (
        heads.reshape(1, rows, width, head_cols),
        grad.reshape(1, rows, width, channels),
        reduce_total.astype(jnp.float32)[None],
        spatial_total.astype(jnp.float32)[None],
        expand_total.astype(jnp.float32)[None],
        norms[0:2][None],
        norms[2:4][None],
        norms[4 : 4 + across].reshape(1, channels),
        norms[4 + across : 4 + 2 * across].reshape(1, channels),
        head_w_out,
        head_b_out,
    )


def solution(mesh):
    placed = (
        P("section", "dp", None, None),
        P(),
        P(None, "dp", None),
        P(None, "dp", None, None),
        P("section", None, None),
        P("section", None, None, None),
        P("section", None, None),
        P("section", None, None),
        P("section", None, None),
        P("section", None),
        P("section", None),
        P(),
        P(),
        P(None, "dp", None, None),
    )
    return jax.shard_map(
        local,
        mesh=mesh,
        in_specs=placed,
        out_specs=(
            P("section", "dp", None, None),
            P("section", "dp", None, None),
            P("section", None, None),
            P("section", None, None, None),
            P("section", None, None),
            P("section", None, None),
            P("section", None, None),
            P("section", None),
            P("section", None),
            P("section", None),
            P("section"),
        ),
        check_vma=False,
    )
```

```python
import functools
import math

import jax
import jax.numpy as jnp
from jax import lax
from jax.experimental import pallas as pl
from jax.experimental.pallas import tpu as pltpu
from jax.sharding import PartitionSpec as P

TASKS = 3
HEAD_OUT = 16

EPS = 1e-05
SOFT = 0.05
SHARP = 0.1
LEVELS = 1024.0
ACROSS = (((0,), (0,)), ((), ()))
BESIDE = (((1,), (1,)), ((), ()))
MESH = pl.DeviceIdType.MESH
TILE = 512
LIMIT = 56 * 2**20


def grid_of(size):
    side = math.isqrt(size // 4)
    assert side * side * 4 == size
    return (4, side, side)


class Reducer:
    IDLE = 1

    def __init__(self, size, across, taps):
        self.size = size
        nz, ny, nx = grid_of(size)
        self.strides = {}
        for axis, count, stride in (("x", nx, 1), ("y", ny, nx), ("z", nz, nx * ny)):
            for level in range(count.bit_length() - 1):
                self.strides[axis + str(level)] = stride << level
        later = [bit for bit in self.strides if bit[1] != "0"]
        self.orders = [[a + "0" for a in order] + later for order in ("xyz", "yxz", "zxy")]
        self.levels = len(self.strides)
        self.pace, self.lag = (2, 3) if self.levels <= 4 else (3, 2)
        self.row_bits = [bit for bit in self.strides if bit[0] != "x"]
        self.x_bits = [bit for bit in self.strides if bit[0] == "x"]
        self.shape = (2,) * len(self.row_bits) + (16, TILE)
        self.half = 16 << len(self.row_bits)
        self.lines = 2 * self.half
        self.per_tile = TILE // self.lines
        self.counts = [across * self.per_tile, taps * self.per_tile, across * self.per_tile + 1]
        self.real = sum(self.counts)
        self.bursts = [-(-count // 3) for count in self.counts]
        self.starts, self.bases = [], []
        group = unit = 0
        for burst, count in zip(self.bursts, self.counts):
            self.starts.append(group)
            self.bases.append(unit)
            group += burst + self.IDLE
            unit += count
        self.block_groups = group
        self.stages = 2 * self.levels + 3
        self.slots = 3 * (2 + -(-self.lag * self.levels // self.pace))

    def scratch(self):
        units, bf16 = 2 * self.real, jnp.bfloat16
        return [
            pltpu.VMEM((self.slots, 2) + self.shape, bf16),
            pltpu.VMEM((units,) + self.shape, bf16),
            pltpu.VMEM((units,) + self.shape, bf16),
            pltpu.SemaphoreType.DMA((units, 2)),
            pltpu.SemaphoreType.DMA((units, 2)),
            pltpu.SemaphoreType.DMA((units, 2 * self.levels)),
            pltpu.SemaphoreType.DMA((units, 2 * self.levels)),
        ]

    def totals(self, across, taps):
        tail = (self.per_tile, 2) + self.shape
        return [
            (self.per_tile, 2) + self.shape[:-1] + (across * TILE,),
            (taps,) + tail,
            (across,) + tail,
            (2,) + self.shape,
        ]

    def bind(self, total, scratch):
        self.total = total
        (
            self.ring,
            self.res,
            self.land,
            self.pair_send,
            self.pair_recv,
            self.send_sem,
            self.recv_sem,
        ) = scratch
        self.section, self.me = lax.axis_index("section"), lax.axis_index("dp")
        self.bit = {bit: (self.me // stride) % 2 for bit, stride in self.strides.items()}
        self.clock = 0

    def partner(self, bit):
        return (self.section, self.me + (1 - 2 * self.bit[bit]) * self.strides[bit])

    def slot(self, unit):
        if isinstance(unit, int):
            return unit % self.slots
        return lax.rem(unit, self.slots)

    def region(self, order, level, flip):
        place = {bit: self.bit[bit] for bit in order[:level]}
        if flip:
            place[order[level - 1]] = 1 - place[order[level - 1]]
        rows = tuple(place.get(bit, slice(None)) for bit in self.row_bits)
        cols, start, width = slice(None), 0, TILE
        for bit in self.x_bits:
            if bit in place:
                width //= 2
                start = start + place[bit] * width
                cols = pl.ds(pl.multiple_of(start, width), width)
        return rows + (slice(None), cols)

    def pair(self, unit):
        return pltpu.make_async_remote_copy(
            src_ref=self.ring.at[self.slot(unit), 1 - self.section],
            dst_ref=self.res.at[unit],
            send_sem=self.pair_send.at[unit, 1],
            recv_sem=self.pair_recv.at[unit, 0],
            device_id=(1 - self.section, self.me),
            device_id_type=MESH,
        )

    def acc(self, unit):
        return self.ring.at[self.slot(unit), self.section]

    def halve(self, unit, order, level):
        return pltpu.make_async_remote_copy(
            src_ref=self.acc(unit).at[self.region(order, level + 1, True)],
            dst_ref=self.land.at[(unit,) + self.region(order, level + 1, False)],
            send_sem=self.send_sem.at[unit, level],
            recv_sem=self.recv_sem.at[unit, level],
            device_id=self.partner(order[level]),
            device_id_type=MESH,
        )

    def halved(self, unit, order, level):
        self.halve(unit, order, level).wait()
        keep = self.region(order, level + 1, False)
        kept = self.acc(unit).at[keep]
        came = self.land.at[(unit,) + self.region(order, level + 1, True)]
        target = self.res.at[(unit,) + keep] if level == self.levels - 1 else kept
        total = kept[...].astype(jnp.float32) + came[...].astype(jnp.float32)
        target[...] = total.astype(jnp.bfloat16)

    def double(self, unit, order, level):
        ref = self.res.at[(unit,) + self.region(order, level + 1, False)]
        return pltpu.make_async_remote_copy(
            src_ref=ref,
            dst_ref=ref,
            send_sem=self.send_sem.at[unit, self.levels + level],
            recv_sem=self.recv_sem.at[unit, self.levels + level],
            device_id=self.partner(order[level]),
            device_id_type=MESH,
        )

    def places(self, index):
        expand, spatial, reduce, small = self.total
        tile, part = index // self.per_tile, index % self.per_tile
        across, taps = reduce.shape[0], spatial.shape[0]
        half = self.section
        inner = (slice(None),) * (len(self.shape) - 1)

        def in_expand():
            cols = tile * TILE if isinstance(tile, int) else pl.multiple_of(tile * TILE, TILE)
            return expand.at[(part, half) + inner + (pl.ds(cols, TILE),)]

        return [
            (0 <= tile < across if isinstance(tile, int) else tile < across, in_expand),
            (
                self.both(tile >= across, tile < across + taps),
                lambda: spatial.at[tile - across, part, half],
            ),
            (
                self.both(tile >= across + taps, index < self.real - 1),
                lambda: reduce.at[tile - across - taps, part, half],
            ),
            (index == self.real - 1, lambda: small.at[half]),
        ]

    @staticmethod
    def both(first, second):
        if isinstance(first, bool) and isinstance(second, bool):
            return first and second
        return jnp.logical_and(first, second)

    def final(self, unit, target):
        here = pltpu.make_async_copy(self.res.at[unit], target, self.pair_send.at[unit, 0])
        away = pltpu.make_async_remote_copy(
            src_ref=self.res.at[unit],
            dst_ref=target,
            send_sem=self.pair_send.at[unit, 0],
            recv_sem=self.pair_recv.at[unit, 1],
            device_id=(1 - self.section, self.me),
            device_id_type=MESH,
        )
        return here, away

    def owner(self, unit):
        if isinstance(unit, int):
            return self.section == 1 - unit // self.real, unit % self.real
        later = (unit >= self.real).astype(jnp.int32)
        return self.section == 1 - later, unit - later * self.real

    def finish(self, unit):
        mine, index = self.owner(unit)

        def send(place):
            pl.when(mine)(lambda: self.final(unit, place())[0].start())
            pl.when(jnp.logical_not(mine))(lambda: self.final(unit, place())[1].start())

        for wanted, place in self.places(index):
            if isinstance(wanted, bool):
                if wanted:
                    send(place)
            else:
                pl.when(wanted)(functools.partial(send, place))

    def finished(self, unit):
        mine, _ = self.owner(unit)
        here, away = self.final(unit, self.total[3].at[self.section])

        @pl.when(mine)
        def _():
            here.wait()
            away.wait_recv()

        pl.when(jnp.logical_not(mine))(away.wait_send)

    def step(self, number, unit, slot):
        order, levels = self.orders[slot], self.levels
        if number == 0:
            self.pair(unit).start()
        elif number == 1:
            self.pair(unit).wait()
            acc = self.acc(unit)
            total = acc[...].astype(jnp.float32) + self.res[unit].astype(jnp.float32)
            acc[...] = total.astype(jnp.bfloat16)
            self.halve(unit, order, 0).start()
        elif number <= levels:
            self.halved(unit, order, number - 2)
            self.halve(unit, order, number - 1).start()
        elif number == levels + 1:
            self.halved(unit, order, levels - 1)
            self.double(unit, order, levels - 1).start()
        elif number <= 2 * levels:
            level = 2 * levels - number
            self.double(unit, order, level + 1).wait()
            self.double(unit, order, level).start()
        elif number == 2 * levels + 1:
            self.double(unit, order, 0).wait()
            self.finish(unit)
        else:
            self.finished(unit)

    def locate(self, group):
        block, inside = group // self.block_groups, group % self.block_groups
        if not 0 <= block < 2:
            return None
        for start, burst, base, count in zip(self.starts, self.bursts, self.bases, self.counts):
            at = inside - start
            if 0 <= at < burst:
                return block * self.real + base + 3 * at, min(3, count - 3 * at)
        return None

    def found(self, group):
        later = (group >= self.block_groups).astype(jnp.int32)
        inside = group - later * self.block_groups
        valid, unit, left = jnp.bool_(False), jnp.int32(0), jnp.int32(0)
        for start, burst, base, count in zip(self.starts, self.bursts, self.bases, self.counts):
            at = inside - start
            here = jnp.logical_and(at >= 0, at < burst)
            valid = jnp.logical_or(valid, here)
            unit = jnp.where(here, base + 3 * at, unit)
            left = jnp.where(here, count - 3 * at, left)
        return jnp.logical_and(valid, group >= 0), unit + later * self.real, left

    def tick(self, time, ahead=None):
        for number in reversed(range(self.stages)):
            when = time - self.lag * number
            if when % self.pace:
                continue
            group = when // self.pace
            if ahead is None:
                place = self.locate(group)
                if place is not None:
                    for slot in range(place[1]):
                        self.step(number, place[0] + slot, slot)
                continue
            valid, unit, left = self.found(group + ahead)

            @pl.when(valid)
            def _():
                for slot in range(3):
                    step = functools.partial(self.step, number, unit + slot, slot)
                    if slot == 0:
                        step()
                    else:
                        pl.when(slot < left)(step)

    def idle(self, block, burst):
        goal = self.pace * (block * self.block_groups + self.starts[burst])
        if self.clock < goal:
            self.pump()

    def pump(self, count=1):
        for _ in range(count):
            self.tick(self.clock)
            self.clock += 1

    def reach(self, block, burst):
        goal = self.pace * (block * self.block_groups + self.starts[burst])
        assert self.clock <= goal
        self.pump(goal - self.clock)

    def burst(self, block, burst, tiles, put, extra=None):
        base = block * self.real + self.bases[burst]
        self.reach(block, burst)
        if tiles % 3 == 0 and extra is None:
            start, groups = self.clock, self.per_tile

            @pl.loop(0, tiles // 3)
            def _(turn):
                ahead = turn * groups
                time = start
                for part in range(3):
                    tile = 3 * turn + part
                    put(tile, base + tile * self.per_tile)
                    for _ in range((part + 1) * groups // 3 - part * groups // 3):
                        for _ in range(self.pace):
                            self.tick(time, ahead)
                            time += 1

            self.clock += self.pace * groups * (tiles // 3)
            return
        units = 0
        for tile in range(tiles):
            put(tile, base + tile * self.per_tile)
            before, units = units, units + self.per_tile
            self.pump(self.pace * (units // 3 - before // 3))
        if extra is not None:
            extra(base + units)
            before, units = units, units + 1
            self.pump(self.pace * (units // 3 - before // 3))
        if units % 3:
            self.pump(self.pace)

    def drain(self):
        last = self.pace * (self.block_groups + self.starts[2] + self.bursts[2] - 1)
        self.pump(last + self.lag * (self.stages - 1) + 1 - self.clock)


def sigmoid(v):
    return 0.5 + 0.5 * jnp.tanh(0.5 * v)


def silu_parts(v):
    sigma = sigmoid(v)
    return v * sigma, sigma * (1.0 + v * (1.0 - sigma))


def folded(x):
    return jnp.sum(x.reshape(x.shape[0] // 8, 8, x.shape[1]), axis=0)


class Exchange:
    def __init__(self, size, send_sem, recv_sem, edge_send, edge_recv):
        self.size = size
        self.section, self.me = lax.axis_index("section"), lax.axis_index("dp")
        self.send_sem, self.recv_sem = send_sem, recv_sem
        self.edge_send, self.edge_recv = edge_send, edge_recv

    def greet(self):
        barrier = pltpu.get_barrier_semaphore()
        for step in range(1, self.size):
            peer = (self.section, lax.rem(self.me + step, self.size))
            pl.semaphore_signal(barrier, inc=1, device_id=peer, device_id_type=MESH)
        other = (1 - self.section, self.me)
        pl.semaphore_signal(barrier, inc=1, device_id=other, device_id_type=MESH)
        pl.semaphore_wait(barrier, self.size)

    def copies(self, number, slots):
        return [
            pltpu.make_async_remote_copy(
                src_ref=slots.at[0],
                dst_ref=slots.at[step],
                send_sem=self.send_sem.at[number, step],
                recv_sem=self.recv_sem.at[number, step],
                device_id=(self.section, lax.rem(self.me + step, self.size)),
                device_id_type=MESH,
            )
            for step in range(1, self.size)
        ]

    def edges(self, number, first, last, landing):
        made = []
        for way, (ref, step) in enumerate(((first, self.size - 1), (last, 1))):
            made.append(
                pltpu.make_async_remote_copy(
                    src_ref=ref,
                    dst_ref=landing.at[1 - way],
                    send_sem=self.edge_send.at[number, way],
                    recv_sem=self.edge_recv.at[number, 1 - way],
                    device_id=(self.section, lax.rem(self.me + step, self.size)),
                    device_id_type=MESH,
                )
            )
        return made

    def start_edges(self, number, first, last, landing):
        up, down = self.edges(number, first, last, landing)
        pl.when(self.me > 0)(up.start)
        pl.when(self.me < self.size - 1)(down.start)

    def wait_edges(self, number, first, last, landing):
        up, down = self.edges(number, first, last, landing)
        pl.when(self.me > 0)(up.wait_send)
        pl.when(self.me > 0)(down.wait_recv)
        pl.when(self.me < self.size - 1)(down.wait_send)
        pl.when(self.me < self.size - 1)(up.wait_recv)


def forward_kernel(
    size,
    u_hbm,
    bits_hbm,
    cot_hbm,
    wr_hbm,
    ws_hbm,
    we_hbm,
    ig_ref,
    ib_ref,
    og_ref,
    ob_ref,
    hwt_ref,
    hb_ref,
    info_ref,
    heads_ref,
    hwg_ref,
    hbg_ref,
    igs,
    ibs,
    ogs,
    obs,
    rs_ref,
    rc_ref,
    info_out,
    merged_hbm,
    u1_hbm,
    zc_hbm,
    za_hbm,
    zb_hbm,
    r1_hbm,
    wr_all,
    ws_all,
    we_all,
    wr,
    ws,
    we,
    u0,
    u1,
    a_ref,
    b_ref,
    e_ref,
    cat,
    r2,
    za,
    zb,
    zc,
    merged,
    bits,
    cot,
    edge,
    halo,
    live_halo,
    msg,
    msg_c,
    first_msg,
    stat,
    stat_c,
    send_sem,
    recv_sem,
    edge_send,
    edge_recv,
    w_load,
    w_send,
    w_recv,
    w_out,
    in_sem,
    bit_sem,
    out_sem,
):
    link = Exchange(size, send_sem, recv_sem, edge_send, edge_recv)
    section, me = link.section, link.me
    pixels, channels = u0.shape
    inner = a_ref.shape[1]
    rows, width = bits_hbm.shape[1], bits_hbm.shape[2]
    f32, bf16 = jnp.float32, jnp.bfloat16

    load_u = pltpu.make_async_copy(u_hbm, u0, in_sem.at[0])
    load_cot = pltpu.make_async_copy(cot_hbm.at[section], cot, in_sem.at[1])

    def load_bits(chunk):
        return pltpu.make_async_copy(
            bits_hbm.at[section, chunk], bits.at[chunk % 2], bit_sem.at[chunk % 2]
        )

    load_u.start()
    load_cot.start()
    load_bits(0).start()
    load_bits(1).start()

    weights = ((wr_hbm, wr, wr_all), (ws_hbm, ws, ws_all), (we_hbm, we, we_all))

    def local_load(kind):
        source, target, _ = weights[kind]
        return pltpu.make_async_copy(source, target.at[section], w_load.at[kind])

    def pushed(kind):
        source, target, _ = weights[kind]
        return pltpu.make_async_remote_copy(
            src_ref=source,
            dst_ref=target.at[section],
            send_sem=w_send.at[kind],
            recv_sem=w_recv.at[kind],
            device_id=(1 - section, me),
            device_id_type=MESH,
        )

    vectors = ((ig_ref, igs), (ib_ref, ibs), (og_ref, ogs), (ob_ref, obs))

    def pushed_vector(kind):
        source, target = vectors[kind]
        return pltpu.make_async_remote_copy(
            src_ref=source,
            dst_ref=target.at[section],
            send_sem=w_send.at[3 + kind],
            recv_sem=w_recv.at[3 + kind],
            device_id=(1 - section, me),
            device_id_type=MESH,
        )

    def save_weight(kind, layer):
        _, target, saved = weights[kind]
        return pltpu.make_async_copy(target.at[layer], saved.at[layer], w_out.at[kind, layer])

    for kind in range(3):
        local_load(kind).start()
    link.greet()
    for kind in range(4):
        pushed_vector(kind).start()
    for kind in range(3):
        pushed(kind).start()
    for source, target in vectors:
        target[section] = source[...]

    def need_weight(kind, layer):
        pl.when(section == layer)(local_load(kind).wait)
        pl.when(section != layer)(pushed(kind).wait_recv)
        save_weight(kind, layer).start()

    own = pl.ds(width, pixels)
    live_edges = (info_ref.at[pl.ds(0, width)], info_ref.at[pl.ds(pixels - width, width)])

    def live_at(start, count):
        return info_ref[pl.ds(start, count), 0:1]

    def drop_chunk(chunk):
        load_bits(chunk).wait()
        start = pl.multiple_of(chunk * width, 16)
        target = cot[chunk].astype(f32) * live_at(start, width)
        task = lax.broadcasted_iota(jnp.int32, target.shape, 1) // HEAD_OUT
        parts = [jnp.where(task == k, target, 0.0).astype(bf16) for k in range(TASKS)]

        @pl.loop(0, channels // TILE)
        def _(tile):
            cols = pl.ds(pl.multiple_of(tile * TILE, TILE), TILE)
            table = hwt_ref[:, cols]
            signed = magnitude = weighted = None
            for part in parts:
                value = jnp.dot(part, table, preferred_element_type=f32)
                square = value * value
                whole = square + SOFT * SOFT
                inverse = lax.rsqrt(whole)
                if signed is None:
                    signed, magnitude, weighted = value, whole * inverse, square * inverse
                else:
                    signed = signed + value
                    magnitude = magnitude + whole * inverse
                    weighted = weighted + square * inverse
            level = bits[chunk % 2, :, cols].astype(f32)
            reach = 0.25 / SHARP
            inside = reach * (signed / magnitude) + (
                reach * (1.0 - 1.0 / LEVELS) - (2.0 * reach / LEVELS) * level
            )
            value = 0.5 * signed + (0.5 * jnp.tanh(inside)) * weighted
            merged[pl.ds(start, width), cols] = value.astype(bf16)

        if chunk + 2 < rows:
            load_bits(chunk + 2).start()

    live_all = info_ref[:, 0:1]
    count_here = jnp.sum(live_all, axis=0, keepdims=True)
    share = 1.0 / count_here

    def column_stats(values):
        mean = jnp.sum(values * live_all, axis=0, keepdims=True) * share
        apart = values - mean
        return mean, jnp.sum(live_all * apart * apart, axis=0, keepdims=True)

    def counts(step):
        return first_msg[step, 2:3, 0:1]

    def combine(slots):
        number = counts(0)
        mean = slots[0, 0:1] * counts(0)
        spread = slots[0, 1:2]
        for step in range(1, size):
            number = number + counts(step)
            mean = mean + slots[step, 0:1] * counts(step)
            spread = spread + slots[step, 1:2]
        mean = mean / number
        for step in range(size):
            apart = slots[step, 0:1] - mean
            spread = spread + counts(step) * apart * apart
        return mean, lax.rsqrt(spread / number + EPS), number

    load_u.wait()
    load_cot.wait()
    drop_chunk(0)
    first_msg[0, 2:3] = jnp.broadcast_to(count_here, (1, inner))
    first_msg[0, 3:4] = jnp.zeros((1, inner), f32)
    zc_out = za_out = zb_out = r1_out = None
    u1_out = pltpu.make_async_copy(u1, u1_hbm, out_sem.at[0])
    for layer in range(2):
        x_ref = (u0, u1)[layer]
        need_weight(0, layer)
        slots = first_msg if layer == 0 else msg.at[0]

        @pl.loop(0, inner // 256)
        def _(tile):
            cols = pl.ds(pl.multiple_of(tile * 256, 256), 256)
            values = jnp.dot(x_ref[...], wr[layer, :, cols], preferred_element_type=f32)
            a_ref[:, cols] = values
            mean, spread = column_stats(values)
            slots[0, 0:1, cols] = mean
            slots[0, 1:2, cols] = spread

        if layer == 1:
            for copy in (za_out, zb_out, r1_out, zc_out):
                copy.wait()
            u1_out.start()
        sends = link.copies(3 * layer, slots)
        for copy in sends:
            copy.start()
        centre = slots[0, 0:1]
        edge[0] = (a_ref[0:width] - centre).astype(bf16)
        edge[1] = (a_ref[pixels - width : pixels] - centre).astype(bf16)
        a_edges = (edge.at[0], edge.at[1])
        a_halo = halo.at[2 * layer]
        link.start_edges(2 * layer, *a_edges, a_halo)
        if layer == 0:
            link.start_edges(4, *live_edges, live_halo)
            for kind in range(4):
                pushed_vector(kind).wait()
        drop_chunk(1 + 3 * layer)
        for copy in sends:
            copy.wait()
        mean, inverse, number = combine(slots)
        stat[layer, 0:1], stat[layer, 1:2] = mean, inverse
        rs_ref[layer, 0:1] = inverse
        rs_ref[layer, 2:3] = jnp.broadcast_to(number, (1, inner))

        def first_act(row, values, inside):
            normed = (values - stat[layer, 0:1]) * stat[layer, 1:2]
            affine = normed * igs[layer, 0:1] + ibs[layer, 0:1]
            act = affine * sigmoid(affine)
            if inside is not None:
                act = jnp.where(inside, act, 0.0)
            here = pl.ds(pl.multiple_of(row * width, 16), width)
            masks = info_ref[0:width]
            cat[here, 0:inner] = (pltpu.roll(act, 1, 0) * masks[:, 1:2]).astype(bf16)
            cat[here, inner : 2 * inner] = act.astype(bf16)
            cat[here, 2 * inner : 3 * inner] = (
                pltpu.roll(act, width - 1, 0) * masks[:, 2:3]
            ).astype(bf16)
            return normed

        @pl.loop(0, rows)
        def _(row):
            here = pl.ds(pl.multiple_of(row * width, 16), width)
            za[here] = first_act(row + 1, a_ref[here], None).astype(bf16)

        link.wait_edges(2 * layer, *a_edges, a_halo)
        first_act(0, a_halo[0].astype(f32) + slots[1, 0:1], me > 0)
        first_act(rows + 1, a_halo[1].astype(f32) + slots[size - 1, 0:1], me < size - 1)

        za_out = pltpu.make_async_copy(za, za_hbm.at[layer], out_sem.at[1])
        r1_out = pltpu.make_async_copy(
            cat.at[:, pl.ds(inner, inner)], r1_hbm.at[layer], out_sem.at[2]
        )
        za_out.start()
        r1_out.start()
        need_weight(1, layer)
        slots = msg.at[1 + 2 * layer]

        @pl.loop(0, inner // 256)
        def _(tile):
            cols = pl.ds(pl.multiple_of(tile * 256, 256), 256)
            values = None
            for tap in range(3):
                table = ws[layer, 3 * tap : 3 * tap + 3, :, cols].reshape(3 * inner, 256)
                value = jnp.dot(
                    cat[tap * width : tap * width + pixels], table, preferred_element_type=f32
                )
                values = value if values is None else values + value
            b_ref[:, cols] = values
            mean, spread = column_stats(values)
            slots[0, 0:1, cols] = mean
            slots[0, 1:2, cols] = spread

        sends = link.copies(3 * layer + 1, slots)
        for copy in sends:
            copy.start()
        drop_chunk(2 + 3 * layer)
        for copy in sends:
            copy.wait()
        mean, inverse, _ = combine(slots)
        stat[layer, 2:3], stat[layer, 3:4] = mean, inverse
        rs_ref[layer, 1:2] = inverse

        @pl.loop(0, rows)
        def _(row):
            here = pl.ds(pl.multiple_of(row * width, 16), width)
            normed = (b_ref[here] - stat[layer, 2:3]) * stat[layer, 3:4]
            zb[pl.ds(pl.multiple_of((row + 1) * width, 16), width)] = normed.astype(bf16)
            affine = normed * igs[layer, 1:2] + ibs[layer, 1:2]
            r2[here] = (affine * sigmoid(affine)).astype(bf16)

        b_edges = (zb.at[pl.ds(width, width)], zb.at[pl.ds(pixels, width)])
        b_halo = halo.at[2 * layer + 1]
        link.start_edges(2 * layer + 1, *b_edges, b_halo)
        need_weight(2, layer)
        slots = msg_c.at[layer]

        @pl.loop(0, channels // 256)
        def _(tile):
            cols = pl.ds(pl.multiple_of(tile * 256, 256), 256)
            values = jnp.dot(r2[...], we[layer, :, cols], preferred_element_type=f32)
            e_ref[:, cols] = values
            mean, spread = column_stats(values)
            slots[0, 0:1, cols] = mean
            slots[0, 1:2, cols] = spread

        sends = link.copies(3 * layer + 2, slots)
        for copy in sends:
            copy.start()
        drop_chunk(3 + 3 * layer)
        if layer == 0:
            link.wait_edges(4, *live_edges, live_halo)
            info_out[own] = info_ref[...]
            info_out[0:width] = live_halo[0]
            info_out[pixels + width : pixels + 2 * width] = live_halo[1]
        if layer == 1:
            drop_chunk(7)
            pltpu.make_async_copy(merged, merged_hbm, out_sem.at[4]).start()
        link.wait_edges(2 * layer + 1, *b_edges, b_halo)
        for side, row in ((0, 0), (1, rows + 1)):
            zb[row * width : (row + 1) * width] = b_halo[side]
        zb_out = pltpu.make_async_copy(zb, zb_hbm.at[layer], out_sem.at[3])
        zb_out.start()
        for copy in sends:
            copy.wait()
        mean, inverse, _ = combine(slots)
        stat_c[0:1], stat_c[1:2] = mean, inverse
        rc_ref[layer] = inverse
        out_ref = (u1, u0)[layer]

        @pl.loop(0, rows * (channels // TILE))
        def _(chunk):
            row, tile = chunk // (channels // TILE), chunk % (channels // TILE)
            here = pl.ds(pl.multiple_of(row * width, 16), width)
            cols = pl.ds(pl.multiple_of(tile * TILE, TILE), TILE)
            normed = (e_ref[here, cols] - stat_c[0:1, cols]) * stat_c[1:2, cols]
            zc[here, cols] = normed.astype(bf16)
            total = normed * ogs[layer, :, cols] + obs[layer, :, cols] + x_ref[here, cols].astype(f32)
            out_ref[here, cols] = (total * sigmoid(total)).astype(bf16)

        zc_out = pltpu.make_async_copy(zc, zc_hbm.at[layer], out_sem.at[5])
        zc_out.start()

    heads_ref[...] = (
        lax.dot_general(u0[...], hwt_ref[...], BESIDE, preferred_element_type=f32) + hb_ref[...]
    )
    target = cot[...].astype(f32).reshape(pixels, -1) * live_all
    hbg_ref[...] = jnp.sum(target, axis=0, keepdims=True)
    target = target.astype(bf16)

    @pl.loop(0, channels // 256)
    def _(tile):
        cols = pl.ds(pl.multiple_of(tile * 256, 256), 256)
        hwg_ref[:, cols] = lax.dot_general(target, u0[:, cols], ACROSS, preferred_element_type=f32)

    for copy in (za_out, zb_out, r1_out, zc_out, u1_out):
        copy.wait()
    pltpu.make_async_copy(merged, merged_hbm, out_sem.at[4]).wait()
    for kind in range(3):
        pushed(kind).wait_send()
        for layer in range(2):
            save_weight(kind, layer).wait()


def forward(u, bits, cot, wr, ws, we, ig, ib, og, ob, hwt, hb, info):
    size = lax.axis_size("dp")
    pixels, channels = u.shape
    inner = wr.shape[1]
    _, rows, width, head_cols = cot.shape
    f32, bf16 = jnp.float32, jnp.bfloat16
    padded = pixels + 2 * width
    anywhere = pl.BlockSpec(memory_space=pl.ANY)
    vmem = pl.BlockSpec(memory_space=pltpu.VMEM)

    def out(kind, *shape):
        return jax.ShapeDtypeStruct(shape, kind)

    return pl.pallas_call(
        functools.partial(forward_kernel, size),
        out_shape=[
            out(f32, pixels, head_cols),
            out(f32, head_cols, channels),
            out(f32, 1, head_cols),
            out(f32, 2, 2, inner),
            out(f32, 2, 2, inner),
            out(f32, 2, 1, channels),
            out(f32, 2, 1, channels),
            out(f32, 2, 8, inner),
            out(f32, 2, 1, channels),
            out(f32, padded, 128),
            out(bf16, pixels, channels),
            out(bf16, pixels, channels),
            out(bf16, 2, pixels, channels),
            out(bf16, 2, pixels, inner),
            out(bf16, 2, padded, inner),
            out(bf16, 2, padded, inner),
            out(bf16, 2, channels, inner),
            out(bf16, 2, 9, inner, inner),
            out(bf16, 2, inner, channels),
        ],
        in_specs=[anywhere] * 6 + [vmem] * 7,
        out_specs=[vmem] * 10 + [anywhere] * 9,
        scratch_shapes=[
            pltpu.VMEM((2, channels, inner), bf16),
            pltpu.VMEM((2, 9, inner, inner), bf16),
            pltpu.VMEM((2, inner, channels), bf16),
            pltpu.VMEM((pixels, channels), bf16),
            pltpu.VMEM((pixels, channels), bf16),
            pltpu.VMEM((pixels, inner), f32),
            pltpu.VMEM((pixels, inner), f32),
            pltpu.VMEM((pixels, channels), f32),
            pltpu.VMEM((padded, 3 * inner), bf16),
            pltpu.VMEM((pixels, inner), bf16),
            pltpu.VMEM((pixels, inner), bf16),
            pltpu.VMEM((padded, inner), bf16),
            pltpu.VMEM((pixels, channels), bf16),
            pltpu.VMEM((pixels, channels), bf16),
            pltpu.VMEM((2, width, channels), jnp.int32),
            pltpu.VMEM((rows, width, head_cols), bf16),
            pltpu.VMEM((2, width, inner), bf16),
            pltpu.VMEM((4, 2, width, inner), bf16),
            pltpu.VMEM((2, width, 128), f32),
            pltpu.VMEM((4, size, 2, inner), f32),
            pltpu.VMEM((2, size, 2, channels), f32),
            pltpu.VMEM((size, 4, inner), f32),
            pltpu.VMEM((2, 8, inner), f32),
            pltpu.VMEM((2, channels), f32),
            pltpu.SemaphoreType.DMA((6, size)),
            pltpu.SemaphoreType.DMA((6, size)),
            pltpu.SemaphoreType.DMA((5, 2)),
            pltpu.SemaphoreType.DMA((5, 2)),
            pltpu.SemaphoreType.DMA((3,)),
            pltpu.SemaphoreType.DMA((7,)),
            pltpu.SemaphoreType.DMA((7,)),
            pltpu.SemaphoreType.DMA((3, 2)),
            pltpu.SemaphoreType.DMA((2,)),
            pltpu.SemaphoreType.DMA((2,)),
            pltpu.SemaphoreType.DMA((6,)),
        ],
        compiler_params=pltpu.CompilerParams(
            collective_id=1, has_side_effects=True, vmem_limit_bytes=LIMIT
        ),
    )(u, bits, cot, wr, ws, we, ig, ib, og, ob, hwt, hb, info)


def backward_kernel(
    size,
    reducer,
    u0_hbm,
    u1_hbm,
    merged_hbm,
    zc_hbm,
    za_hbm,
    zb_hbm,
    r1_hbm,
    wr_all,
    ws_all,
    we_all,
    igs,
    ibs,
    ogs,
    obs,
    rs_ref,
    rc_ref,
    hwg_ref,
    hbg_ref,
    info_ref,
    grad_hbm,
    expand_hbm,
    spatial_hbm,
    reduce_hbm,
    small_hbm,
    wr,
    ws,
    we,
    u_ref,
    d_ref,
    zc,
    za,
    zb,
    r1,
    r2,
    wide,
    dz_ref,
    da,
    small,
    edge,
    halo,
    msg,
    msg_c,
    part_sum,
    sums,
    sums_c,
    send_sem,
    recv_sem,
    edge_send,
    edge_recv,
    in_sem,
    out_sem,
    *scratch,
):
    reducer.bind((expand_hbm, spatial_hbm, reduce_hbm, small_hbm), scratch)
    link = Exchange(size, send_sem, recv_sem, edge_send, edge_recv)
    section, me = link.section, link.me
    pixels, channels = d_ref.shape
    inner = da.shape[1]
    width = halo.shape[2]
    rows = pixels // width
    across = channels // TILE
    f32, bf16 = jnp.float32, jnp.bfloat16
    own = pl.ds(width, pixels)
    de, cat = wide.at[pl.ds(0, pixels)], wide.at[:, pl.ds(0, 3 * inner)]

    def loads(layer):
        return {
            "zc": pltpu.make_async_copy(zc_hbm.at[layer], zc, in_sem.at[0]),
            "za": pltpu.make_async_copy(za_hbm.at[layer], za, in_sem.at[1]),
            "zb": pltpu.make_async_copy(zb_hbm.at[layer], zb, in_sem.at[2]),
            "r1": pltpu.make_async_copy(r1_hbm.at[layer], r1, in_sem.at[3]),
            "wr": pltpu.make_async_copy(wr_all.at[layer], wr, in_sem.at[4]),
            "ws": pltpu.make_async_copy(ws_all.at[layer], ws, in_sem.at[5]),
            "we": pltpu.make_async_copy(we_all.at[layer], we, in_sem.at[6]),
            "u": pltpu.make_async_copy((u0_hbm, u1_hbm)[layer], u_ref.at[layer], in_sem.at[7 + layer]),
        }

    load_d = pltpu.make_async_copy(merged_hbm, d_ref, in_sem.at[9])
    first, second = loads(1), loads(0)
    load_d.start()
    for name in ("u", "zc", "we", "zb", "ws", "za", "r1", "wr"):
        first[name].start()
    second["u"].start()
    link.greet()
    live_all = info_ref[own, 0:1]

    def put_tile(unit, make):
        @pl.loop(0, 2)
        def _(side):
            cols = pl.ds(pl.multiple_of(side * 256, 256), 256)
            value = make(side).astype(bf16)
            inside = (slice(None),) * len(reducer.shape)
            for part in range(reducer.per_tile):
                lines = value[part * reducer.lines : (part + 1) * reducer.lines]
                at = (reducer.slot(unit + part),) + inside + (cols,)
                reducer.ring[at] = lines.reshape((2,) + reducer.shape[:-1] + (256,))

    def column_sums(values):
        return jnp.sum(values, axis=0, keepdims=True)

    def total_of(slots):
        found = slots[0]
        for step in range(1, size):
            found = found + slots[step]
        return found

    def expand_tiles(layer):
        def put(tile, unit):
            def make(side):
                cols = pl.ds(pl.multiple_of(tile * TILE + side * 256, 256), 256)
                return lax.dot_general(r2[...], de[:, cols], ACROSS, preferred_element_type=f32)

            put_tile(unit, make)

        reducer.burst(1 - layer, 0, across, put)

    def spatial_tiles(layer):
        def put(tap, unit):
            shift, side_step = tap // 3, tap % 3

            def make(side):
                at = pl.ds(pl.multiple_of(shift * width, 16), pixels)
                cols = pl.ds(pl.multiple_of(side_step * inner + side * 256, 256), 256)
                return lax.dot_general(r1[at], cat[own, cols], ACROSS, preferred_element_type=f32)

            put_tile(unit, make)

        reducer.burst(1 - layer, 1, 9, put)

    def reduce_tiles(layer):
        def put(tile, unit):
            def make(side):
                cols = pl.ds(pl.multiple_of(side * 256, 256), 256)
                lines = pl.ds(pl.multiple_of(tile * TILE, TILE), TILE)
                return lax.dot_general(
                    u_ref[layer, :, lines], da[:, cols], ACROSS, preferred_element_type=f32
                )

            put_tile(unit, make)

        reducer.burst(1 - layer, 2, across, put, functools.partial(small_unit, layer))

    def small_unit(layer, unit):
        half = channels // 2
        head_cols = hwg_ref.shape[0]
        small[...] = jnp.zeros_like(small)
        for k in range(2):
            at = layer * half + k * TILE
            small[k * head_cols : (k + 1) * head_cols] = hwg_ref[:, at : at + TILE]
        row = 2 * head_cols
        small[row : row + 1, 0:head_cols] = hbg_ref[...]
        only = (me == 0).astype(f32)
        small[row + 8 : row + 9] = sums[0, 1:2] * only
        small[row + 9 : row + 10] = sums[1, 1:2] * only
        small[row + 10 : row + 11] = sums[0, 0:1] * only
        small[row + 11 : row + 12] = sums[1, 0:1] * only
        for k in range(across):
            cols = slice(k * TILE, (k + 1) * TILE)
            small[row + 12 + k : row + 13 + k] = sums_c[1:2, cols] * only
            small[row + 12 + across + k : row + 13 + across + k] = sums_c[0:1, cols] * only
        slot = reducer.slot(unit)
        blank = jnp.zeros(reducer.shape, bf16)
        reducer.ring[slot, 0] = small[0 : reducer.half].astype(bf16).reshape(reducer.shape)
        reducer.ring[slot, 1] = blank

    load_d.wait()
    for layer in (1, 0):
        now = (second, first)[layer]
        now["u"].wait()
        now["zc"].wait()
        part_sum[...] = jnp.zeros_like(part_sum)

        def dt_chunk(chunk):
            row, tile = chunk // across, chunk % across
            here = pl.ds(pl.multiple_of(row * width, 16), width)
            cols = pl.ds(pl.multiple_of(tile * TILE, TILE), TILE)
            normed = zc[here, cols].astype(f32)
            total = (
                normed * ogs[layer, :, cols]
                + obs[layer, :, cols]
                + u_ref[layer, here, cols].astype(f32)
            )
            _, slope = silu_parts(total)
            dt = d_ref[here, cols].astype(f32) * slope
            d_ref[here, cols] = dt.astype(bf16)
            part_sum[0, :, cols] += folded(dt)
            part_sum[1, :, cols] += folded(dt * normed)

        for part in range(2):
            pl.loop(part * (rows * across // 2), (part + 1) * (rows * across // 2))(dt_chunk)
            if layer == 0:
                reducer.idle(0, 2)
        slots = msg_c.at[1 - layer]
        slots[0, 0:1] = column_sums(part_sum[0])
        slots[0, 1:2] = column_sums(part_sum[1])
        sends = link.copies(3 * layer, slots)
        for copy in sends:
            copy.start()
        if layer == 0:
            reduce_tiles(1)
        for copy in sends:
            copy.wait()
        sums_c[...] = total_of(slots)
        number = rs_ref[layer, 2:3, 0:1]
        share = 1.0 / number

        def de_chunk(chunk):
            row, tile = chunk // across, chunk % across
            here = pl.ds(pl.multiple_of(row * width, 16), width)
            cols = pl.ds(pl.multiple_of(tile * TILE, TILE), TILE)
            live = info_ref[pl.ds(pl.multiple_of((row + 1) * width, 16), width), 0:1]
            normed = zc[here, cols].astype(f32)
            away = (sums_c[0:1, cols] + normed * sums_c[1:2, cols]) * share
            scale = rc_ref[layer, :, cols] * ogs[layer, :, cols]
            value = scale * (d_ref[here, cols].astype(f32) - live * away)
            de[here, cols] = value.astype(bf16)

        for part in range(4):
            pl.loop(part * (rows * across // 4), (part + 1) * (rows * across // 4))(de_chunk)
            if layer == 0:
                reducer.idle(1, 0)
        now["we"].wait()
        now["zb"].wait()
        slots = msg.at[2 * layer]

        for tile in range(inner // 256):
            if tile > 0 and layer == 0:
                reducer.idle(1, 0)
            cols = pl.ds(tile * 256, 256)
            dr2 = lax.dot_general(de[...], we[cols], BESIDE, preferred_element_type=f32)
            normed = zb[own, cols].astype(f32)
            act, slope = silu_parts(normed * igs[layer, 1:2, cols] + ibs[layer, 1:2, cols])
            r2[:, cols] = act.astype(bf16)
            dz = dr2 * slope
            dz_ref[:, cols] = dz
            slots[0, 0:1, cols] = column_sums(dz)
            slots[0, 1:2, cols] = column_sums(dz * normed)

        sends = link.copies(3 * layer + 1, slots)
        for copy in sends:
            copy.start()
        edge[0] = dz_ref[0:width].astype(bf16)
        edge[1] = dz_ref[pixels - width : pixels].astype(bf16)
        edges = (edge.at[0], edge.at[1])
        landing = halo.at[layer]
        link.start_edges(layer, *edges, landing)
        if layer == 1:
            second["zc"].start()
            second["we"].start()
        expand_tiles(layer)
        for copy in sends:
            copy.wait()
        sums[1] = total_of(slots)

        def db_row(row, dz, inside):
            here = pl.ds(pl.multiple_of(row * width, 16), width)
            live = info_ref[here, 0:1]
            normed = zb[here].astype(f32)
            away = (sums[1, 0:1] + normed * sums[1, 1:2]) * share
            value = (rs_ref[layer, 1:2] * igs[layer, 1:2]) * (dz - live * away)
            if inside is not None:
                value = jnp.where(inside, value, 0.0)
            masks = info_ref[pl.ds(width, width), :]
            cat[here, 0:inner] = (pltpu.roll(value, width - 1, 0) * masks[:, 2:3]).astype(bf16)
            cat[here, inner : 2 * inner] = value.astype(bf16)
            cat[here, 2 * inner : 3 * inner] = (
                pltpu.roll(value, 1, 0) * masks[:, 1:2]
            ).astype(bf16)

        def own_db(row):
            db_row(row + 1, dz_ref[pl.ds(pl.multiple_of(row * width, 16), width)], None)

        pl.loop(0, rows // 2)(own_db)
        reducer.idle(1 - layer, 1)
        pl.loop(rows // 2, rows)(own_db)
        reducer.idle(1 - layer, 1)

        link.wait_edges(layer, *edges, landing)
        db_row(0, landing[0].astype(f32), me > 0)
        db_row(rows + 1, landing[1].astype(f32), me < size - 1)
        reducer.idle(1 - layer, 1)

        if layer == 1:
            second["zb"].start()
        now["ws"].wait()
        now["za"].wait()
        slots = msg.at[2 * layer + 1]

        for tile in range(inner // 256):
            if tile > 0:
                reducer.idle(1 - layer, 1)
            cols = pl.ds(tile * 256, 256)
            dr1 = None
            for tap in range(9):
                start = (2 - tap // 3) * width
                block = cat[start : start + pixels, (tap % 3) * inner : (tap % 3 + 1) * inner]
                value = lax.dot_general(block, ws[tap, cols], BESIDE, preferred_element_type=f32)
                dr1 = value if dr1 is None else dr1 + value
            normed = za[:, cols].astype(f32)
            _, slope = silu_parts(normed * igs[layer, 0:1, cols] + ibs[layer, 0:1, cols])
            dz = dr1 * slope
            dz_ref[:, cols] = dz
            slots[0, 0:1, cols] = column_sums(dz)
            slots[0, 1:2, cols] = column_sums(dz * normed)

        sends = link.copies(3 * layer + 2, slots)
        for copy in sends:
            copy.start()
        if layer == 1:
            second["ws"].start()
        now["r1"].wait()
        spatial_tiles(layer)
        for copy in sends:
            copy.wait()
        sums[0] = total_of(slots)
        if layer == 1:
            second["r1"].start()

        @pl.loop(0, rows)
        def _(row):
            here = pl.ds(pl.multiple_of(row * width, 16), width)
            live = info_ref[pl.ds(pl.multiple_of((row + 1) * width, 16), width), 0:1]
            away = (sums[0, 0:1] + za[here].astype(f32) * sums[0, 1:2]) * share
            value = (rs_ref[layer, 0:1] * igs[layer, 0:1]) * (dz_ref[here] - live * away)
            da[here] = value.astype(bf16)

        if layer == 1:
            second["za"].start()
        now["wr"].wait()
        reducer.idle(1 - layer, 2)

        def du_tile(tile):
            cols = pl.ds(pl.multiple_of(tile * 256, 256), 256)
            du = lax.dot_general(da[...], wr[cols], BESIDE, preferred_element_type=f32)
            d_ref[:, cols] = (du + d_ref[:, cols].astype(f32)).astype(bf16)

        if layer == 0:
            reduce_tiles(0)
        for part in range(4):
            pl.loop(part * (channels // 1024), (part + 1) * (channels // 1024))(du_tile)
            if part < 3:
                if layer == 0:
                    reducer.pump(2)
                else:
                    reducer.idle(1 - layer, 2)
        if layer == 1:
            second["wr"].start()
    out = pltpu.make_async_copy(d_ref, grad_hbm, out_sem)
    out.start()
    reducer.drain()
    out.wait()


def backward(u0, u1, merged, zc, za, zb, r1, wr, ws, we, igs, ibs, ogs, obs, rs, rc, hwg, hbg, info):
    size = lax.axis_size("dp")
    pixels, channels = u0.shape
    inner = za.shape[2]
    padded = zb.shape[1]
    width = (padded - pixels) // 2
    f32, bf16 = jnp.float32, jnp.bfloat16
    anywhere = pl.BlockSpec(memory_space=pl.ANY)
    vmem = pl.BlockSpec(memory_space=pltpu.VMEM)
    taps = ws.shape[1]
    reducer = Reducer(size, channels // TILE, taps)
    totals = reducer.totals(channels // TILE, taps)
    return pl.pallas_call(
        functools.partial(backward_kernel, size, reducer),
        out_shape=[
            jax.ShapeDtypeStruct((pixels, channels), bf16),
        ]
        + [jax.ShapeDtypeStruct(shape, bf16) for shape in totals],
        in_specs=[anywhere] * 10 + [vmem] * 9,
        out_specs=[anywhere] * 5,
        scratch_shapes=[
            pltpu.VMEM((channels, inner), bf16),
            pltpu.VMEM((9, inner, inner), bf16),
            pltpu.VMEM((inner, channels), bf16),
            pltpu.VMEM((2, pixels, channels), bf16),
            pltpu.VMEM((pixels, channels), bf16),
            pltpu.VMEM((pixels, channels), bf16),
            pltpu.VMEM((pixels, inner), bf16),
            pltpu.VMEM((padded, inner), bf16),
            pltpu.VMEM((padded, inner), bf16),
            pltpu.VMEM((pixels, inner), bf16),
            pltpu.VMEM((padded, channels), bf16),
            pltpu.VMEM((pixels, inner), f32),
            pltpu.VMEM((pixels, inner), bf16),
            pltpu.VMEM((reducer.half, TILE), f32),
            pltpu.VMEM((2, width, inner), bf16),
            pltpu.VMEM((2, 2, width, inner), bf16),
            pltpu.VMEM((4, size, 2, inner), f32),
            pltpu.VMEM((2, size, 2, channels), f32),
            pltpu.VMEM((2, 8, channels), f32),
            pltpu.VMEM((2, 2, inner), f32),
            pltpu.VMEM((2, channels), f32),
            pltpu.SemaphoreType.DMA((6, size)),
            pltpu.SemaphoreType.DMA((6, size)),
            pltpu.SemaphoreType.DMA((2, 2)),
            pltpu.SemaphoreType.DMA((2, 2)),
            pltpu.SemaphoreType.DMA((10,)),
            pltpu.SemaphoreType.DMA,
        ]
        + reducer.scratch(),
        compiler_params=pltpu.CompilerParams(
            collective_id=2, has_side_effects=True, vmem_limit_bytes=63 * 2**20
        ),
    )(u0, u1, merged, zc, za, zb, r1, wr, ws, we, igs, ibs, ogs, obs, rs, rc, hwg, hbg, info)


def pixel_info(pixel_mask, starts):
    width = pixel_mask.shape[1]
    columns = jnp.arange(width, dtype=jnp.int32)
    crop = jnp.sum((columns[:, None] >= starts[None, :]).astype(jnp.int32), axis=1)
    outside = jnp.full((1,), -1, jnp.int32)
    left = jnp.concatenate([outside, crop[:-1]]) == crop
    right = jnp.concatenate([crop[1:], outside]) == crop
    lane = jnp.arange(128, dtype=jnp.int32)
    first = jnp.where(lane == 0, pixel_mask[:, :, None], 0)
    links = jnp.where(lane == 1, left[:, None].astype(jnp.int32), 0)
    links = links + jnp.where(lane == 2, right[:, None].astype(jnp.int32), 0)
    return (first + links[None]).astype(jnp.float32).reshape(-1, 128)


def pick(array, index):
    return lax.dynamic_index_in_dim(array, index, 0, keepdims=False)


def local(
    canvases,
    crop_starts,
    pixel_mask,
    drop_bits,
    reduce_weight,
    spatial_weight,
    expand_weight,
    inner_gain,
    inner_bias,
    outer_gain,
    outer_bias,
    head_weight,
    head_bias,
    head_cotangent,
):
    section = lax.axis_index("section")
    first = section == 0
    rows, width, channels = canvases.shape[1:]
    head_cols = head_weight.shape[1]
    pixels = rows * width
    flat = canvases.reshape(pixels, channels)
    info = pixel_info(pick(pixel_mask, section), pick(crop_starts, section))
    heads, hwg, hbg, igs, ibs, ogs, obs, rs, rc, info, merged, u1, zc, za, zb, r1, wr, ws, we = forward(
        flat,
        drop_bits,
        head_cotangent,
        reduce_weight[0],
        spatial_weight[0],
        expand_weight[0],
        inner_gain[0],
        inner_bias[0],
        outer_gain,
        outer_bias,
        head_weight.T,
        head_bias[None],
        info,
    )
    grad, expand_total, spatial_total, reduce_total, small = backward(
        flat, u1, merged, zc, za, zb, r1, wr, ws, we, igs, ibs, ogs, obs, rs, rc, hwg, hbg, info
    )
    small = small.reshape(-1, TILE).astype(jnp.float32)
    expand_total = expand_total.reshape(TILE, channels)
    spatial_total = spatial_total.reshape(-1, TILE, TILE)
    reduce_total = reduce_total.reshape(channels, TILE)
    half = channels // 2
    across = channels // TILE
    head_w_out = jnp.concatenate([small[:head_cols].T, small[head_cols : 2 * head_cols].T])
    row = 2 * head_cols
    cut = head_cols // 2
    head_b_out = jnp.where(first, small[row, :cut], small[row, cut:head_cols])
    norms = small[row + 8 :]
    return (
        heads.reshape(1, rows, width, head_cols),
        grad.reshape(1, rows, width, channels),
        reduce_total.astype(jnp.float32)[None],
        spatial_total.astype(jnp.float32)[None],
        expand_total.astype(jnp.float32)[None],
        norms[0:2][None],
        norms[2:4][None],
        norms[4 : 4 + across].reshape(1, channels),
        norms[4 + across : 4 + 2 * across].reshape(1, channels),
        head_w_out,
        head_b_out,
    )


def solution(mesh):
    placed = (
        P("section", "dp", None, None),
        P(),
        P(None, "dp", None),
        P(None, "dp", None, None),
        P("section", None, None),
        P("section", None, None, None),
        P("section", None, None),
        P("section", None, None),
        P("section", None, None),
        P("section", None),
        P("section", None),
        P(),
        P(),
        P(None, "dp", None, None),
    )
    return jax.shard_map(
        local,
        mesh=mesh,
        in_specs=placed,
        out_specs=(
            P("section", "dp", None, None),
            P("section", "dp", None, None),
            P("section", None, None),
            P("section", None, None, None),
            P("section", None, None),
            P("section", None, None),
            P("section", None, None),
            P("section", None),
            P("section", None),
            P("section", None),
            P("section"),
        ),
        check_vma=False,
    )
```

```python
import functools
import math

import jax
import jax.numpy as jnp
from jax import lax
from jax.experimental import pallas as pl
from jax.experimental.pallas import tpu as pltpu
from jax.sharding import PartitionSpec as P

TASKS = 3
HEAD_OUT = 16

EPS = 1e-05
SOFT = 0.05
SHARP = 0.1
LEVELS = 1024.0
ACROSS = (((0,), (0,)), ((), ()))
BESIDE = (((1,), (1,)), ((), ()))
MESH = pl.DeviceIdType.MESH
TILE = 512
LIMIT = 56 * 2**20


def grid_of(size):
    side = math.isqrt(size // 4)
    assert side * side * 4 == size
    return (4, side, side)


class Reducer:
    PACE = 3
    BETWEEN = (7, 9, 6)

    def __init__(self, size, across, taps):
        self.size = size
        nz, ny, nx = grid_of(size)
        self.strides = {}
        for axis, count, stride in (("x", nx, 1), ("y", ny, nx), ("z", nz, nx * ny)):
            for level in range(count.bit_length() - 1):
                self.strides[axis + str(level)] = stride << level
        later = [bit for bit in self.strides if bit[1] != "0"]
        self.orders = [
            [[a + "0" for a in order] + later for order in ("xyz", "yxz", third)]
            for third in ("zxy", "zyx")
        ]
        self.levels = len(self.strides)
        self.row_bits = [bit for bit in self.strides if bit[0] != "x"]
        self.x_bits = [bit for bit in self.strides if bit[0] == "x"]
        self.shape = (2,) * len(self.row_bits) + (16, TILE)
        self.half = 16 << len(self.row_bits)
        self.lines = 2 * self.half
        self.per_tile = TILE // self.lines
        self.counts = [across * self.per_tile, taps * self.per_tile, across * self.per_tile + 1]
        self.real = sum(self.counts)
        self.stages = 2 * self.levels + 3
        self.lag = 4 if self.levels <= 4 else 2
        self.plan(across, taps)

    def plan(self, across, taps):
        tiles = (across, taps, across)
        whole = sum(tiles) + sum(self.BETWEEN)
        assert whole % self.PACE == 0
        self.bursts, written = [], []
        place = base = 0
        for block in range(2):
            clock = block * whole
            for burst in range(3):
                if block == 1 and burst == 2:
                    clock -= self.BETWEEN[1] - 1
                groups = -(-self.counts[burst] // 3)
                ready = []
                for group in range(groups):
                    last = min((3 * group + 2) // self.per_tile, tiles[burst] - 1)
                    ready.append(-(-(clock + last) // self.PACE) - group)
                place = max([place] + ready)
                self.bursts.append((place, groups, base, self.counts[burst]))
                for unit in range(self.counts[burst]):
                    written.append(clock + min(unit // self.per_tile, tiles[burst] - 1))
                place += groups
                base += self.counts[burst]
                clock += tiles[burst] + self.BETWEEN[burst]
        self.last = self.PACE * (place - 1)
        reduced = []
        for place, groups, _, count in self.bursts:
            for unit in range(count):
                reduced.append(self.PACE * (place + unit // 3) + self.lag * (self.levels + 1))
        self.slots = 1
        while any(
            reduced[unit] >= written[unit + self.slots] for unit in range(len(written) - self.slots)
        ):
            self.slots += 1

    def scratch(self):
        units, bf16 = 2 * self.real, jnp.bfloat16
        return [
            pltpu.VMEM((self.slots, 2) + self.shape, bf16),
            pltpu.VMEM((units,) + self.shape, bf16),
            pltpu.VMEM((units,) + self.shape, bf16),
            pltpu.SemaphoreType.DMA((units, 2)),
            pltpu.SemaphoreType.DMA((units, 2)),
            pltpu.SemaphoreType.DMA((units, 2 * self.levels)),
            pltpu.SemaphoreType.DMA((units, 2 * self.levels)),
        ]

    def totals(self, across, taps):
        tail = (self.per_tile, 2) + self.shape
        return [
            (self.per_tile, 2) + self.shape[:-1] + (across * TILE,),
            (taps,) + tail,
            (across,) + tail,
            (2,) + self.shape,
        ]

    def bind(self, total, scratch):
        self.total = total
        (
            self.ring,
            self.res,
            self.land,
            self.pair_send,
            self.pair_recv,
            self.send_sem,
            self.recv_sem,
        ) = scratch
        self.section, self.me = lax.axis_index("section"), lax.axis_index("dp")
        self.bit = {bit: (self.me // stride) % 2 for bit, stride in self.strides.items()}
        self.clock = 0

    def partner(self, bit):
        return (self.section, self.me + (1 - 2 * self.bit[bit]) * self.strides[bit])

    def slot(self, unit):
        if isinstance(unit, int):
            return unit % self.slots
        return lax.rem(unit, self.slots)

    def region(self, order, level, flip):
        place = {bit: self.bit[bit] for bit in order[:level]}
        if flip:
            place[order[level - 1]] = 1 - place[order[level - 1]]
        rows = tuple(place.get(bit, slice(None)) for bit in self.row_bits)
        cols, start, width = slice(None), 0, TILE
        for bit in self.x_bits:
            if bit in place:
                width //= 2
                start = start + place[bit] * width
                cols = pl.ds(pl.multiple_of(start, width), width)
        return rows + (slice(None), cols)

    def pair(self, unit):
        return pltpu.make_async_remote_copy(
            src_ref=self.ring.at[self.slot(unit), 1 - self.section],
            dst_ref=self.res.at[unit],
            send_sem=self.pair_send.at[unit, 1],
            recv_sem=self.pair_recv.at[unit, 0],
            device_id=(1 - self.section, self.me),
            device_id_type=MESH,
        )

    def acc(self, unit):
        return self.ring.at[self.slot(unit), self.section]

    def halve(self, unit, order, level):
        return pltpu.make_async_remote_copy(
            src_ref=self.acc(unit).at[self.region(order, level + 1, True)],
            dst_ref=self.land.at[(unit,) + self.region(order, level + 1, False)],
            send_sem=self.send_sem.at[unit, level],
            recv_sem=self.recv_sem.at[unit, level],
            device_id=self.partner(order[level]),
            device_id_type=MESH,
        )

    def halved(self, unit, order, level):
        self.halve(unit, order, level).wait()
        keep = self.region(order, level + 1, False)
        kept = self.acc(unit).at[keep]
        came = self.land.at[(unit,) + self.region(order, level + 1, True)]
        target = self.res.at[(unit,) + keep] if level == self.levels - 1 else kept
        total = kept[...].astype(jnp.float32) + came[...].astype(jnp.float32)
        target[...] = total.astype(jnp.bfloat16)

    def double(self, unit, order, level):
        ref = self.res.at[(unit,) + self.region(order, level + 1, False)]
        return pltpu.make_async_remote_copy(
            src_ref=ref,
            dst_ref=ref,
            send_sem=self.send_sem.at[unit, self.levels + level],
            recv_sem=self.recv_sem.at[unit, self.levels + level],
            device_id=self.partner(order[level]),
            device_id_type=MESH,
        )

    def places(self, index):
        expand, spatial, reduce, small = self.total
        tile, part = index // self.per_tile, index % self.per_tile
        across, taps = reduce.shape[0], spatial.shape[0]
        half = self.section
        inner = (slice(None),) * (len(self.shape) - 1)

        def in_expand():
            cols = tile * TILE if isinstance(tile, int) else pl.multiple_of(tile * TILE, TILE)
            return expand.at[(part, half) + inner + (pl.ds(cols, TILE),)]

        return [
            (0 <= tile < across if isinstance(tile, int) else tile < across, in_expand),
            (
                self.both(tile >= across, tile < across + taps),
                lambda: spatial.at[tile - across, part, half],
            ),
            (
                self.both(tile >= across + taps, index < self.real - 1),
                lambda: reduce.at[tile - across - taps, part, half],
            ),
            (index == self.real - 1, lambda: small.at[half]),
        ]

    @staticmethod
    def both(first, second):
        if isinstance(first, bool) and isinstance(second, bool):
            return first and second
        return jnp.logical_and(first, second)

    def final(self, unit, target):
        here = pltpu.make_async_copy(self.res.at[unit], target, self.pair_send.at[unit, 0])
        away = pltpu.make_async_remote_copy(
            src_ref=self.res.at[unit],
            dst_ref=target,
            send_sem=self.pair_send.at[unit, 0],
            recv_sem=self.pair_recv.at[unit, 1],
            device_id=(1 - self.section, self.me),
            device_id_type=MESH,
        )
        return here, away

    def owner(self, unit):
        if isinstance(unit, int):
            return self.section == 1 - unit // self.real, unit % self.real
        later = (unit >= self.real).astype(jnp.int32)
        return self.section == 1 - later, unit - later * self.real

    def finish(self, unit):
        mine, index = self.owner(unit)

        def send(place):
            pl.when(mine)(lambda: self.final(unit, place())[0].start())
            pl.when(jnp.logical_not(mine))(lambda: self.final(unit, place())[1].start())

        for wanted, place in self.places(index):
            if isinstance(wanted, bool):
                if wanted:
                    send(place)
            else:
                pl.when(wanted)(functools.partial(send, place))

    def finished(self, unit):
        mine, _ = self.owner(unit)
        here, away = self.final(unit, self.total[3].at[self.section])

        @pl.when(mine)
        def _():
            here.wait()
            away.wait_recv()

        pl.when(jnp.logical_not(mine))(away.wait_send)

    def step(self, number, unit, order):
        levels = self.levels
        if number == 0:
            self.pair(unit).start()
        elif number == 1:
            self.pair(unit).wait()
            acc = self.acc(unit)
            total = acc[...].astype(jnp.float32) + self.res[unit].astype(jnp.float32)
            acc[...] = total.astype(jnp.bfloat16)
            self.halve(unit, order, 0).start()
        elif number <= levels:
            self.halved(unit, order, number - 2)
            self.halve(unit, order, number - 1).start()
        elif number == levels + 1:
            self.halved(unit, order, levels - 1)
            self.double(unit, order, levels - 1).start()
        elif number <= 2 * levels:
            level = 2 * levels - number
            self.double(unit, order, level + 1).wait()
            self.double(unit, order, level).start()
        elif number == 2 * levels + 1:
            self.double(unit, order, 0).wait()
            self.finish(unit)
        else:
            self.finished(unit)

    def locate(self, group):
        for place, groups, base, count in self.bursts:
            at = group - place
            if 0 <= at < groups:
                return base + 3 * at, min(3, count - 3 * at)
        return None

    def tick(self, time):
        for number in reversed(range(self.stages)):
            when = time - self.lag * number
            if when % self.PACE:
                continue
            group = when // self.PACE
            place = self.locate(group)
            if place is not None:
                for slot in range(place[1]):
                    order = self.orders[group % 2][slot]
                    self.step(number, place[0] + slot, order)

    def pump(self, count=1):
        for _ in range(count):
            self.tick(self.clock)
            self.clock += 1

    def burst(self, number, tiles, put, extra=None):
        base = self.bursts[number][2]
        for tile in range(tiles):
            put(tile, base + tile * self.per_tile)
            if tile == tiles - 1 and extra is not None:
                extra(base + tiles * self.per_tile)
            self.pump()

    def drain(self):
        self.pump(self.last + self.lag * (self.stages - 1) + 1 - self.clock)


def sigmoid(v):
    return 0.5 + 0.5 * jnp.tanh(0.5 * v)


def silu_parts(v):
    sigma = sigmoid(v)
    return v * sigma, sigma * (1.0 + v * (1.0 - sigma))


def folded(x):
    return jnp.sum(x.reshape(x.shape[0] // 8, 8, x.shape[1]), axis=0)


class Exchange:
    def __init__(self, size, send_sem, recv_sem, edge_send, edge_recv):
        self.size = size
        self.section, self.me = lax.axis_index("section"), lax.axis_index("dp")
        self.send_sem, self.recv_sem = send_sem, recv_sem
        self.edge_send, self.edge_recv = edge_send, edge_recv

    def greet(self):
        barrier = pltpu.get_barrier_semaphore()
        for step in range(1, self.size):
            peer = (self.section, lax.rem(self.me + step, self.size))
            pl.semaphore_signal(barrier, inc=1, device_id=peer, device_id_type=MESH)
        other = (1 - self.section, self.me)
        pl.semaphore_signal(barrier, inc=1, device_id=other, device_id_type=MESH)
        pl.semaphore_wait(barrier, self.size)

    def copies(self, number, slots):
        return [
            pltpu.make_async_remote_copy(
                src_ref=slots.at[0],
                dst_ref=slots.at[step],
                send_sem=self.send_sem.at[number, step],
                recv_sem=self.recv_sem.at[number, step],
                device_id=(self.section, lax.rem(self.me + step, self.size)),
                device_id_type=MESH,
            )
            for step in range(1, self.size)
        ]

    def edges(self, number, first, last, landing):
        made = []
        for way, (ref, step) in enumerate(((first, self.size - 1), (last, 1))):
            made.append(
                pltpu.make_async_remote_copy(
                    src_ref=ref,
                    dst_ref=landing.at[1 - way],
                    send_sem=self.edge_send.at[number, way],
                    recv_sem=self.edge_recv.at[number, 1 - way],
                    device_id=(self.section, lax.rem(self.me + step, self.size)),
                    device_id_type=MESH,
                )
            )
        return made

    def start_edges(self, number, first, last, landing):
        up, down = self.edges(number, first, last, landing)
        pl.when(self.me > 0)(up.start)
        pl.when(self.me < self.size - 1)(down.start)

    def wait_edges(self, number, first, last, landing):
        up, down = self.edges(number, first, last, landing)
        pl.when(self.me > 0)(up.wait_send)
        pl.when(self.me > 0)(down.wait_recv)
        pl.when(self.me < self.size - 1)(down.wait_send)
        pl.when(self.me < self.size - 1)(up.wait_recv)


def forward_kernel(
    size,
    u_hbm,
    bits_hbm,
    cot_hbm,
    wr_hbm,
    ws_hbm,
    we_hbm,
    ig_ref,
    ib_ref,
    og_ref,
    ob_ref,
    hwt_ref,
    hb_ref,
    info_ref,
    mask_ref,
    heads_ref,
    hwg_ref,
    hbg_ref,
    igs,
    ibs,
    ogs,
    obs,
    rs_ref,
    rc_ref,
    info_out,
    sums_out,
    merged_hbm,
    u1_hbm,
    zc_hbm,
    za_hbm,
    zb_hbm,
    r1_hbm,
    wr_all,
    ws_all,
    we_all,
    wr,
    ws,
    we,
    u0,
    u1,
    a_ref,
    b_ref,
    e_ref,
    cat,
    r2,
    za,
    zb,
    zc,
    merged,
    bits,
    cot,
    edge,
    halo,
    live_halo,
    msg,
    msg_c,
    first_msg,
    stat,
    stat_c,
    part_sum,
    send_sem,
    recv_sem,
    edge_send,
    edge_recv,
    w_load,
    w_send,
    w_recv,
    w_out,
    in_sem,
    bit_sem,
    out_sem,
):
    link = Exchange(size, send_sem, recv_sem, edge_send, edge_recv)
    section, me = link.section, link.me
    pixels, channels = u0.shape
    inner = a_ref.shape[1]
    rows, width = bits_hbm.shape[1], bits_hbm.shape[2]
    f32, bf16 = jnp.float32, jnp.bfloat16

    load_u = pltpu.make_async_copy(u_hbm, u0, in_sem.at[0])
    load_cot = pltpu.make_async_copy(cot_hbm.at[section], cot, in_sem.at[1])

    def load_bits(chunk):
        return pltpu.make_async_copy(
            bits_hbm.at[section, chunk], bits.at[chunk % 2], bit_sem.at[chunk % 2]
        )

    load_u.start()
    load_cot.start()
    load_bits(0).start()
    load_bits(1).start()

    weights = ((wr_hbm, wr, wr_all), (ws_hbm, ws, ws_all), (we_hbm, we, we_all))

    def local_load(kind):
        source, target, _ = weights[kind]
        return pltpu.make_async_copy(source, target.at[section], w_load.at[kind])

    def pushed(kind):
        source, target, _ = weights[kind]
        return pltpu.make_async_remote_copy(
            src_ref=source,
            dst_ref=target.at[section],
            send_sem=w_send.at[kind],
            recv_sem=w_recv.at[kind],
            device_id=(1 - section, me),
            device_id_type=MESH,
        )

    vectors = ((ig_ref, igs), (ib_ref, ibs), (og_ref, ogs), (ob_ref, obs))

    def pushed_vector(kind):
        source, target = vectors[kind]
        return pltpu.make_async_remote_copy(
            src_ref=source,
            dst_ref=target.at[section],
            send_sem=w_send.at[3 + kind],
            recv_sem=w_recv.at[3 + kind],
            device_id=(1 - section, me),
            device_id_type=MESH,
        )

    def save_weight(kind, layer):
        _, target, saved = weights[kind]
        return pltpu.make_async_copy(target.at[layer], saved.at[layer], w_out.at[kind, layer])

    for kind in range(3):
        local_load(kind).start()
    link.greet()
    for kind in range(4):
        pushed_vector(kind).start()
    for kind in range(3):
        pushed(kind).start()
    for source, target in vectors:
        target[section] = source[...]

    def need_weight(kind, layer):
        pl.when(section == layer)(local_load(kind).wait)
        pl.when(section != layer)(pushed(kind).wait_recv)
        save_weight(kind, layer).start()

    own = pl.ds(width, pixels)
    live_edges = (info_ref.at[pl.ds(0, width)], info_ref.at[pl.ds(pixels - width, width)])

    def drop_chunk(chunk):
        load_bits(chunk).wait()
        start = pl.multiple_of(chunk * width, 16)
        target = cot[chunk].astype(f32) * mask_ref[chunk : chunk + 1]
        task = lax.broadcasted_iota(jnp.int32, target.shape, 0) // HEAD_OUT
        parts = [jnp.where(task == k, target, 0.0).astype(bf16) for k in range(TASKS)]

        @pl.loop(0, channels // TILE)
        def _(tile):
            cols = pl.ds(pl.multiple_of(tile * TILE, TILE), TILE)
            table = hwt_ref[:, cols]
            signed = magnitude = weighted = None
            for part in parts:
                value = lax.dot_general(part, table, ACROSS, preferred_element_type=f32)
                square = value * value
                whole = square + SOFT * SOFT
                inverse = lax.rsqrt(whole)
                if signed is None:
                    signed, magnitude, weighted = value, whole * inverse, square * inverse
                else:
                    signed = signed + value
                    magnitude = magnitude + whole * inverse
                    weighted = weighted + square * inverse
            level = bits[chunk % 2, :, cols].astype(f32)
            reach = 0.25 / SHARP
            inside = reach * (signed / magnitude) + (
                reach * (1.0 - 1.0 / LEVELS) - (2.0 * reach / LEVELS) * level
            )
            value = 0.5 * signed + (0.5 * jnp.tanh(inside)) * weighted
            merged[pl.ds(start, width), cols] = value.astype(bf16)

        if chunk + 2 < rows:
            load_bits(chunk + 2).start()

    live_all = info_ref[:, 0:1]
    count_here = jnp.sum(live_all, axis=0, keepdims=True)
    share = 1.0 / count_here

    def column_stats(values):
        mean = jnp.sum(values * live_all, axis=0, keepdims=True) * share
        apart = values - mean
        return mean, jnp.sum(live_all * apart * apart, axis=0, keepdims=True)

    def counts(step):
        return first_msg[step, 2:3, 0:1]

    def combine(slots):
        number = counts(0)
        mean = slots[0, 0:1] * counts(0)
        spread = slots[0, 1:2]
        for step in range(1, size):
            number = number + counts(step)
            mean = mean + slots[step, 0:1] * counts(step)
            spread = spread + slots[step, 1:2]
        mean = mean / number
        for step in range(size):
            apart = slots[step, 0:1] - mean
            spread = spread + counts(step) * apart * apart
        return mean, lax.rsqrt(spread / number + EPS), number

    load_u.wait()
    load_cot.wait()
    drop_chunk(0)
    first_msg[0, 2:3] = jnp.broadcast_to(count_here, (1, inner))
    first_msg[0, 3:4] = jnp.zeros((1, inner), f32)
    zc_out = za_out = zb_out = r1_out = None
    u1_out = pltpu.make_async_copy(u1, u1_hbm, out_sem.at[0])
    for layer in range(2):
        x_ref = (u0, u1)[layer]
        need_weight(0, layer)
        slots = first_msg if layer == 0 else msg.at[0]

        @pl.loop(0, inner // 256)
        def _(tile):
            cols = pl.ds(pl.multiple_of(tile * 256, 256), 256)
            values = jnp.dot(x_ref[...], wr[layer, :, cols], preferred_element_type=f32)
            a_ref[:, cols] = values
            mean, spread = column_stats(values)
            slots[0, 0:1, cols] = mean
            slots[0, 1:2, cols] = spread

        if layer == 1:
            for copy in (za_out, zb_out, r1_out, zc_out):
                copy.wait()
            u1_out.start()
        sends = link.copies(3 * layer, slots)
        for copy in sends:
            copy.start()
        centre = slots[0, 0:1]
        edge[0] = (a_ref[0:width] - centre).astype(bf16)
        edge[1] = (a_ref[pixels - width : pixels] - centre).astype(bf16)
        a_edges = (edge.at[0], edge.at[1])
        a_halo = halo.at[2 * layer]
        link.start_edges(2 * layer, *a_edges, a_halo)
        if layer == 0:
            link.start_edges(4, *live_edges, live_halo)
            for kind in range(4):
                pushed_vector(kind).wait()
        drop_chunk(1 + 3 * layer)
        for copy in sends:
            copy.wait()
        mean, inverse, number = combine(slots)
        stat[layer, 0:1], stat[layer, 1:2] = mean, inverse
        rs_ref[layer, 0:1] = inverse
        rs_ref[layer, 2:3] = jnp.broadcast_to(number, (1, inner))

        def first_act(row, values, inside):
            normed = (values - stat[layer, 0:1]) * stat[layer, 1:2]
            affine = normed * igs[layer, 0:1] + ibs[layer, 0:1]
            act = affine * sigmoid(affine)
            if inside is not None:
                act = jnp.where(inside, act, 0.0)
            here = pl.ds(pl.multiple_of(row * width, 16), width)
            masks = info_ref[0:width]
            cat[here, 0:inner] = (pltpu.roll(act, 1, 0) * masks[:, 1:2]).astype(bf16)
            cat[here, inner : 2 * inner] = act.astype(bf16)
            cat[here, 2 * inner : 3 * inner] = (
                pltpu.roll(act, width - 1, 0) * masks[:, 2:3]
            ).astype(bf16)
            return normed

        @pl.loop(0, rows)
        def _(row):
            here = pl.ds(pl.multiple_of(row * width, 16), width)
            za[here] = first_act(row + 1, a_ref[here], None).astype(bf16)

        link.wait_edges(2 * layer, *a_edges, a_halo)
        first_act(0, a_halo[0].astype(f32) + slots[1, 0:1], me > 0)
        first_act(rows + 1, a_halo[1].astype(f32) + slots[size - 1, 0:1], me < size - 1)

        za_out = pltpu.make_async_copy(za, za_hbm.at[layer], out_sem.at[1])
        r1_out = pltpu.make_async_copy(
            cat.at[:, pl.ds(inner, inner)], r1_hbm.at[layer], out_sem.at[2]
        )
        za_out.start()
        r1_out.start()
        need_weight(1, layer)
        slots = msg.at[1 + 2 * layer]

        @pl.loop(0, inner // 256)
        def _(tile):
            cols = pl.ds(pl.multiple_of(tile * 256, 256), 256)
            values = None
            for tap in range(3):
                table = ws[layer, 3 * tap : 3 * tap + 3, :, cols].reshape(3 * inner, 256)
                value = jnp.dot(
                    cat[tap * width : tap * width + pixels], table, preferred_element_type=f32
                )
                values = value if values is None else values + value
            b_ref[:, cols] = values
            mean, spread = column_stats(values)
            slots[0, 0:1, cols] = mean
            slots[0, 1:2, cols] = spread

        sends = link.copies(3 * layer + 1, slots)
        for copy in sends:
            copy.start()
        drop_chunk(2 + 3 * layer)
        for copy in sends:
            copy.wait()
        mean, inverse, _ = combine(slots)
        stat[layer, 2:3], stat[layer, 3:4] = mean, inverse
        rs_ref[layer, 1:2] = inverse

        @pl.loop(0, rows)
        def _(row):
            here = pl.ds(pl.multiple_of(row * width, 16), width)
            normed = (b_ref[here] - stat[layer, 2:3]) * stat[layer, 3:4]
            zb[pl.ds(pl.multiple_of((row + 1) * width, 16), width)] = normed.astype(bf16)
            affine = normed * igs[layer, 1:2] + ibs[layer, 1:2]
            r2[here] = (affine * sigmoid(affine)).astype(bf16)

        b_edges = (zb.at[pl.ds(width, width)], zb.at[pl.ds(pixels, width)])
        b_halo = halo.at[2 * layer + 1]
        link.start_edges(2 * layer + 1, *b_edges, b_halo)
        need_weight(2, layer)
        slots = msg_c.at[layer]

        @pl.loop(0, channels // 256)
        def _(tile):
            cols = pl.ds(pl.multiple_of(tile * 256, 256), 256)
            values = jnp.dot(r2[...], we[layer, :, cols], preferred_element_type=f32)
            e_ref[:, cols] = values
            mean, spread = column_stats(values)
            slots[0, 0:1, cols] = mean
            slots[0, 1:2, cols] = spread

        sends = link.copies(3 * layer + 2, slots)
        for copy in sends:
            copy.start()
        drop_chunk(3 + 3 * layer)
        if layer == 0:
            link.wait_edges(4, *live_edges, live_halo)
            info_out[own] = info_ref[...]
            info_out[0:width] = live_halo[0]
            info_out[pixels + width : pixels + 2 * width] = live_halo[1]
        if layer == 1:
            drop_chunk(7)
        link.wait_edges(2 * layer + 1, *b_edges, b_halo)
        for side, row in ((0, 0), (1, rows + 1)):
            zb[row * width : (row + 1) * width] = b_halo[side]
        zb_out = pltpu.make_async_copy(zb, zb_hbm.at[layer], out_sem.at[3])
        zb_out.start()
        for copy in sends:
            copy.wait()
        mean, inverse, _ = combine(slots)
        stat_c[0:1], stat_c[1:2] = mean, inverse
        rc_ref[layer] = inverse
        out_ref = (u1, u0)[layer]
        if layer == 1:
            part_sum[...] = jnp.zeros_like(part_sum)

        @pl.loop(0, rows * (channels // TILE))
        def _(chunk):
            row, tile = chunk // (channels // TILE), chunk % (channels // TILE)
            here = pl.ds(pl.multiple_of(row * width, 16), width)
            cols = pl.ds(pl.multiple_of(tile * TILE, TILE), TILE)
            normed = (e_ref[here, cols] - stat_c[0:1, cols]) * stat_c[1:2, cols]
            zc[here, cols] = normed.astype(bf16)
            total = normed * ogs[layer, :, cols] + obs[layer, :, cols] + x_ref[here, cols].astype(f32)
            if layer == 0:
                out_ref[here, cols] = (total * sigmoid(total)).astype(bf16)
            else:
                act, slope = silu_parts(total)
                out_ref[here, cols] = act.astype(bf16)
                dt = merged[here, cols].astype(f32) * slope
                merged[here, cols] = dt.astype(bf16)
                part_sum[0, :, cols] += folded(dt)
                part_sum[1, :, cols] += folded(dt * normed)

        zc_out = pltpu.make_async_copy(zc, zc_hbm.at[layer], out_sem.at[5])
        zc_out.start()

    pltpu.make_async_copy(merged, merged_hbm, out_sem.at[4]).start()
    slots = msg_c.at[2]
    slots[0, 0:1] = jnp.sum(part_sum[0], axis=0, keepdims=True)
    slots[0, 1:2] = jnp.sum(part_sum[1], axis=0, keepdims=True)
    sends = link.copies(6, slots)
    for copy in sends:
        copy.start()

    bias_sum = None
    for row in range(rows):
        lines = pl.ds(row * width, width)
        heads_ref[row] = (
            lax.dot_general(hwt_ref[...], u0[lines], BESIDE, preferred_element_type=f32)
            + hb_ref[...].T
        )
        target = cot[row].astype(f32) * mask_ref[row : row + 1]
        lanes = jnp.sum(target, axis=1, keepdims=True)
        bias_sum = lanes if bias_sum is None else bias_sum + lanes
        part = jnp.dot(target.astype(bf16), u0[lines], preferred_element_type=f32)
        if row == 0:
            hwg_ref[...] = part
        else:
            hwg_ref[...] += part
    hbg_ref[...] = bias_sum

    for copy in sends:
        copy.wait()
    found = slots[0]
    for step in range(1, size):
        found = found + slots[step]
    sums_out[...] = found
    for copy in (za_out, zb_out, r1_out, zc_out, u1_out):
        copy.wait()
    pltpu.make_async_copy(merged, merged_hbm, out_sem.at[4]).wait()
    for kind in range(3):
        pushed(kind).wait_send()
        for layer in range(2):
            save_weight(kind, layer).wait()


def forward(u, bits, cot, wr, ws, we, ig, ib, og, ob, hwt, hb, info, mask):
    size = lax.axis_size("dp")
    pixels, channels = u.shape
    inner = wr.shape[1]
    _, rows, head_cols, width = cot.shape
    f32, bf16 = jnp.float32, jnp.bfloat16
    padded = pixels + 2 * width
    anywhere = pl.BlockSpec(memory_space=pl.ANY)
    vmem = pl.BlockSpec(memory_space=pltpu.VMEM)

    def out(kind, *shape):
        return jax.ShapeDtypeStruct(shape, kind)

    return pl.pallas_call(
        functools.partial(forward_kernel, size),
        out_shape=[
            out(f32, rows, head_cols, width),
            out(f32, head_cols, channels),
            out(f32, head_cols, 1),
            out(f32, 2, 2, inner),
            out(f32, 2, 2, inner),
            out(f32, 2, 1, channels),
            out(f32, 2, 1, channels),
            out(f32, 2, 8, inner),
            out(f32, 2, 1, channels),
            out(f32, padded, 128),
            out(f32, 2, channels),
            out(bf16, pixels, channels),
            out(bf16, pixels, channels),
            out(bf16, 2, pixels, channels),
            out(bf16, 2, pixels, inner),
            out(bf16, 2, padded, inner),
            out(bf16, 2, padded, inner),
            out(bf16, 2, channels, inner),
            out(bf16, 2, 9, inner, inner),
            out(bf16, 2, inner, channels),
        ],
        in_specs=[anywhere] * 6 + [vmem] * 8,
        out_specs=[vmem] * 11 + [anywhere] * 9,
        scratch_shapes=[
            pltpu.VMEM((2, channels, inner), bf16),
            pltpu.VMEM((2, 9, inner, inner), bf16),
            pltpu.VMEM((2, inner, channels), bf16),
            pltpu.VMEM((pixels, channels), bf16),
            pltpu.VMEM((pixels, channels), bf16),
            pltpu.VMEM((pixels, inner), f32),
            pltpu.VMEM((pixels, inner), f32),
            pltpu.VMEM((pixels, channels), f32),
            pltpu.VMEM((padded, 3 * inner), bf16),
            pltpu.VMEM((pixels, inner), bf16),
            pltpu.VMEM((pixels, inner), bf16),
            pltpu.VMEM((padded, inner), bf16),
            pltpu.VMEM((pixels, channels), bf16),
            pltpu.VMEM((pixels, channels), bf16),
            pltpu.VMEM((2, width, channels), jnp.int32),
            pltpu.VMEM((rows, head_cols, width), bf16),
            pltpu.VMEM((2, width, inner), bf16),
            pltpu.VMEM((4, 2, width, inner), bf16),
            pltpu.VMEM((2, width, 128), f32),
            pltpu.VMEM((4, size, 2, inner), f32),
            pltpu.VMEM((3, size, 2, channels), f32),
            pltpu.VMEM((size, 4, inner), f32),
            pltpu.VMEM((2, 8, inner), f32),
            pltpu.VMEM((2, channels), f32),
            pltpu.VMEM((2, 8, channels), f32),
            pltpu.SemaphoreType.DMA((7, size)),
            pltpu.SemaphoreType.DMA((7, size)),
            pltpu.SemaphoreType.DMA((5, 2)),
            pltpu.SemaphoreType.DMA((5, 2)),
            pltpu.SemaphoreType.DMA((3,)),
            pltpu.SemaphoreType.DMA((7,)),
            pltpu.SemaphoreType.DMA((7,)),
            pltpu.SemaphoreType.DMA((3, 2)),
            pltpu.SemaphoreType.DMA((2,)),
            pltpu.SemaphoreType.DMA((2,)),
            pltpu.SemaphoreType.DMA((6,)),
        ],
        compiler_params=pltpu.CompilerParams(
            collective_id=1, has_side_effects=True, vmem_limit_bytes=LIMIT
        ),
    )(u, bits, cot, wr, ws, we, ig, ib, og, ob, hwt, hb, info, mask)


def backward_kernel(
    size,
    reducer,
    u0_hbm,
    u1_hbm,
    merged_hbm,
    zc_hbm,
    za_hbm,
    zb_hbm,
    r1_hbm,
    wr_all,
    ws_all,
    we_all,
    igs,
    ibs,
    ogs,
    obs,
    rs_ref,
    rc_ref,
    hwg_ref,
    hbg_ref,
    info_ref,
    sums_ref,
    grad_hbm,
    expand_hbm,
    spatial_hbm,
    reduce_hbm,
    small_hbm,
    wr,
    ws,
    we,
    u_ref,
    d_ref,
    zc,
    za,
    zb,
    r1,
    r2,
    wide,
    dz_ref,
    da,
    small,
    edge,
    halo,
    msg,
    msg_c,
    part_sum,
    sums,
    sums_c,
    send_sem,
    recv_sem,
    edge_send,
    edge_recv,
    in_sem,
    out_sem,
    *scratch,
):
    reducer.bind((expand_hbm, spatial_hbm, reduce_hbm, small_hbm), scratch)
    link = Exchange(size, send_sem, recv_sem, edge_send, edge_recv)
    section, me = link.section, link.me
    pixels, channels = d_ref.shape
    inner = da.shape[1]
    width = halo.shape[2]
    rows = pixels // width
    across = channels // TILE
    f32, bf16 = jnp.float32, jnp.bfloat16
    own = pl.ds(width, pixels)
    de, cat = wide.at[pl.ds(0, pixels)], wide.at[:, pl.ds(0, 3 * inner)]

    def loads(layer):
        return {
            "zc": pltpu.make_async_copy(zc_hbm.at[layer], zc, in_sem.at[0]),
            "za": pltpu.make_async_copy(za_hbm.at[layer], za, in_sem.at[1]),
            "zb": pltpu.make_async_copy(zb_hbm.at[layer], zb, in_sem.at[2]),
            "r1": pltpu.make_async_copy(r1_hbm.at[layer], r1, in_sem.at[3]),
            "wr": pltpu.make_async_copy(wr_all.at[layer], wr, in_sem.at[4]),
            "ws": pltpu.make_async_copy(ws_all.at[layer], ws, in_sem.at[5]),
            "we": pltpu.make_async_copy(we_all.at[layer], we, in_sem.at[6]),
            "u": pltpu.make_async_copy((u0_hbm, u1_hbm)[layer], u_ref.at[layer], in_sem.at[7 + layer]),
        }

    load_d = pltpu.make_async_copy(merged_hbm, d_ref, in_sem.at[9])
    first, second = loads(1), loads(0)
    load_d.start()
    for name in ("zc", "we", "zb", "ws", "za", "r1", "wr", "u"):
        first[name].start()
    second["u"].start()
    link.greet()
    live_all = info_ref[own, 0:1]

    def put_tile(unit, make):
        @pl.loop(0, 2)
        def _(side):
            cols = pl.ds(pl.multiple_of(side * 256, 256), 256)
            value = make(side).astype(bf16)
            inside = (slice(None),) * len(reducer.shape)
            for part in range(reducer.per_tile):
                lines = value[part * reducer.lines : (part + 1) * reducer.lines]
                at = (reducer.slot(unit + part),) + inside + (cols,)
                reducer.ring[at] = lines.reshape((2,) + reducer.shape[:-1] + (256,))

    def column_sums(values):
        return jnp.sum(values, axis=0, keepdims=True)

    def total_of(slots):
        found = slots[0]
        for step in range(1, size):
            found = found + slots[step]
        return found

    def expand_tiles(layer):
        def put(tile, unit):
            def make(side):
                cols = pl.ds(pl.multiple_of(tile * TILE + side * 256, 256), 256)
                return lax.dot_general(r2[...], de[:, cols], ACROSS, preferred_element_type=f32)

            put_tile(unit, make)

        reducer.burst(3 * (1 - layer), across, put)

    def spatial_tiles(layer):
        def put(tap, unit):
            shift, side_step = tap // 3, tap % 3

            def make(side):
                at = pl.ds(pl.multiple_of(shift * width, 16), pixels)
                cols = pl.ds(pl.multiple_of(side_step * inner + side * 256, 256), 256)
                return lax.dot_general(r1[at], cat[own, cols], ACROSS, preferred_element_type=f32)

            put_tile(unit, make)

        reducer.burst(3 * (1 - layer) + 1, 9, put)

    def reduce_tiles(layer):
        def put(tile, unit):
            def make(side):
                cols = pl.ds(pl.multiple_of(side * 256, 256), 256)
                lines = pl.ds(pl.multiple_of(tile * TILE, TILE), TILE)
                return lax.dot_general(
                    u_ref[layer, :, lines], da[:, cols], ACROSS, preferred_element_type=f32
                )

            put_tile(unit, make)

        reducer.burst(3 * (1 - layer) + 2, across, put, functools.partial(small_unit, layer))

    def small_unit(layer, unit):
        half = channels // 2
        head_cols = hwg_ref.shape[0]
        small[...] = jnp.zeros_like(small)
        for k in range(2):
            at = layer * half + k * TILE
            small[k * head_cols : (k + 1) * head_cols] = hwg_ref[:, at : at + TILE]
        row = 2 * head_cols
        small[row : row + 1, 0:head_cols] = hbg_ref[...].T
        only = (me == 0).astype(f32)
        small[row + 8 : row + 9] = sums[0, 1:2] * only
        small[row + 9 : row + 10] = sums[1, 1:2] * only
        small[row + 10 : row + 11] = sums[0, 0:1] * only
        small[row + 11 : row + 12] = sums[1, 0:1] * only
        for k in range(across):
            cols = slice(k * TILE, (k + 1) * TILE)
            small[row + 12 + k : row + 13 + k] = sums_c[1:2, cols] * only
            small[row + 12 + across + k : row + 13 + across + k] = sums_c[0:1, cols] * only
        slot = reducer.slot(unit)
        blank = jnp.zeros(reducer.shape, bf16)
        reducer.ring[slot, 0] = small[0 : reducer.half].astype(bf16).reshape(reducer.shape)
        reducer.ring[slot, 1] = blank

    load_d.wait()
    for layer in (1, 0):
        now = (second, first)[layer]
        now["zc"].wait()
        if layer == 0:
            now["u"].wait()
            first["u"].wait()
        if layer == 0:
            part_sum[...] = jnp.zeros_like(part_sum)

        def dt_chunk(chunk):
            row, tile = chunk // across, chunk % across
            here = pl.ds(pl.multiple_of(row * width, 16), width)
            cols = pl.ds(pl.multiple_of(tile * TILE, TILE), TILE)
            normed = zc[here, cols].astype(f32)
            total = (
                normed * ogs[layer, :, cols]
                + obs[layer, :, cols]
                + u_ref[layer, here, cols].astype(f32)
            )
            _, slope = silu_parts(total)
            dt = d_ref[here, cols].astype(f32) * slope
            d_ref[here, cols] = dt.astype(bf16)
            part_sum[0, :, cols] += folded(dt)
            part_sum[1, :, cols] += folded(dt * normed)

        if layer == 1:
            sums_c[...] = sums_ref[...]
        else:
            for part in range(4):
                pl.loop(part * (rows * across // 4), (part + 1) * (rows * across // 4))(dt_chunk)
                reducer.pump()
            slots = msg_c
            slots[0, 0:1] = column_sums(part_sum[0])
            slots[0, 1:2] = column_sums(part_sum[1])
            sends = link.copies(0, slots)
            for copy in sends:
                copy.start()
            reduce_tiles(1)
            for copy in sends:
                copy.wait()
            sums_c[...] = total_of(slots)
        number = rs_ref[layer, 2:3, 0:1]
        share = 1.0 / number

        def de_chunk(chunk):
            row, tile = chunk // across, chunk % across
            here = pl.ds(pl.multiple_of(row * width, 16), width)
            cols = pl.ds(pl.multiple_of(tile * TILE, TILE), TILE)
            live = info_ref[pl.ds(pl.multiple_of((row + 1) * width, 16), width), 0:1]
            normed = zc[here, cols].astype(f32)
            away = (sums_c[0:1, cols] + normed * sums_c[1:2, cols]) * share
            scale = rc_ref[layer, :, cols] * ogs[layer, :, cols]
            value = scale * (d_ref[here, cols].astype(f32) - live * away)
            de[here, cols] = value.astype(bf16)

        for part in range(4):
            pl.loop(part * (rows * across // 4), (part + 1) * (rows * across // 4))(de_chunk)
            if layer == 0:
                reducer.pump()
        now["we"].wait()
        now["zb"].wait()
        slots = msg.at[2 * layer]

        for tile in range(inner // 256):
            cols = pl.ds(tile * 256, 256)
            dr2 = lax.dot_general(de[...], we[cols], BESIDE, preferred_element_type=f32)
            normed = zb[own, cols].astype(f32)
            act, slope = silu_parts(normed * igs[layer, 1:2, cols] + ibs[layer, 1:2, cols])
            r2[:, cols] = act.astype(bf16)
            dz = dr2 * slope
            dz_ref[:, cols] = dz
            slots[0, 0:1, cols] = column_sums(dz)
            slots[0, 1:2, cols] = column_sums(dz * normed)
            if layer == 0:
                reducer.pump()

        sends = link.copies(3 * layer + 1, slots)
        for copy in sends:
            copy.start()
        edge[0] = dz_ref[0:width].astype(bf16)
        edge[1] = dz_ref[pixels - width : pixels].astype(bf16)
        edges = (edge.at[0], edge.at[1])
        landing = halo.at[layer]
        link.start_edges(layer, *edges, landing)
        if layer == 1:
            second["zc"].start()
            second["we"].start()
        expand_tiles(layer)
        for copy in sends:
            copy.wait()
        sums[1] = total_of(slots)

        def db_row(row, dz, inside):
            here = pl.ds(pl.multiple_of(row * width, 16), width)
            live = info_ref[here, 0:1]
            normed = zb[here].astype(f32)
            away = (sums[1, 0:1] + normed * sums[1, 1:2]) * share
            value = (rs_ref[layer, 1:2] * igs[layer, 1:2]) * (dz - live * away)
            if inside is not None:
                value = jnp.where(inside, value, 0.0)
            masks = info_ref[pl.ds(width, width), :]
            cat[here, 0:inner] = (pltpu.roll(value, width - 1, 0) * masks[:, 2:3]).astype(bf16)
            cat[here, inner : 2 * inner] = value.astype(bf16)
            cat[here, 2 * inner : 3 * inner] = (
                pltpu.roll(value, 1, 0) * masks[:, 1:2]
            ).astype(bf16)

        def own_db(row):
            db_row(row + 1, dz_ref[pl.ds(pl.multiple_of(row * width, 16), width)], None)

        pl.loop(0, rows // 2)(own_db)
        reducer.pump()
        pl.loop(rows // 2, rows)(own_db)
        reducer.pump()

        link.wait_edges(layer, *edges, landing)
        db_row(0, landing[0].astype(f32), me > 0)
        db_row(rows + 1, landing[1].astype(f32), me < size - 1)
        reducer.pump()

        if layer == 1:
            second["zb"].start()
        now["ws"].wait()
        now["za"].wait()
        slots = msg.at[2 * layer + 1]

        for tile in range(inner // 256):
            cols = pl.ds(tile * 256, 256)
            dr1 = None
            for tap in range(9):
                start = (2 - tap // 3) * width
                block = cat[start : start + pixels, (tap % 3) * inner : (tap % 3 + 1) * inner]
                value = lax.dot_general(block, ws[tap, cols], BESIDE, preferred_element_type=f32)
                dr1 = value if dr1 is None else dr1 + value
                if tap == 4:
                    reducer.pump()
            normed = za[:, cols].astype(f32)
            _, slope = silu_parts(normed * igs[layer, 0:1, cols] + ibs[layer, 0:1, cols])
            dz = dr1 * slope
            dz_ref[:, cols] = dz
            slots[0, 0:1, cols] = column_sums(dz)
            slots[0, 1:2, cols] = column_sums(dz * normed)
            reducer.pump()

        sends = link.copies(3 * layer + 2, slots)
        for copy in sends:
            copy.start()
        if layer == 1:
            second["ws"].start()
        now["r1"].wait()
        spatial_tiles(layer)
        for copy in sends:
            copy.wait()
        sums[0] = total_of(slots)
        if layer == 1:
            second["r1"].start()

        @pl.loop(0, rows)
        def _(row):
            here = pl.ds(pl.multiple_of(row * width, 16), width)
            live = info_ref[pl.ds(pl.multiple_of((row + 1) * width, 16), width), 0:1]
            away = (sums[0, 0:1] + za[here].astype(f32) * sums[0, 1:2]) * share
            value = (rs_ref[layer, 0:1] * igs[layer, 0:1]) * (dz_ref[here] - live * away)
            da[here] = value.astype(bf16)

        if layer == 1:
            second["za"].start()
        now["wr"].wait()
        reducer.pump()

        def du_tile(tile):
            cols = pl.ds(pl.multiple_of(tile * 256, 256), 256)
            du = lax.dot_general(da[...], wr[cols], BESIDE, preferred_element_type=f32)
            d_ref[:, cols] = (du + d_ref[:, cols].astype(f32)).astype(bf16)

        if layer == 0:
            reduce_tiles(0)
        for part in range(4):
            pl.loop(part * (channels // 1024), (part + 1) * (channels // 1024))(du_tile)
            reducer.pump()
        if layer == 1:
            second["wr"].start()
    out = pltpu.make_async_copy(d_ref, grad_hbm, out_sem)
    out.start()
    reducer.drain()
    out.wait()


def backward(u0, u1, merged, zc, za, zb, r1, wr, ws, we, igs, ibs, ogs, obs, rs, rc, hwg, hbg, info, sums):
    size = lax.axis_size("dp")
    pixels, channels = u0.shape
    inner = za.shape[2]
    padded = zb.shape[1]
    width = (padded - pixels) // 2
    f32, bf16 = jnp.float32, jnp.bfloat16
    anywhere = pl.BlockSpec(memory_space=pl.ANY)
    vmem = pl.BlockSpec(memory_space=pltpu.VMEM)
    taps = ws.shape[1]
    reducer = Reducer(size, channels // TILE, taps)
    totals = reducer.totals(channels // TILE, taps)
    return pl.pallas_call(
        functools.partial(backward_kernel, size, reducer),
        out_shape=[
            jax.ShapeDtypeStruct((pixels, channels), bf16),
        ]
        + [jax.ShapeDtypeStruct(shape, bf16) for shape in totals],
        in_specs=[anywhere] * 10 + [vmem] * 10,
        out_specs=[anywhere] * 5,
        scratch_shapes=[
            pltpu.VMEM((channels, inner), bf16),
            pltpu.VMEM((9, inner, inner), bf16),
            pltpu.VMEM((inner, channels), bf16),
            pltpu.VMEM((2, pixels, channels), bf16),
            pltpu.VMEM((pixels, channels), bf16),
            pltpu.VMEM((pixels, channels), bf16),
            pltpu.VMEM((pixels, inner), bf16),
            pltpu.VMEM((padded, inner), bf16),
            pltpu.VMEM((padded, inner), bf16),
            pltpu.VMEM((pixels, inner), bf16),
            pltpu.VMEM((padded, channels), bf16),
            pltpu.VMEM((pixels, inner), f32),
            pltpu.VMEM((pixels, inner), bf16),
            pltpu.VMEM((reducer.half, TILE), f32),
            pltpu.VMEM((2, width, inner), bf16),
            pltpu.VMEM((2, 2, width, inner), bf16),
            pltpu.VMEM((4, size, 2, inner), f32),
            pltpu.VMEM((size, 2, channels), f32),
            pltpu.VMEM((2, 8, channels), f32),
            pltpu.VMEM((2, 2, inner), f32),
            pltpu.VMEM((2, channels), f32),
            pltpu.SemaphoreType.DMA((6, size)),
            pltpu.SemaphoreType.DMA((6, size)),
            pltpu.SemaphoreType.DMA((2, 2)),
            pltpu.SemaphoreType.DMA((2, 2)),
            pltpu.SemaphoreType.DMA((10,)),
            pltpu.SemaphoreType.DMA,
        ]
        + reducer.scratch(),
        compiler_params=pltpu.CompilerParams(
            collective_id=2, has_side_effects=True, vmem_limit_bytes=63 * 2**20
        ),
    )(u0, u1, merged, zc, za, zb, r1, wr, ws, we, igs, ibs, ogs, obs, rs, rc, hwg, hbg, info, sums)


def pixel_info(pixel_mask, starts):
    width = pixel_mask.shape[1]
    columns = jnp.arange(width, dtype=jnp.int32)
    crop = jnp.sum((columns[:, None] >= starts[None, :]).astype(jnp.int32), axis=1)
    outside = jnp.full((1,), -1, jnp.int32)
    left = jnp.concatenate([outside, crop[:-1]]) == crop
    right = jnp.concatenate([crop[1:], outside]) == crop
    lane = jnp.arange(128, dtype=jnp.int32)
    first = jnp.where(lane == 0, pixel_mask[:, :, None], 0)
    links = jnp.where(lane == 1, left[:, None].astype(jnp.int32), 0)
    links = links + jnp.where(lane == 2, right[:, None].astype(jnp.int32), 0)
    return (first + links[None]).astype(jnp.float32).reshape(-1, 128)


def finish_kernel(
    head_cols,
    expand_in,
    spatial_in,
    reduce_in,
    small_in,
    grad_in,
    expand,
    spatial,
    reduce,
    gains,
    biases,
    outer,
    outer_b,
    head_w,
    head_b,
    grad,
):
    expand[...] = expand_in[...].astype(jnp.float32)
    spatial[...] = spatial_in[...].astype(jnp.float32)
    reduce[...] = reduce_in[...].astype(jnp.float32)
    grad[...] = grad_in[...]

    @pl.when(pl.program_id(0) == 0)
    def _():
        small = small_in[...].astype(jnp.float32)
        across = outer.shape[1] // TILE
        for k in range(2):
            head_w[:, k * TILE : (k + 1) * TILE] = small[k * head_cols : (k + 1) * head_cols]
        row, cut = 2 * head_cols, head_cols // 2
        one, other = small[row : row + 1, :cut], small[row : row + 1, cut:head_cols]
        head_b[...] = jnp.where(lax.axis_index("section") == 0, one, other)
        row += 8
        gains[...] = small[row : row + 2]
        biases[...] = small[row + 2 : row + 4]
        for k in range(across):
            cols = slice(k * TILE, (k + 1) * TILE)
            outer[:, cols] = small[row + 4 + k : row + 5 + k]
            outer_b[:, cols] = small[row + 4 + across + k : row + 5 + across + k]


def finish(expand, spatial, reduce, small, grad, head_cols):
    steps = 2
    channels = expand.shape[1]

    def rows(x, kind):
        block = pl.BlockSpec((x.shape[0] // steps, x.shape[1]), lambda i: (i, 0))
        return block, jax.ShapeDtypeStruct(x.shape, kind)

    def whole(*shape):
        return pl.BlockSpec(shape, lambda i: (0, 0)), jax.ShapeDtypeStruct(shape, jnp.float32)

    ins = [rows(x, x.dtype)[0] for x in (expand, spatial, reduce)]
    ins += [pl.BlockSpec((128, TILE), lambda i: (0, 0)), rows(grad, grad.dtype)[0]]
    outs = [rows(x, jnp.float32) for x in (expand, spatial, reduce)]
    outs += [whole(2, TILE), whole(2, TILE), whole(1, channels), whole(1, channels)]
    outs += [whole(head_cols, 2 * TILE), whole(1, head_cols // 2), rows(grad, grad.dtype)]
    return pl.pallas_call(
        functools.partial(finish_kernel, head_cols),
        grid=(steps,),
        in_specs=ins,
        out_specs=[block for block, _ in outs],
        out_shape=[shape for _, shape in outs],
        compiler_params=pltpu.CompilerParams(vmem_limit_bytes=LIMIT),
    )(expand, spatial, reduce, small, grad)


def pick(array, index):
    return lax.dynamic_index_in_dim(array, index, 0, keepdims=False)


def local(
    canvases,
    crop_starts,
    pixel_mask,
    drop_bits,
    reduce_weight,
    spatial_weight,
    expand_weight,
    inner_gain,
    inner_bias,
    outer_gain,
    outer_bias,
    head_weight,
    head_bias,
    head_cotangent,
):
    section = lax.axis_index("section")
    first = section == 0
    rows, width, channels = canvases.shape[1:]
    head_cols = head_weight.shape[1]
    pixels = rows * width
    flat = canvases.reshape(pixels, channels)
    mask = pick(pixel_mask, section)
    info = pixel_info(mask, pick(crop_starts, section))
    heads, hwg, hbg, igs, ibs, ogs, obs, rs, rc, info, sums, merged, u1, zc, za, zb, r1, wr, ws, we = forward(
        flat,
        drop_bits,
        jnp.swapaxes(head_cotangent, 2, 3),
        reduce_weight[0],
        spatial_weight[0],
        expand_weight[0],
        inner_gain[0],
        inner_bias[0],
        outer_gain,
        outer_bias,
        head_weight.T,
        head_bias[None],
        info,
        mask.astype(jnp.float32),
    )
    grad, expand_total, spatial_total, reduce_total, small = backward(
        flat, u1, merged, zc, za, zb, r1, wr, ws, we, igs, ibs, ogs, obs, rs, rc, hwg, hbg, info, sums
    )
    expand, spatial, reduce, gains, biases, outer, outer_b, head_w, head_b, grad = finish(
        expand_total.reshape(TILE, channels),
        spatial_total.reshape(-1, TILE),
        reduce_total.reshape(channels, TILE),
        small.reshape(-1, TILE),
        grad,
        head_cols,
    )
    return (
        jnp.swapaxes(heads, 1, 2)[None],
        grad.reshape(1, rows, width, channels),
        reduce[None],
        spatial.reshape(1, -1, TILE, TILE),
        expand[None],
        gains[None],
        biases[None],
        outer,
        outer_b,
        head_w.T,
        head_b.reshape(-1),
    )


def solution(mesh):
    placed = (
        P("section", "dp", None, None),
        P(),
        P(None, "dp", None),
        P(None, "dp", None, None),
        P("section", None, None),
        P("section", None, None, None),
        P("section", None, None),
        P("section", None, None),
        P("section", None, None),
        P("section", None),
        P("section", None),
        P(),
        P(),
        P(None, "dp", None, None),
    )
    return jax.shard_map(
        local,
        mesh=mesh,
        in_specs=placed,
        out_specs=(
            P("section", "dp", None, None),
            P("section", "dp", None, None),
            P("section", None, None),
            P("section", None, None, None),
            P("section", None, None),
            P("section", None, None),
            P("section", None, None),
            P("section", None),
            P("section", None),
            P("section", None),
            P("section"),
        ),
        check_vma=False,
    )
```

```python
import functools
import math

import jax
import jax.numpy as jnp
from jax import lax
from jax.experimental import pallas as pl
from jax.experimental.pallas import tpu as pltpu
from jax.sharding import PartitionSpec as P

TASKS = 3
HEAD_OUT = 16

EPS = 1e-05
SOFT = 0.05
SHARP = 0.1
LEVELS = 1024.0
ACROSS = (((0,), (0,)), ((), ()))
BESIDE = (((1,), (1,)), ((), ()))
MESH = pl.DeviceIdType.MESH
TILE = 512
LIMIT = 56 * 2**20


def grid_of(size):
    side = math.isqrt(size // 4)
    assert side * side * 4 == size
    return (4, side, side)


class Reducer:
    PACE = 3
    BETWEEN = (7, 9, 6)

    def __init__(self, size, across, taps):
        self.size = size
        nz, ny, nx = grid_of(size)
        self.strides = {}
        for axis, count, stride in (("x", nx, 1), ("y", ny, nx), ("z", nz, nx * ny)):
            for level in range(count.bit_length() - 1):
                self.strides[axis + str(level)] = stride << level
        later = [bit for bit in self.strides if bit[1] != "0"]
        self.orders = [
            [[a + "0" for a in order] + later for order in ("xyz", "yxz", third)]
            for third in ("zxy", "zyx")
        ]
        self.levels = len(self.strides)
        self.row_bits = [bit for bit in self.strides if bit[0] != "x"]
        self.x_bits = [bit for bit in self.strides if bit[0] == "x"]
        self.shape = (2,) * len(self.row_bits) + (16, TILE)
        self.half = 16 << len(self.row_bits)
        self.lines = 2 * self.half
        self.per_tile = TILE // self.lines
        self.counts = [across * self.per_tile, taps * self.per_tile, across * self.per_tile + 1]
        self.real = sum(self.counts)
        self.stages = 2 * self.levels + 3
        self.lag = 5 if self.levels <= 4 else 2
        self.plan(across, taps)

    def plan(self, across, taps):
        tiles = (across, taps, across)
        whole = sum(tiles) + sum(self.BETWEEN)
        assert whole % self.PACE == 0
        self.bursts, written = [], []
        place = base = 0
        for block in range(2):
            clock = block * whole
            for burst in range(3):
                if block == 1 and burst == 2:
                    clock -= self.BETWEEN[1] - 1
                groups = -(-self.counts[burst] // 3)
                ready = []
                for group in range(groups):
                    last = min((3 * group + 2) // self.per_tile, tiles[burst] - 1)
                    ready.append(-(-(clock + last) // self.PACE) - group)
                place = max([place] + ready)
                self.bursts.append((place, groups, base, self.counts[burst]))
                for unit in range(self.counts[burst]):
                    written.append(clock + min(unit // self.per_tile, tiles[burst] - 1))
                place += groups
                base += self.counts[burst]
                clock += tiles[burst] + self.BETWEEN[burst]
        self.last = self.PACE * (place - 1)
        reduced = []
        for place, groups, _, count in self.bursts:
            for unit in range(count):
                reduced.append(self.PACE * (place + unit // 3) + self.lag * (self.levels + 1))
        self.slots = 1
        while any(
            reduced[unit] >= written[unit + self.slots] for unit in range(len(written) - self.slots)
        ):
            self.slots += 1

    def scratch(self):
        units, bf16 = 2 * self.real, jnp.bfloat16
        return [
            pltpu.VMEM((self.slots, 2) + self.shape, bf16),
            pltpu.VMEM((units,) + self.shape, bf16),
            pltpu.VMEM((units,) + self.shape, bf16),
            pltpu.SemaphoreType.DMA((units, 2)),
            pltpu.SemaphoreType.DMA((units, 2)),
            pltpu.SemaphoreType.DMA((units, 2 * self.levels)),
            pltpu.SemaphoreType.DMA((units, 2 * self.levels)),
        ]

    def totals(self, across, taps):
        tail = (self.per_tile, 2) + self.shape
        return [
            (self.per_tile, 2) + self.shape[:-1] + (across * TILE,),
            (taps,) + tail,
            (across,) + tail,
            (2,) + self.shape,
        ]

    def bind(self, total, scratch):
        self.total = total
        (
            self.ring,
            self.res,
            self.land,
            self.pair_send,
            self.pair_recv,
            self.send_sem,
            self.recv_sem,
        ) = scratch
        self.section, self.me = lax.axis_index("section"), lax.axis_index("dp")
        self.bit = {bit: (self.me // stride) % 2 for bit, stride in self.strides.items()}
        self.clock = 0

    def partner(self, bit):
        return (self.section, self.me + (1 - 2 * self.bit[bit]) * self.strides[bit])

    def slot(self, unit):
        if isinstance(unit, int):
            return unit % self.slots
        return lax.rem(unit, self.slots)

    def region(self, order, level, flip):
        place = {bit: self.bit[bit] for bit in order[:level]}
        if flip:
            place[order[level - 1]] = 1 - place[order[level - 1]]
        rows = tuple(place.get(bit, slice(None)) for bit in self.row_bits)
        cols, start, width = slice(None), 0, TILE
        for bit in self.x_bits:
            if bit in place:
                width //= 2
                start = start + place[bit] * width
                cols = pl.ds(pl.multiple_of(start, width), width)
        return rows + (slice(None), cols)

    def pair(self, unit):
        return pltpu.make_async_remote_copy(
            src_ref=self.ring.at[self.slot(unit), 1 - self.section],
            dst_ref=self.res.at[unit],
            send_sem=self.pair_send.at[unit, 1],
            recv_sem=self.pair_recv.at[unit, 0],
            device_id=(1 - self.section, self.me),
            device_id_type=MESH,
        )

    def acc(self, unit):
        return self.ring.at[self.slot(unit), self.section]

    def halve(self, unit, order, level):
        return pltpu.make_async_remote_copy(
            src_ref=self.acc(unit).at[self.region(order, level + 1, True)],
            dst_ref=self.land.at[(unit,) + self.region(order, level + 1, False)],
            send_sem=self.send_sem.at[unit, level],
            recv_sem=self.recv_sem.at[unit, level],
            device_id=self.partner(order[level]),
            device_id_type=MESH,
        )

    def halved(self, unit, order, level):
        self.halve(unit, order, level).wait()
        keep = self.region(order, level + 1, False)
        kept = self.acc(unit).at[keep]
        came = self.land.at[(unit,) + self.region(order, level + 1, True)]
        target = self.res.at[(unit,) + keep] if level == self.levels - 1 else kept
        total = kept[...].astype(jnp.float32) + came[...].astype(jnp.float32)
        target[...] = total.astype(jnp.bfloat16)

    def double(self, unit, order, level):
        ref = self.res.at[(unit,) + self.region(order, level + 1, False)]
        return pltpu.make_async_remote_copy(
            src_ref=ref,
            dst_ref=ref,
            send_sem=self.send_sem.at[unit, self.levels + level],
            recv_sem=self.recv_sem.at[unit, self.levels + level],
            device_id=self.partner(order[level]),
            device_id_type=MESH,
        )

    def places(self, index):
        expand, spatial, reduce, small = self.total
        tile, part = index // self.per_tile, index % self.per_tile
        across, taps = reduce.shape[0], spatial.shape[0]
        half = self.section
        inner = (slice(None),) * (len(self.shape) - 1)

        def in_expand():
            cols = tile * TILE if isinstance(tile, int) else pl.multiple_of(tile * TILE, TILE)
            return expand.at[(part, half) + inner + (pl.ds(cols, TILE),)]

        return [
            (0 <= tile < across if isinstance(tile, int) else tile < across, in_expand),
            (
                self.both(tile >= across, tile < across + taps),
                lambda: spatial.at[tile - across, part, half],
            ),
            (
                self.both(tile >= across + taps, index < self.real - 1),
                lambda: reduce.at[tile - across - taps, part, half],
            ),
            (index == self.real - 1, lambda: small.at[half]),
        ]

    @staticmethod
    def both(first, second):
        if isinstance(first, bool) and isinstance(second, bool):
            return first and second
        return jnp.logical_and(first, second)

    def final(self, unit, target):
        here = pltpu.make_async_copy(self.res.at[unit], target, self.pair_send.at[unit, 0])
        away = pltpu.make_async_remote_copy(
            src_ref=self.res.at[unit],
            dst_ref=target,
            send_sem=self.pair_send.at[unit, 0],
            recv_sem=self.pair_recv.at[unit, 1],
            device_id=(1 - self.section, self.me),
            device_id_type=MESH,
        )
        return here, away

    def owner(self, unit):
        if isinstance(unit, int):
            return self.section == 1 - unit // self.real, unit % self.real
        later = (unit >= self.real).astype(jnp.int32)
        return self.section == 1 - later, unit - later * self.real

    def finish(self, unit):
        mine, index = self.owner(unit)

        def send(place):
            pl.when(mine)(lambda: self.final(unit, place())[0].start())
            pl.when(jnp.logical_not(mine))(lambda: self.final(unit, place())[1].start())

        for wanted, place in self.places(index):
            if isinstance(wanted, bool):
                if wanted:
                    send(place)
            else:
                pl.when(wanted)(functools.partial(send, place))

    def finished(self, unit):
        mine, _ = self.owner(unit)
        here, away = self.final(unit, self.total[3].at[self.section])

        @pl.when(mine)
        def _():
            here.wait()
            away.wait_recv()

        pl.when(jnp.logical_not(mine))(away.wait_send)

    def step(self, number, unit, order):
        levels = self.levels
        if number == 0:
            self.pair(unit).start()
        elif number == 1:
            self.pair(unit).wait()
            acc = self.acc(unit)
            total = acc[...].astype(jnp.float32) + self.res[unit].astype(jnp.float32)
            acc[...] = total.astype(jnp.bfloat16)
            self.halve(unit, order, 0).start()
        elif number <= levels:
            self.halved(unit, order, number - 2)
            self.halve(unit, order, number - 1).start()
        elif number == levels + 1:
            self.halved(unit, order, levels - 1)
            self.double(unit, order, levels - 1).start()
        elif number <= 2 * levels:
            level = 2 * levels - number
            self.double(unit, order, level + 1).wait()
            self.double(unit, order, level).start()
        elif number == 2 * levels + 1:
            self.double(unit, order, 0).wait()
            self.finish(unit)
        else:
            self.finished(unit)

    def locate(self, group):
        for place, groups, base, count in self.bursts:
            at = group - place
            if 0 <= at < groups:
                return base + 3 * at, min(3, count - 3 * at)
        return None

    def tick(self, time):
        for number in reversed(range(self.stages)):
            when = time - self.lag * number
            if when % self.PACE:
                continue
            group = when // self.PACE
            place = self.locate(group)
            if place is not None:
                for slot in range(place[1]):
                    order = self.orders[group % 2][slot]
                    self.step(number, place[0] + slot, order)

    def pump(self, count=1):
        for _ in range(count):
            self.tick(self.clock)
            self.clock += 1

    def burst(self, number, tiles, put, extra=None):
        base = self.bursts[number][2]
        for tile in range(tiles):
            put(tile, base + tile * self.per_tile)
            if tile == tiles - 1 and extra is not None:
                extra(base + tiles * self.per_tile)
            self.pump()

    def drain(self):
        self.pump(self.last + self.lag * (self.stages - 1) + 1 - self.clock)


def sigmoid(v):
    return 0.5 + 0.5 * jnp.tanh(0.5 * v)


def silu_parts(v):
    sigma = sigmoid(v)
    return v * sigma, sigma * (1.0 + v * (1.0 - sigma))


def folded(x):
    return jnp.sum(x.reshape(x.shape[0] // 8, 8, x.shape[1]), axis=0)


class Exchange:
    def __init__(self, size, send_sem, recv_sem, edge_send, edge_recv):
        self.size = size
        self.section, self.me = lax.axis_index("section"), lax.axis_index("dp")
        self.send_sem, self.recv_sem = send_sem, recv_sem
        self.edge_send, self.edge_recv = edge_send, edge_recv

    def greet(self):
        barrier = pltpu.get_barrier_semaphore()
        for step in range(1, self.size):
            peer = (self.section, lax.rem(self.me + step, self.size))
            pl.semaphore_signal(barrier, inc=1, device_id=peer, device_id_type=MESH)
        other = (1 - self.section, self.me)
        pl.semaphore_signal(barrier, inc=1, device_id=other, device_id_type=MESH)

    def met(self):
        pl.semaphore_wait(pltpu.get_barrier_semaphore(), self.size)

    def copies(self, number, slots):
        return [
            pltpu.make_async_remote_copy(
                src_ref=slots.at[0],
                dst_ref=slots.at[step],
                send_sem=self.send_sem.at[number, step],
                recv_sem=self.recv_sem.at[number, step],
                device_id=(self.section, lax.rem(self.me + step, self.size)),
                device_id_type=MESH,
            )
            for step in range(1, self.size)
        ]

    def edges(self, number, first, last, landing):
        made = []
        for way, (ref, step) in enumerate(((first, self.size - 1), (last, 1))):
            made.append(
                pltpu.make_async_remote_copy(
                    src_ref=ref,
                    dst_ref=landing.at[1 - way],
                    send_sem=self.edge_send.at[number, way],
                    recv_sem=self.edge_recv.at[number, 1 - way],
                    device_id=(self.section, lax.rem(self.me + step, self.size)),
                    device_id_type=MESH,
                )
            )
        return made

    def start_edges(self, number, first, last, landing):
        up, down = self.edges(number, first, last, landing)
        pl.when(self.me > 0)(up.start)
        pl.when(self.me < self.size - 1)(down.start)

    def wait_edges(self, number, first, last, landing):
        up, down = self.edges(number, first, last, landing)
        pl.when(self.me > 0)(up.wait_send)
        pl.when(self.me > 0)(down.wait_recv)
        pl.when(self.me < self.size - 1)(down.wait_send)
        pl.when(self.me < self.size - 1)(up.wait_recv)


def forward_kernel(
    size,
    u_hbm,
    bits_hbm,
    cot_hbm,
    wr_hbm,
    ws_hbm,
    we_hbm,
    ig_ref,
    ib_ref,
    og_ref,
    ob_ref,
    hwt_ref,
    hb_ref,
    info_ref,
    mask_ref,
    heads_ref,
    hwg_ref,
    hbg_ref,
    igs,
    ibs,
    ogs,
    obs,
    rs_ref,
    rc_ref,
    info_out,
    sums_out,
    merged_hbm,
    u1_hbm,
    zc_hbm,
    za_hbm,
    zb_hbm,
    r1_hbm,
    wr_all,
    ws_all,
    we_all,
    wr,
    ws,
    we,
    u0,
    u1,
    a_ref,
    b_ref,
    e_ref,
    cat,
    r2,
    za,
    zb,
    zc,
    merged,
    bits,
    cot,
    edge,
    halo,
    live_halo,
    msg,
    msg_c,
    first_msg,
    stat,
    stat_c,
    part_sum,
    send_sem,
    recv_sem,
    edge_send,
    edge_recv,
    w_load,
    w_send,
    w_recv,
    w_out,
    in_sem,
    bit_sem,
    out_sem,
):
    link = Exchange(size, send_sem, recv_sem, edge_send, edge_recv)
    section, me = link.section, link.me
    pixels, channels = u0.shape
    inner = a_ref.shape[1]
    half = channels // 2
    rows, width = bits_hbm.shape[1], bits_hbm.shape[2]
    f32, bf16 = jnp.float32, jnp.bfloat16

    load_u = pltpu.make_async_copy(u_hbm, u0, in_sem.at[0])
    load_cot = pltpu.make_async_copy(cot_hbm.at[section], cot, in_sem.at[1])

    def load_bits(chunk):
        return pltpu.make_async_copy(
            bits_hbm.at[section, chunk], bits.at[chunk % 2], bit_sem.at[chunk % 2]
        )

    link.greet()
    load_u.start()
    load_cot.start()
    load_bits(0).start()
    load_bits(1).start()

    weights = ((wr_hbm, wr, wr_all), (ws_hbm, ws, ws_all), (we_hbm, we, we_all))

    def local_load(kind):
        source, target, _ = weights[kind]
        return pltpu.make_async_copy(source, target.at[section], w_load.at[kind])

    def pushed(kind):
        source, target, _ = weights[kind]
        return pltpu.make_async_remote_copy(
            src_ref=source,
            dst_ref=target.at[section],
            send_sem=w_send.at[kind],
            recv_sem=w_recv.at[kind],
            device_id=(1 - section, me),
            device_id_type=MESH,
        )

    vectors = ((ig_ref, igs), (ib_ref, ibs), (og_ref, ogs), (ob_ref, obs))

    def pushed_vector(kind):
        source, target = vectors[kind]
        return pltpu.make_async_remote_copy(
            src_ref=source,
            dst_ref=target.at[section],
            send_sem=w_send.at[3 + kind],
            recv_sem=w_recv.at[3 + kind],
            device_id=(1 - section, me),
            device_id_type=MESH,
        )

    def save_weight(kind, layer):
        _, target, saved = weights[kind]
        return pltpu.make_async_copy(target.at[layer], saved.at[layer], w_out.at[kind, layer])

    for kind in range(3):
        local_load(kind).start()
    link.met()
    for kind in range(4):
        pushed_vector(kind).start()
    for kind in range(3):
        pushed(kind).start()
    for source, target in vectors:
        target[section] = source[...]

    def need_weight(kind, layer):
        pl.when(section == layer)(local_load(kind).wait)
        pl.when(section != layer)(pushed(kind).wait_recv)
        save_weight(kind, layer).start()

    own = pl.ds(width, pixels)
    live_edges = (info_ref.at[pl.ds(0, width)], info_ref.at[pl.ds(pixels - width, width)])

    def drop_chunk(chunk):
        load_bits(chunk).wait()
        start = pl.multiple_of(chunk * width, 16)
        target = cot[chunk].astype(f32) * mask_ref[chunk : chunk + 1]
        task = lax.broadcasted_iota(jnp.int32, target.shape, 0) // HEAD_OUT
        parts = [jnp.where(task == k, target, 0.0).astype(bf16) for k in range(TASKS)]

        @pl.loop(0, channels // TILE)
        def _(tile):
            cols = pl.ds(pl.multiple_of(tile * TILE, TILE), TILE)
            table = hwt_ref[:, cols]
            signed = magnitude = weighted = None
            for part in parts:
                value = lax.dot_general(part, table, ACROSS, preferred_element_type=f32)
                square = value * value
                whole = square + SOFT * SOFT
                inverse = lax.rsqrt(whole)
                if signed is None:
                    signed, magnitude, weighted = value, whole * inverse, square * inverse
                else:
                    signed = signed + value
                    magnitude = magnitude + whole * inverse
                    weighted = weighted + square * inverse
            level = bits[chunk % 2, :, cols].astype(f32)
            reach = 0.25 / SHARP
            inside = reach * (signed / magnitude) + (
                reach * (1.0 - 1.0 / LEVELS) - (2.0 * reach / LEVELS) * level
            )
            value = 0.5 * signed + (0.5 * jnp.tanh(inside)) * weighted
            merged[pl.ds(start, width), cols] = value.astype(bf16)

        if chunk + 2 < rows:
            load_bits(chunk + 2).start()

    live_all = info_ref[:, 0:1]
    count_here = jnp.sum(live_all, axis=0, keepdims=True)
    share = 1.0 / count_here

    def column_stats(values):
        mean = jnp.sum(values * live_all, axis=0, keepdims=True) * share
        apart = values - mean
        return mean, jnp.sum(live_all * apart * apart, axis=0, keepdims=True)

    def counts(step):
        return first_msg[step, 2:3, 0:1]

    def combine(slots):
        number = counts(0)
        mean = slots[0, 0:1] * counts(0)
        spread = slots[0, 1:2]
        for step in range(1, size):
            number = number + counts(step)
            mean = mean + slots[step, 0:1] * counts(step)
            spread = spread + slots[step, 1:2]
        mean = mean / number
        for step in range(size):
            apart = slots[step, 0:1] - mean
            spread = spread + counts(step) * apart * apart
        return mean, lax.rsqrt(spread / number + EPS), number

    load_u.wait()
    load_cot.wait()
    first_msg[0, 2:3] = jnp.broadcast_to(count_here, (1, inner))
    first_msg[0, 3:4] = jnp.zeros((1, inner), f32)
    zc_out = za_out = zb_out = r1_out = None
    u1_out = pltpu.make_async_copy(u1, u1_hbm, out_sem.at[0])
    for layer in range(2):
        x_ref = (u0, u1)[layer]
        need_weight(0, layer)
        slots = first_msg if layer == 0 else msg.at[0]

        @pl.loop(0, inner // 256)
        def _(tile):
            cols = pl.ds(pl.multiple_of(tile * 256, 256), 256)
            values = jnp.dot(x_ref[...], wr[layer, :, cols], preferred_element_type=f32)
            a_ref[:, cols] = values
            mean, spread = column_stats(values)
            slots[0, 0:1, cols] = mean
            slots[0, 1:2, cols] = spread

        if layer == 1:
            for copy in (za_out, zb_out, r1_out, zc_out):
                copy.wait()
            u1_out.start()
        sends = link.copies(3 * layer, slots)
        for copy in sends:
            copy.start()
        centre = slots[0, 0:1]
        edge[0] = (a_ref[0:width] - centre).astype(bf16)
        edge[1] = (a_ref[pixels - width : pixels] - centre).astype(bf16)
        a_edges = (edge.at[0], edge.at[1])
        a_halo = halo.at[2 * layer]
        link.start_edges(2 * layer, *a_edges, a_halo)
        if layer == 0:
            link.start_edges(4, *live_edges, live_halo)
            for kind in range(4):
                pushed_vector(kind).wait()
        if layer == 0:
            drop_chunk(0)
        drop_chunk(1 + 3 * layer)
        for copy in sends:
            copy.wait()
        mean, inverse, number = combine(slots)
        stat[layer, 0:1], stat[layer, 1:2] = mean, inverse
        rs_ref[layer, 0:1] = inverse
        rs_ref[layer, 2:3] = jnp.broadcast_to(number, (1, inner))

        def first_act(row, values, inside):
            normed = (values - stat[layer, 0:1]) * stat[layer, 1:2]
            affine = normed * igs[layer, 0:1] + ibs[layer, 0:1]
            act = affine * sigmoid(affine)
            if inside is not None:
                act = jnp.where(inside, act, 0.0)
            here = pl.ds(pl.multiple_of(row * width, 16), width)
            masks = info_ref[0:width]
            cat[here, 0:inner] = (pltpu.roll(act, 1, 0) * masks[:, 1:2]).astype(bf16)
            cat[here, inner : 2 * inner] = act.astype(bf16)
            cat[here, 2 * inner : 3 * inner] = (
                pltpu.roll(act, width - 1, 0) * masks[:, 2:3]
            ).astype(bf16)
            return normed

        @pl.loop(0, rows)
        def _(row):
            here = pl.ds(pl.multiple_of(row * width, 16), width)
            za[here] = first_act(row + 1, a_ref[here], None).astype(bf16)

        link.wait_edges(2 * layer, *a_edges, a_halo)
        first_act(0, a_halo[0].astype(f32) + slots[1, 0:1], me > 0)
        first_act(rows + 1, a_halo[1].astype(f32) + slots[size - 1, 0:1], me < size - 1)

        za_out = pltpu.make_async_copy(za, za_hbm.at[layer], out_sem.at[1])
        r1_out = pltpu.make_async_copy(
            cat.at[:, pl.ds(inner, inner)], r1_hbm.at[layer], out_sem.at[2]
        )
        za_out.start()
        r1_out.start()
        need_weight(1, layer)
        slots = msg.at[1 + 2 * layer]

        @pl.loop(0, inner // 256)
        def _(tile):
            cols = pl.ds(pl.multiple_of(tile * 256, 256), 256)
            values = None
            for tap in range(3):
                table = ws[layer, 3 * tap : 3 * tap + 3, :, cols].reshape(3 * inner, 256)
                value = jnp.dot(
                    cat[tap * width : tap * width + pixels], table, preferred_element_type=f32
                )
                values = value if values is None else values + value
            b_ref[:, cols] = values
            mean, spread = column_stats(values)
            slots[0, 0:1, cols] = mean
            slots[0, 1:2, cols] = spread

        sends = link.copies(3 * layer + 1, slots)
        for copy in sends:
            copy.start()
        drop_chunk(2 + 3 * layer)
        for copy in sends:
            copy.wait()
        mean, inverse, _ = combine(slots)
        stat[layer, 2:3], stat[layer, 3:4] = mean, inverse
        rs_ref[layer, 1:2] = inverse

        @pl.loop(0, rows)
        def _(row):
            here = pl.ds(pl.multiple_of(row * width, 16), width)
            normed = (b_ref[here] - stat[layer, 2:3]) * stat[layer, 3:4]
            zb[pl.ds(pl.multiple_of((row + 1) * width, 16), width)] = normed.astype(bf16)
            affine = normed * igs[layer, 1:2] + ibs[layer, 1:2]
            r2[here] = (affine * sigmoid(affine)).astype(bf16)

        b_edges = (zb.at[pl.ds(width, width)], zb.at[pl.ds(pixels, width)])
        b_halo = halo.at[2 * layer + 1]
        link.start_edges(2 * layer + 1, *b_edges, b_halo)
        need_weight(2, layer)
        sends = []
        for side in range(2):
            slots = msg_c.at[layer, side]

            @pl.loop(0, half // 256)
            def _(tile):
                cols = pl.ds(pl.multiple_of(side * half + tile * 256, 256), 256)
                at = pl.ds(pl.multiple_of(tile * 256, 256), 256)
                values = jnp.dot(r2[...], we[layer, :, cols], preferred_element_type=f32)
                e_ref[:, cols] = values
                mean, spread = column_stats(values)
                slots[0, 0:1, at] = mean
                slots[0, 1:2, at] = spread

            sends += link.copies((2 if side == 0 else 7) + 3 * layer, slots)
            for copy in sends[-(size - 1) :]:
                copy.start()
        drop_chunk(3 + 3 * layer)
        if layer == 0:
            link.wait_edges(4, *live_edges, live_halo)
            info_out[own] = info_ref[...]
            info_out[0:width] = live_halo[0]
            info_out[pixels + width : pixels + 2 * width] = live_halo[1]
        if layer == 1:
            drop_chunk(7)
        link.wait_edges(2 * layer + 1, *b_edges, b_halo)
        for side, row in ((0, 0), (1, rows + 1)):
            zb[row * width : (row + 1) * width] = b_halo[side]
        zb_out = pltpu.make_async_copy(zb, zb_hbm.at[layer], out_sem.at[3])
        zb_out.start()
        for copy in sends:
            copy.wait()
        for side in range(2):
            cols = slice(side * half, (side + 1) * half)
            mean, inverse, _ = combine(msg_c.at[layer, side])
            stat_c[0:1, cols], stat_c[1:2, cols] = mean, inverse
            rc_ref[layer, :, cols] = inverse
        out_ref = (u1, u0)[layer]
        if layer == 1:
            part_sum[...] = jnp.zeros_like(part_sum)

        def last_act(chunk):
            tile, row = chunk // rows, chunk % rows
            here = pl.ds(pl.multiple_of(row * width, 16), width)
            cols = pl.ds(pl.multiple_of(tile * TILE, TILE), TILE)
            normed = (e_ref[here, cols] - stat_c[0:1, cols]) * stat_c[1:2, cols]
            zc[here, cols] = normed.astype(bf16)
            total = normed * ogs[layer, :, cols] + obs[layer, :, cols] + x_ref[here, cols].astype(f32)
            if layer == 0:
                out_ref[here, cols] = (total * sigmoid(total)).astype(bf16)
            else:
                act, slope = silu_parts(total)
                out_ref[here, cols] = act.astype(bf16)
                dt = merged[here, cols].astype(f32) * slope
                merged[here, cols] = dt.astype(bf16)
                part_sum[0, :, cols] += folded(dt)
                part_sum[1, :, cols] += folded(dt * normed)

        turns = rows * (channels // TILE)
        if layer == 0:
            pl.loop(0, turns)(last_act)
        else:
            sends = []
            for side in range(2):
                pl.loop(side * (turns // 2), (side + 1) * (turns // 2))(last_act)
                slots = msg_c.at[2, side]
                cols = slice(side * half, (side + 1) * half)
                slots[0, 0:1] = jnp.sum(part_sum[0, :, cols], axis=0, keepdims=True)
                slots[0, 1:2] = jnp.sum(part_sum[1, :, cols], axis=0, keepdims=True)
                sends += link.copies((6, 8)[side], slots)
                for copy in sends[-(size - 1) :]:
                    copy.start()
        zc_out = pltpu.make_async_copy(zc, zc_hbm.at[layer], out_sem.at[5])
        zc_out.start()

    pltpu.make_async_copy(merged, merged_hbm, out_sem.at[4]).start()

    bias_sum = None
    for row in range(rows):
        lines = pl.ds(row * width, width)
        heads_ref[row] = (
            lax.dot_general(hwt_ref[...], u0[lines], BESIDE, preferred_element_type=f32)
            + hb_ref[...].T
        )
        target = cot[row].astype(f32) * mask_ref[row : row + 1]
        lanes = jnp.sum(target, axis=1, keepdims=True)
        bias_sum = lanes if bias_sum is None else bias_sum + lanes
        part = jnp.dot(target.astype(bf16), u0[lines], preferred_element_type=f32)
        if row == 0:
            hwg_ref[...] = part
        else:
            hwg_ref[...] += part
    hbg_ref[...] = bias_sum

    for copy in sends:
        copy.wait()
    for side in range(2):
        found = msg_c[2, side, 0]
        for step in range(1, size):
            found = found + msg_c[2, side, step]
        sums_out[:, side * half : (side + 1) * half] = found
    for copy in (za_out, zb_out, r1_out, zc_out, u1_out):
        copy.wait()
    pltpu.make_async_copy(merged, merged_hbm, out_sem.at[4]).wait()
    for kind in range(3):
        pushed(kind).wait_send()
        for layer in range(2):
            save_weight(kind, layer).wait()


def forward(u, bits, cot, wr, ws, we, ig, ib, og, ob, hwt, hb, info, mask):
    size = lax.axis_size("dp")
    pixels, channels = u.shape
    inner = wr.shape[1]
    _, rows, head_cols, width = cot.shape
    f32, bf16 = jnp.float32, jnp.bfloat16
    padded = pixels + 2 * width
    anywhere = pl.BlockSpec(memory_space=pl.ANY)
    vmem = pl.BlockSpec(memory_space=pltpu.VMEM)

    def out(kind, *shape):
        return jax.ShapeDtypeStruct(shape, kind)

    return pl.pallas_call(
        functools.partial(forward_kernel, size),
        out_shape=[
            out(f32, rows, head_cols, width),
            out(f32, head_cols, channels),
            out(f32, head_cols, 1),
            out(f32, 2, 2, inner),
            out(f32, 2, 2, inner),
            out(f32, 2, 1, channels),
            out(f32, 2, 1, channels),
            out(f32, 2, 8, inner),
            out(f32, 2, 1, channels),
            out(f32, padded, 128),
            out(f32, 2, channels),
            out(bf16, pixels, channels),
            out(bf16, pixels, channels),
            out(bf16, 2, pixels, channels),
            out(bf16, 2, pixels, inner),
            out(bf16, 2, padded, inner),
            out(bf16, 2, padded, inner),
            out(bf16, 2, channels, inner),
            out(bf16, 2, 9, inner, inner),
            out(bf16, 2, inner, channels),
        ],
        in_specs=[anywhere] * 6 + [vmem] * 8,
        out_specs=[vmem] * 11 + [anywhere] * 9,
        scratch_shapes=[
            pltpu.VMEM((2, channels, inner), bf16),
            pltpu.VMEM((2, 9, inner, inner), bf16),
            pltpu.VMEM((2, inner, channels), bf16),
            pltpu.VMEM((pixels, channels), bf16),
            pltpu.VMEM((pixels, channels), bf16),
            pltpu.VMEM((pixels, inner), f32),
            pltpu.VMEM((pixels, inner), f32),
            pltpu.VMEM((pixels, channels), f32),
            pltpu.VMEM((padded, 3 * inner), bf16),
            pltpu.VMEM((pixels, inner), bf16),
            pltpu.VMEM((pixels, inner), bf16),
            pltpu.VMEM((padded, inner), bf16),
            pltpu.VMEM((pixels, channels), bf16),
            pltpu.VMEM((pixels, channels), bf16),
            pltpu.VMEM((2, width, channels), jnp.int32),
            pltpu.VMEM((rows, head_cols, width), bf16),
            pltpu.VMEM((2, width, inner), bf16),
            pltpu.VMEM((4, 2, width, inner), bf16),
            pltpu.VMEM((2, width, 128), f32),
            pltpu.VMEM((4, size, 2, inner), f32),
            pltpu.VMEM((3, 2, size, 2, channels // 2), f32),
            pltpu.VMEM((size, 4, inner), f32),
            pltpu.VMEM((2, 8, inner), f32),
            pltpu.VMEM((2, channels), f32),
            pltpu.VMEM((2, 8, channels), f32),
            pltpu.SemaphoreType.DMA((11, size)),
            pltpu.SemaphoreType.DMA((11, size)),
            pltpu.SemaphoreType.DMA((5, 2)),
            pltpu.SemaphoreType.DMA((5, 2)),
            pltpu.SemaphoreType.DMA((3,)),
            pltpu.SemaphoreType.DMA((7,)),
            pltpu.SemaphoreType.DMA((7,)),
            pltpu.SemaphoreType.DMA((3, 2)),
            pltpu.SemaphoreType.DMA((2,)),
            pltpu.SemaphoreType.DMA((2,)),
            pltpu.SemaphoreType.DMA((6,)),
        ],
        compiler_params=pltpu.CompilerParams(
            collective_id=1, has_side_effects=True, vmem_limit_bytes=LIMIT
        ),
    )(u, bits, cot, wr, ws, we, ig, ib, og, ob, hwt, hb, info, mask)


def backward_kernel(
    size,
    reducer,
    u0_hbm,
    u1_hbm,
    merged_hbm,
    zc_hbm,
    za_hbm,
    zb_hbm,
    r1_hbm,
    wr_all,
    ws_all,
    we_all,
    igs,
    ibs,
    ogs,
    obs,
    rs_ref,
    rc_ref,
    hwg_ref,
    hbg_ref,
    info_ref,
    sums_ref,
    grad_hbm,
    expand_hbm,
    spatial_hbm,
    reduce_hbm,
    small_hbm,
    wr,
    ws,
    we,
    u_ref,
    d_ref,
    zc,
    za,
    zb,
    r1,
    r2,
    wide,
    dz_ref,
    da,
    small,
    edge,
    halo,
    msg,
    msg_c,
    part_sum,
    sums,
    sums_c,
    send_sem,
    recv_sem,
    edge_send,
    edge_recv,
    in_sem,
    out_sem,
    *scratch,
):
    reducer.bind((expand_hbm, spatial_hbm, reduce_hbm, small_hbm), scratch)
    link = Exchange(size, send_sem, recv_sem, edge_send, edge_recv)
    section, me = link.section, link.me
    pixels, channels = d_ref.shape
    inner = da.shape[1]
    width = halo.shape[2]
    rows = pixels // width
    across = channels // TILE
    f32, bf16 = jnp.float32, jnp.bfloat16
    own = pl.ds(width, pixels)
    de, cat = wide.at[pl.ds(0, pixels)], wide.at[:, pl.ds(0, 3 * inner)]

    def loads(layer):
        return {
            "zc": pltpu.make_async_copy(zc_hbm.at[layer], zc, in_sem.at[0]),
            "za": pltpu.make_async_copy(za_hbm.at[layer], za, in_sem.at[1]),
            "zb": pltpu.make_async_copy(zb_hbm.at[layer], zb, in_sem.at[2]),
            "r1": pltpu.make_async_copy(r1_hbm.at[layer], r1, in_sem.at[3]),
            "wr": pltpu.make_async_copy(wr_all.at[layer], wr, in_sem.at[4]),
            "ws": pltpu.make_async_copy(ws_all.at[layer], ws, in_sem.at[5]),
            "we": pltpu.make_async_copy(we_all.at[layer], we, in_sem.at[6]),
            "u": pltpu.make_async_copy((u0_hbm, u1_hbm)[layer], u_ref.at[layer], in_sem.at[7 + layer]),
        }

    load_d = pltpu.make_async_copy(merged_hbm, d_ref, in_sem.at[9])
    first, second = loads(1), loads(0)
    load_d.start()
    for name in ("zc", "we", "zb", "ws", "za", "r1", "wr", "u"):
        first[name].start()
    second["u"].start()
    link.greet()
    live_all = info_ref[own, 0:1]

    def put_tile(unit, make):
        @pl.loop(0, 2)
        def _(side):
            cols = pl.ds(pl.multiple_of(side * 256, 256), 256)
            value = make(side).astype(bf16)
            inside = (slice(None),) * len(reducer.shape)
            for part in range(reducer.per_tile):
                lines = value[part * reducer.lines : (part + 1) * reducer.lines]
                at = (reducer.slot(unit + part),) + inside + (cols,)
                reducer.ring[at] = lines.reshape((2,) + reducer.shape[:-1] + (256,))

    def column_sums(values):
        return jnp.sum(values, axis=0, keepdims=True)

    def total_of(slots):
        found = slots[0]
        for step in range(1, size):
            found = found + slots[step]
        return found

    def expand_tiles(layer):
        def put(tile, unit):
            def make(side):
                cols = pl.ds(pl.multiple_of(tile * TILE + side * 256, 256), 256)
                return lax.dot_general(r2[...], de[:, cols], ACROSS, preferred_element_type=f32)

            put_tile(unit, make)

        reducer.burst(3 * (1 - layer), across, put)

    def spatial_tiles(layer):
        def put(tap, unit):
            shift, side_step = tap // 3, tap % 3

            def make(side):
                at = pl.ds(pl.multiple_of(shift * width, 16), pixels)
                cols = pl.ds(pl.multiple_of(side_step * inner + side * 256, 256), 256)
                return lax.dot_general(r1[at], cat[own, cols], ACROSS, preferred_element_type=f32)

            put_tile(unit, make)

        reducer.burst(3 * (1 - layer) + 1, 9, put)

    def reduce_tiles(layer):
        def put(tile, unit):
            def make(side):
                cols = pl.ds(pl.multiple_of(side * 256, 256), 256)
                lines = pl.ds(pl.multiple_of(tile * TILE, TILE), TILE)
                return lax.dot_general(
                    u_ref[layer, :, lines], da[:, cols], ACROSS, preferred_element_type=f32
                )

            put_tile(unit, make)

        reducer.burst(3 * (1 - layer) + 2, across, put, functools.partial(small_unit, layer))

    def small_unit(layer, unit):
        half = channels // 2
        head_cols = hwg_ref.shape[0]
        small[...] = jnp.zeros_like(small)
        for k in range(2):
            at = layer * half + k * TILE
            small[k * head_cols : (k + 1) * head_cols] = hwg_ref[:, at : at + TILE]
        row = 2 * head_cols
        small[row : row + 1, 0:head_cols] = hbg_ref[...].T
        only = (me == 0).astype(f32)
        small[row + 8 : row + 9] = sums[0, 1:2] * only
        small[row + 9 : row + 10] = sums[1, 1:2] * only
        small[row + 10 : row + 11] = sums[0, 0:1] * only
        small[row + 11 : row + 12] = sums[1, 0:1] * only
        for k in range(across):
            cols = slice(k * TILE, (k + 1) * TILE)
            small[row + 12 + k : row + 13 + k] = sums_c[1:2, cols] * only
            small[row + 12 + across + k : row + 13 + across + k] = sums_c[0:1, cols] * only
        slot = reducer.slot(unit)
        blank = jnp.zeros(reducer.shape, bf16)
        reducer.ring[slot, 0] = small[0 : reducer.half].astype(bf16).reshape(reducer.shape)
        reducer.ring[slot, 1] = blank

    load_d.wait()
    for layer in (1, 0):
        now = (second, first)[layer]
        now["zc"].wait()
        if layer == 0:
            now["u"].wait()
            first["u"].wait()
        if layer == 0:
            part_sum[...] = jnp.zeros_like(part_sum)

        def dt_chunk(chunk):
            tile, row = chunk // rows, chunk % rows
            here = pl.ds(pl.multiple_of(row * width, 16), width)
            cols = pl.ds(pl.multiple_of(tile * TILE, TILE), TILE)
            normed = zc[here, cols].astype(f32)
            total = (
                normed * ogs[layer, :, cols]
                + obs[layer, :, cols]
                + u_ref[layer, here, cols].astype(f32)
            )
            _, slope = silu_parts(total)
            dt = d_ref[here, cols].astype(f32) * slope
            d_ref[here, cols] = dt.astype(bf16)
            part_sum[0, :, cols] += folded(dt)
            part_sum[1, :, cols] += folded(dt * normed)

        if layer == 1:
            sums_c[...] = sums_ref[...]
        else:
            sends = []
            for part in range(4):
                pl.loop(part * (rows * across // 4), (part + 1) * (rows * across // 4))(dt_chunk)
                if part % 2 == 1:
                    slots = msg_c.at[part // 2]
                    cols = slice(part // 2 * (channels // 2), (part // 2 + 1) * (channels // 2))
                    slots[0, 0:1] = column_sums(part_sum[0, :, cols])
                    slots[0, 1:2] = column_sums(part_sum[1, :, cols])
                    sends += link.copies((0, 3)[part // 2], slots)
                    for copy in sends[-(size - 1) :]:
                        copy.start()
                reducer.pump()
            reduce_tiles(1)
            for copy in sends:
                copy.wait()
            for side in range(2):
                cols = slice(side * (channels // 2), (side + 1) * (channels // 2))
                sums_c[:, cols] = total_of(msg_c.at[side])
        number = rs_ref[layer, 2:3, 0:1]
        share = 1.0 / number

        def de_chunk(chunk):
            row, tile = chunk // across, chunk % across
            here = pl.ds(pl.multiple_of(row * width, 16), width)
            cols = pl.ds(pl.multiple_of(tile * TILE, TILE), TILE)
            live = info_ref[pl.ds(pl.multiple_of((row + 1) * width, 16), width), 0:1]
            normed = zc[here, cols].astype(f32)
            away = (sums_c[0:1, cols] + normed * sums_c[1:2, cols]) * share
            scale = rc_ref[layer, :, cols] * ogs[layer, :, cols]
            value = scale * (d_ref[here, cols].astype(f32) - live * away)
            de[here, cols] = value.astype(bf16)

        for part in range(4):
            pl.loop(part * (rows * across // 4), (part + 1) * (rows * across // 4))(de_chunk)
            if layer == 0:
                reducer.pump()
        now["we"].wait()
        now["zb"].wait()
        slots = msg.at[2 * layer]

        for tile in range(inner // 256):
            cols = pl.ds(tile * 256, 256)
            dr2 = lax.dot_general(de[...], we[cols], BESIDE, preferred_element_type=f32)
            normed = zb[own, cols].astype(f32)
            act, slope = silu_parts(normed * igs[layer, 1:2, cols] + ibs[layer, 1:2, cols])
            r2[:, cols] = act.astype(bf16)
            dz = dr2 * slope
            dz_ref[:, cols] = dz
            slots[0, 0:1, cols] = column_sums(dz)
            slots[0, 1:2, cols] = column_sums(dz * normed)
            if layer == 0:
                reducer.pump()

        if layer == 1:
            link.met()
        sends = link.copies(3 * layer + 1, slots)
        for copy in sends:
            copy.start()
        edge[0] = dz_ref[0:width].astype(bf16)
        edge[1] = dz_ref[pixels - width : pixels].astype(bf16)
        edges = (edge.at[0], edge.at[1])
        landing = halo.at[layer]
        link.start_edges(layer, *edges, landing)
        if layer == 1:
            second["zc"].start()
            second["we"].start()
        expand_tiles(layer)
        for copy in sends:
            copy.wait()
        sums[1] = total_of(slots)

        def db_row(row, dz, inside):
            here = pl.ds(pl.multiple_of(row * width, 16), width)
            live = info_ref[here, 0:1]
            normed = zb[here].astype(f32)
            away = (sums[1, 0:1] + normed * sums[1, 1:2]) * share
            value = (rs_ref[layer, 1:2] * igs[layer, 1:2]) * (dz - live * away)
            if inside is not None:
                value = jnp.where(inside, value, 0.0)
            masks = info_ref[pl.ds(width, width), :]
            cat[here, 0:inner] = (pltpu.roll(value, width - 1, 0) * masks[:, 2:3]).astype(bf16)
            cat[here, inner : 2 * inner] = value.astype(bf16)
            cat[here, 2 * inner : 3 * inner] = (
                pltpu.roll(value, 1, 0) * masks[:, 1:2]
            ).astype(bf16)

        def own_db(row):
            db_row(row + 1, dz_ref[pl.ds(pl.multiple_of(row * width, 16), width)], None)

        pl.loop(0, rows // 2)(own_db)
        reducer.pump()
        pl.loop(rows // 2, rows)(own_db)
        reducer.pump()

        link.wait_edges(layer, *edges, landing)
        db_row(0, landing[0].astype(f32), me > 0)
        db_row(rows + 1, landing[1].astype(f32), me < size - 1)
        reducer.pump()

        if layer == 1:
            second["zb"].start()
        now["ws"].wait()
        now["za"].wait()
        slots = msg.at[2 * layer + 1]

        for tile in range(inner // 256):
            cols = pl.ds(tile * 256, 256)
            dr1 = None
            for tap in range(9):
                start = (2 - tap // 3) * width
                block = cat[start : start + pixels, (tap % 3) * inner : (tap % 3 + 1) * inner]
                value = lax.dot_general(block, ws[tap, cols], BESIDE, preferred_element_type=f32)
                dr1 = value if dr1 is None else dr1 + value
                if tap == 4:
                    reducer.pump()
            normed = za[:, cols].astype(f32)
            _, slope = silu_parts(normed * igs[layer, 0:1, cols] + ibs[layer, 0:1, cols])
            dz = dr1 * slope
            dz_ref[:, cols] = dz
            slots[0, 0:1, cols] = column_sums(dz)
            slots[0, 1:2, cols] = column_sums(dz * normed)
            reducer.pump()

        sends = link.copies(3 * layer + 2, slots)
        for copy in sends:
            copy.start()
        if layer == 1:
            second["ws"].start()
        now["r1"].wait()
        spatial_tiles(layer)
        for copy in sends:
            copy.wait()
        sums[0] = total_of(slots)
        if layer == 1:
            second["r1"].start()

        @pl.loop(0, rows)
        def _(row):
            here = pl.ds(pl.multiple_of(row * width, 16), width)
            live = info_ref[pl.ds(pl.multiple_of((row + 1) * width, 16), width), 0:1]
            away = (sums[0, 0:1] + za[here].astype(f32) * sums[0, 1:2]) * share
            value = (rs_ref[layer, 0:1] * igs[layer, 0:1]) * (dz_ref[here] - live * away)
            da[here] = value.astype(bf16)

        if layer == 1:
            second["za"].start()
        now["wr"].wait()
        reducer.pump()

        def du_tile(tile):
            cols = pl.ds(pl.multiple_of(tile * 256, 256), 256)
            du = lax.dot_general(da[...], wr[cols], BESIDE, preferred_element_type=f32)
            d_ref[:, cols] = (du + d_ref[:, cols].astype(f32)).astype(bf16)

        if layer == 0:
            reduce_tiles(0)
        for part in range(4):
            pl.loop(part * (channels // 1024), (part + 1) * (channels // 1024))(du_tile)
            reducer.pump()
        if layer == 1:
            second["wr"].start()
    out = pltpu.make_async_copy(d_ref, grad_hbm, out_sem)
    out.start()
    reducer.drain()
    out.wait()


def backward(u0, u1, merged, zc, za, zb, r1, wr, ws, we, igs, ibs, ogs, obs, rs, rc, hwg, hbg, info, sums):
    size = lax.axis_size("dp")
    pixels, channels = u0.shape
    inner = za.shape[2]
    padded = zb.shape[1]
    width = (padded - pixels) // 2
    f32, bf16 = jnp.float32, jnp.bfloat16
    anywhere = pl.BlockSpec(memory_space=pl.ANY)
    vmem = pl.BlockSpec(memory_space=pltpu.VMEM)
    taps = ws.shape[1]
    reducer = Reducer(size, channels // TILE, taps)
    totals = reducer.totals(channels // TILE, taps)
    return pl.pallas_call(
        functools.partial(backward_kernel, size, reducer),
        out_shape=[
            jax.ShapeDtypeStruct((pixels, channels), bf16),
        ]
        + [jax.ShapeDtypeStruct(shape, bf16) for shape in totals],
        in_specs=[anywhere] * 10 + [vmem] * 10,
        out_specs=[anywhere] * 5,
        scratch_shapes=[
            pltpu.VMEM((channels, inner), bf16),
            pltpu.VMEM((9, inner, inner), bf16),
            pltpu.VMEM((inner, channels), bf16),
            pltpu.VMEM((2, pixels, channels), bf16),
            pltpu.VMEM((pixels, channels), bf16),
            pltpu.VMEM((pixels, channels), bf16),
            pltpu.VMEM((pixels, inner), bf16),
            pltpu.VMEM((padded, inner), bf16),
            pltpu.VMEM((padded, inner), bf16),
            pltpu.VMEM((pixels, inner), bf16),
            pltpu.VMEM((padded, channels), bf16),
            pltpu.VMEM((pixels, inner), f32),
            pltpu.VMEM((pixels, inner), bf16),
            pltpu.VMEM((reducer.half, TILE), f32),
            pltpu.VMEM((2, width, inner), bf16),
            pltpu.VMEM((2, 2, width, inner), bf16),
            pltpu.VMEM((4, size, 2, inner), f32),
            pltpu.VMEM((2, size, 2, channels // 2), f32),
            pltpu.VMEM((2, 8, channels), f32),
            pltpu.VMEM((2, 2, inner), f32),
            pltpu.VMEM((2, channels), f32),
            pltpu.SemaphoreType.DMA((6, size)),
            pltpu.SemaphoreType.DMA((6, size)),
            pltpu.SemaphoreType.DMA((2, 2)),
            pltpu.SemaphoreType.DMA((2, 2)),
            pltpu.SemaphoreType.DMA((10,)),
            pltpu.SemaphoreType.DMA,
        ]
        + reducer.scratch(),
        compiler_params=pltpu.CompilerParams(
            collective_id=2, has_side_effects=True, vmem_limit_bytes=63 * 2**20
        ),
    )(u0, u1, merged, zc, za, zb, r1, wr, ws, we, igs, ibs, ogs, obs, rs, rc, hwg, hbg, info, sums)


def pixel_info(pixel_mask, starts):
    width = pixel_mask.shape[1]
    columns = jnp.arange(width, dtype=jnp.int32)
    crop = jnp.sum((columns[:, None] >= starts[None, :]).astype(jnp.int32), axis=1)
    outside = jnp.full((1,), -1, jnp.int32)
    left = jnp.concatenate([outside, crop[:-1]]) == crop
    right = jnp.concatenate([crop[1:], outside]) == crop
    lane = jnp.arange(128, dtype=jnp.int32)
    first = jnp.where(lane == 0, pixel_mask[:, :, None], 0)
    links = jnp.where(lane == 1, left[:, None].astype(jnp.int32), 0)
    links = links + jnp.where(lane == 2, right[:, None].astype(jnp.int32), 0)
    return (first + links[None]).astype(jnp.float32).reshape(-1, 128)


def finish_kernel(
    head_cols,
    expand_in,
    spatial_in,
    reduce_in,
    small_in,
    grad_in,
    expand,
    spatial,
    reduce,
    gains,
    biases,
    outer,
    outer_b,
    head_w,
    head_b,
    grad,
):
    expand[...] = expand_in[...].astype(jnp.float32)
    spatial[...] = spatial_in[...].astype(jnp.float32)
    reduce[...] = reduce_in[...].astype(jnp.float32)
    grad[...] = grad_in[...]

    @pl.when(pl.program_id(0) == 0)
    def _():
        small = small_in[...].astype(jnp.float32)
        across = outer.shape[1] // TILE
        for k in range(2):
            head_w[:, k * TILE : (k + 1) * TILE] = small[k * head_cols : (k + 1) * head_cols]
        row, cut = 2 * head_cols, head_cols // 2
        one, other = small[row : row + 1, :cut], small[row : row + 1, cut:head_cols]
        head_b[...] = jnp.where(lax.axis_index("section") == 0, one, other)
        row += 8
        gains[...] = small[row : row + 2]
        biases[...] = small[row + 2 : row + 4]
        for k in range(across):
            cols = slice(k * TILE, (k + 1) * TILE)
            outer[:, cols] = small[row + 4 + k : row + 5 + k]
            outer_b[:, cols] = small[row + 4 + across + k : row + 5 + across + k]


def finish(expand, spatial, reduce, small, grad, head_cols):
    steps = 2
    channels = expand.shape[1]

    def rows(x, kind):
        block = pl.BlockSpec((x.shape[0] // steps, x.shape[1]), lambda i: (i, 0))
        return block, jax.ShapeDtypeStruct(x.shape, kind)

    def whole(*shape):
        return pl.BlockSpec(shape, lambda i: (0, 0)), jax.ShapeDtypeStruct(shape, jnp.float32)

    ins = [rows(x, x.dtype)[0] for x in (expand, spatial, reduce)]
    ins += [pl.BlockSpec((128, TILE), lambda i: (0, 0)), rows(grad, grad.dtype)[0]]
    outs = [rows(x, jnp.float32) for x in (expand, spatial, reduce)]
    outs += [whole(2, TILE), whole(2, TILE), whole(1, channels), whole(1, channels)]
    outs += [whole(head_cols, 2 * TILE), whole(1, head_cols // 2), rows(grad, grad.dtype)]
    return pl.pallas_call(
        functools.partial(finish_kernel, head_cols),
        grid=(steps,),
        in_specs=ins,
        out_specs=[block for block, _ in outs],
        out_shape=[shape for _, shape in outs],
        compiler_params=pltpu.CompilerParams(vmem_limit_bytes=LIMIT),
    )(expand, spatial, reduce, small, grad)


def pick(array, index):
    return lax.dynamic_index_in_dim(array, index, 0, keepdims=False)


def local(
    canvases,
    crop_starts,
    pixel_mask,
    drop_bits,
    reduce_weight,
    spatial_weight,
    expand_weight,
    inner_gain,
    inner_bias,
    outer_gain,
    outer_bias,
    head_weight,
    head_bias,
    head_cotangent,
):
    section = lax.axis_index("section")
    first = section == 0
    rows, width, channels = canvases.shape[1:]
    head_cols = head_weight.shape[1]
    pixels = rows * width
    flat = canvases.reshape(pixels, channels)
    mask = pick(pixel_mask, section)
    info = pixel_info(mask, pick(crop_starts, section))
    heads, hwg, hbg, igs, ibs, ogs, obs, rs, rc, info, sums, merged, u1, zc, za, zb, r1, wr, ws, we = forward(
        flat,
        drop_bits,
        jnp.swapaxes(head_cotangent, 2, 3),
        reduce_weight[0],
        spatial_weight[0],
        expand_weight[0],
        inner_gain[0],
        inner_bias[0],
        outer_gain,
        outer_bias,
        head_weight.T,
        head_bias[None],
        info,
        mask.astype(jnp.float32),
    )
    grad, expand_total, spatial_total, reduce_total, small = backward(
        flat, u1, merged, zc, za, zb, r1, wr, ws, we, igs, ibs, ogs, obs, rs, rc, hwg, hbg, info, sums
    )
    expand, spatial, reduce, gains, biases, outer, outer_b, head_w, head_b, grad = finish(
        expand_total.reshape(TILE, channels),
        spatial_total.reshape(-1, TILE),
        reduce_total.reshape(channels, TILE),
        small.reshape(-1, TILE),
        grad,
        head_cols,
    )
    return (
        jnp.swapaxes(heads, 1, 2)[None],
        grad.reshape(1, rows, width, channels),
        reduce[None],
        spatial.reshape(1, -1, TILE, TILE),
        expand[None],
        gains[None],
        biases[None],
        outer,
        outer_b,
        head_w.T,
        head_b.reshape(-1),
    )


def solution(mesh):
    placed = (
        P("section", "dp", None, None),
        P(),
        P(None, "dp", None),
        P(None, "dp", None, None),
        P("section", None, None),
        P("section", None, None, None),
        P("section", None, None),
        P("section", None, None),
        P("section", None, None),
        P("section", None),
        P("section", None),
        P(),
        P(),
        P(None, "dp", None, None),
    )
    return jax.shard_map(
        local,
        mesh=mesh,
        in_specs=placed,
        out_specs=(
            P("section", "dp", None, None),
            P("section", "dp", None, None),
            P("section", None, None),
            P("section", None, None, None),
            P("section", None, None),
            P("section", None, None),
            P("section", None, None),
            P("section", None),
            P("section", None),
            P("section", None),
            P("section"),
        ),
        check_vma=False,
    )
```

```python
import functools
import math

import jax
import jax.numpy as jnp
from jax import lax
from jax.experimental import pallas as pl
from jax.experimental.pallas import tpu as pltpu
from jax.sharding import PartitionSpec as P

TASKS = 3
HEAD_OUT = 16

EPS = 1e-05
SOFT = 0.05
SHARP = 0.1
LEVELS = 1024.0
ACROSS = (((0,), (0,)), ((), ()))
BESIDE = (((1,), (1,)), ((), ()))
MESH = pl.DeviceIdType.MESH
TILE = 512
LIMIT = 56 * 2**20


def grid_of(size):
    side = math.isqrt(size // 4)
    assert side * side * 4 == size
    return (4, side, side)


class Reducer:
    PACE = 3
    BETWEEN = (7, 9, 6)

    def __init__(self, size, across, taps):
        self.size = size
        nz, ny, nx = grid_of(size)
        self.strides = {}
        for axis, count, stride in (("x", nx, 1), ("y", ny, nx), ("z", nz, nx * ny)):
            for level in range(count.bit_length() - 1):
                self.strides[axis + str(level)] = stride << level
        later = [bit for bit in self.strides if bit[1] != "0"]
        self.orders = [
            [[a + "0" for a in order] + later for order in ("xyz", "yxz", third)]
            for third in ("zxy", "zyx")
        ]
        self.levels = len(self.strides)
        self.row_bits = [bit for bit in self.strides if bit[0] != "x"]
        self.x_bits = [bit for bit in self.strides if bit[0] == "x"]
        self.shape = (2,) * len(self.row_bits) + (16, TILE)
        self.half = 16 << len(self.row_bits)
        self.lines = 2 * self.half
        self.per_tile = TILE // self.lines
        self.counts = [across * self.per_tile, taps * self.per_tile, across * self.per_tile + 1]
        self.real = sum(self.counts)
        self.stages = 2 * self.levels + 3
        self.lag = 5 if self.levels <= 4 else 2
        self.plan(across, taps)

    def plan(self, across, taps):
        tiles = (across, taps, across)
        whole = sum(tiles) + sum(self.BETWEEN)
        assert whole % self.PACE == 0
        self.bursts, written = [], []
        place = base = 0
        for block in range(2):
            clock = block * whole
            for burst in range(3):
                if block == 1 and burst == 2:
                    clock -= self.BETWEEN[1] - 1
                groups = -(-self.counts[burst] // 3)
                ready = []
                for group in range(groups):
                    last = min((3 * group + 2) // self.per_tile, tiles[burst] - 1)
                    ready.append(-(-(clock + last) // self.PACE) - group)
                place = max([place] + ready)
                self.bursts.append((place, groups, base, self.counts[burst]))
                for unit in range(self.counts[burst]):
                    written.append(clock + min(unit // self.per_tile, tiles[burst] - 1))
                place += groups
                base += self.counts[burst]
                clock += tiles[burst] + self.BETWEEN[burst]
        self.last = self.PACE * (place - 1)
        reduced = []
        for place, groups, _, count in self.bursts:
            for unit in range(count):
                reduced.append(self.PACE * (place + unit // 3) + self.lag * (self.levels + 1))
        self.slots = 1
        while any(
            reduced[unit] >= written[unit + self.slots] for unit in range(len(written) - self.slots)
        ):
            self.slots += 1

    def scratch(self):
        units, bf16 = 2 * self.real, jnp.bfloat16
        return [
            pltpu.VMEM((self.slots, 2) + self.shape, bf16),
            pltpu.VMEM((units,) + self.shape, bf16),
            pltpu.VMEM((units,) + self.shape, bf16),
            pltpu.SemaphoreType.DMA((units, 2)),
            pltpu.SemaphoreType.DMA((units, 2)),
            pltpu.SemaphoreType.DMA((units, 2 * self.levels)),
            pltpu.SemaphoreType.DMA((units, 2 * self.levels)),
        ]

    def totals(self, across, taps):
        tail = (self.per_tile, 2) + self.shape
        return [
            (self.per_tile, 2) + self.shape[:-1] + (across * TILE,),
            (taps,) + tail,
            (across,) + tail,
            (2,) + self.shape,
        ]

    def bind(self, total, scratch):
        self.total = total
        (
            self.ring,
            self.res,
            self.land,
            self.pair_send,
            self.pair_recv,
            self.send_sem,
            self.recv_sem,
        ) = scratch
        self.section, self.me = lax.axis_index("section"), lax.axis_index("dp")
        self.bit = {bit: (self.me // stride) % 2 for bit, stride in self.strides.items()}
        self.clock = 0

    def partner(self, bit):
        return (self.section, self.me + (1 - 2 * self.bit[bit]) * self.strides[bit])

    def slot(self, unit):
        if isinstance(unit, int):
            return unit % self.slots
        return lax.rem(unit, self.slots)

    def region(self, order, level, flip):
        place = {bit: self.bit[bit] for bit in order[:level]}
        if flip:
            place[order[level - 1]] = 1 - place[order[level - 1]]
        rows = tuple(place.get(bit, slice(None)) for bit in self.row_bits)
        cols, start, width = slice(None), 0, TILE
        for bit in self.x_bits:
            if bit in place:
                width //= 2
                start = start + place[bit] * width
                cols = pl.ds(pl.multiple_of(start, width), width)
        return rows + (slice(None), cols)

    def pair(self, unit):
        return pltpu.make_async_remote_copy(
            src_ref=self.ring.at[self.slot(unit), 1 - self.section],
            dst_ref=self.res.at[unit],
            send_sem=self.pair_send.at[unit, 1],
            recv_sem=self.pair_recv.at[unit, 0],
            device_id=(1 - self.section, self.me),
            device_id_type=MESH,
        )

    def acc(self, unit):
        return self.ring.at[self.slot(unit), self.section]

    def halve(self, unit, order, level):
        return pltpu.make_async_remote_copy(
            src_ref=self.acc(unit).at[self.region(order, level + 1, True)],
            dst_ref=self.land.at[(unit,) + self.region(order, level + 1, False)],
            send_sem=self.send_sem.at[unit, level],
            recv_sem=self.recv_sem.at[unit, level],
            device_id=self.partner(order[level]),
            device_id_type=MESH,
        )

    def halved(self, unit, order, level):
        self.halve(unit, order, level).wait()
        keep = self.region(order, level + 1, False)
        kept = self.acc(unit).at[keep]
        came = self.land.at[(unit,) + self.region(order, level + 1, True)]
        target = self.res.at[(unit,) + keep] if level == self.levels - 1 else kept
        total = kept[...].astype(jnp.float32) + came[...].astype(jnp.float32)
        target[...] = total.astype(jnp.bfloat16)

    def double(self, unit, order, level):
        ref = self.res.at[(unit,) + self.region(order, level + 1, False)]
        return pltpu.make_async_remote_copy(
            src_ref=ref,
            dst_ref=ref,
            send_sem=self.send_sem.at[unit, self.levels + level],
            recv_sem=self.recv_sem.at[unit, self.levels + level],
            device_id=self.partner(order[level]),
            device_id_type=MESH,
        )

    def places(self, index):
        expand, spatial, reduce, small = self.total
        tile, part = index // self.per_tile, index % self.per_tile
        across, taps = reduce.shape[0], spatial.shape[0]
        half = self.section
        inner = (slice(None),) * (len(self.shape) - 1)

        def in_expand():
            cols = tile * TILE if isinstance(tile, int) else pl.multiple_of(tile * TILE, TILE)
            return expand.at[(part, half) + inner + (pl.ds(cols, TILE),)]

        return [
            (0 <= tile < across if isinstance(tile, int) else tile < across, in_expand),
            (
                self.both(tile >= across, tile < across + taps),
                lambda: spatial.at[tile - across, part, half],
            ),
            (
                self.both(tile >= across + taps, index < self.real - 1),
                lambda: reduce.at[tile - across - taps, part, half],
            ),
            (index == self.real - 1, lambda: small.at[half]),
        ]

    @staticmethod
    def both(first, second):
        if isinstance(first, bool) and isinstance(second, bool):
            return first and second
        return jnp.logical_and(first, second)

    def final(self, unit, target):
        here = pltpu.make_async_copy(self.res.at[unit], target, self.pair_send.at[unit, 0])
        away = pltpu.make_async_remote_copy(
            src_ref=self.res.at[unit],
            dst_ref=target,
            send_sem=self.pair_send.at[unit, 0],
            recv_sem=self.pair_recv.at[unit, 1],
            device_id=(1 - self.section, self.me),
            device_id_type=MESH,
        )
        return here, away

    def owner(self, unit):
        if isinstance(unit, int):
            return self.section == 1 - unit // self.real, unit % self.real
        later = (unit >= self.real).astype(jnp.int32)
        return self.section == 1 - later, unit - later * self.real

    def finish(self, unit):
        mine, index = self.owner(unit)

        def send(place):
            pl.when(mine)(lambda: self.final(unit, place())[0].start())
            pl.when(jnp.logical_not(mine))(lambda: self.final(unit, place())[1].start())

        for wanted, place in self.places(index):
            if isinstance(wanted, bool):
                if wanted:
                    send(place)
            else:
                pl.when(wanted)(functools.partial(send, place))

    def finished(self, unit):
        mine, _ = self.owner(unit)
        here, away = self.final(unit, self.total[3].at[self.section])

        @pl.when(mine)
        def _():
            here.wait()
            away.wait_recv()

        pl.when(jnp.logical_not(mine))(away.wait_send)

    def step(self, number, unit, order):
        levels = self.levels
        if number == 0:
            self.pair(unit).start()
        elif number == 1:
            self.pair(unit).wait()
            acc = self.acc(unit)
            total = acc[...].astype(jnp.float32) + self.res[unit].astype(jnp.float32)
            acc[...] = total.astype(jnp.bfloat16)
            self.halve(unit, order, 0).start()
        elif number <= levels:
            self.halved(unit, order, number - 2)
            self.halve(unit, order, number - 1).start()
        elif number == levels + 1:
            self.halved(unit, order, levels - 1)
            self.double(unit, order, levels - 1).start()
        elif number <= 2 * levels:
            level = 2 * levels - number
            self.double(unit, order, level + 1).wait()
            self.double(unit, order, level).start()
        elif number == 2 * levels + 1:
            self.double(unit, order, 0).wait()
            self.finish(unit)
        else:
            self.finished(unit)

    def locate(self, group):
        for place, groups, base, count in self.bursts:
            at = group - place
            if 0 <= at < groups:
                return base + 3 * at, min(3, count - 3 * at)
        return None

    def tick(self, time):
        for number in reversed(range(self.stages)):
            when = time - self.lag * number
            if when % self.PACE:
                continue
            group = when // self.PACE
            place = self.locate(group)
            if place is not None:
                for slot in range(place[1]):
                    order = self.orders[group % 2][slot]
                    self.step(number, place[0] + slot, order)

    def pump(self, count=1):
        for _ in range(count):
            self.tick(self.clock)
            self.clock += 1

    def burst(self, number, tiles, put, extra=None):
        base = self.bursts[number][2]
        for tile in range(tiles):
            put(tile, base + tile * self.per_tile)
            if tile == tiles - 1 and extra is not None:
                extra(base + tiles * self.per_tile)
            self.pump()

    def drain(self):
        self.pump(self.last + self.lag * (self.stages - 1) + 1 - self.clock)


def sigmoid(v):
    return 0.5 + 0.5 * jnp.tanh(0.5 * v)


def silu_parts(v):
    sigma = sigmoid(v)
    return v * sigma, sigma * (1.0 + v * (1.0 - sigma))


def folded(x):
    return jnp.sum(x.reshape(x.shape[0] // 8, 8, x.shape[1]), axis=0)


class Exchange:
    def __init__(self, size, send_sem, recv_sem, edge_send, edge_recv):
        self.size = size
        self.section, self.me = lax.axis_index("section"), lax.axis_index("dp")
        self.send_sem, self.recv_sem = send_sem, recv_sem
        self.edge_send, self.edge_recv = edge_send, edge_recv

    def greet(self):
        barrier = pltpu.get_barrier_semaphore()
        for step in range(1, self.size):
            peer = (self.section, lax.rem(self.me + step, self.size))
            pl.semaphore_signal(barrier, inc=1, device_id=peer, device_id_type=MESH)
        other = (1 - self.section, self.me)
        pl.semaphore_signal(barrier, inc=1, device_id=other, device_id_type=MESH)

    def met(self):
        pl.semaphore_wait(pltpu.get_barrier_semaphore(), self.size)

    def copies(self, number, slots):
        return [
            pltpu.make_async_remote_copy(
                src_ref=slots.at[0],
                dst_ref=slots.at[step],
                send_sem=self.send_sem.at[number, step],
                recv_sem=self.recv_sem.at[number, step],
                device_id=(self.section, lax.rem(self.me + step, self.size)),
                device_id_type=MESH,
            )
            for step in range(1, self.size)
        ]

    def edges(self, number, first, last, landing):
        made = []
        for way, (ref, step) in enumerate(((first, self.size - 1), (last, 1))):
            made.append(
                pltpu.make_async_remote_copy(
                    src_ref=ref,
                    dst_ref=landing.at[1 - way],
                    send_sem=self.edge_send.at[number, way],
                    recv_sem=self.edge_recv.at[number, 1 - way],
                    device_id=(self.section, lax.rem(self.me + step, self.size)),
                    device_id_type=MESH,
                )
            )
        return made

    def start_edges(self, number, first, last, landing):
        up, down = self.edges(number, first, last, landing)
        pl.when(self.me > 0)(up.start)
        pl.when(self.me < self.size - 1)(down.start)

    def wait_edges(self, number, first, last, landing):
        up, down = self.edges(number, first, last, landing)
        pl.when(self.me > 0)(up.wait_send)
        pl.when(self.me > 0)(down.wait_recv)
        pl.when(self.me < self.size - 1)(down.wait_send)
        pl.when(self.me < self.size - 1)(up.wait_recv)


def forward_kernel(
    size,
    u_hbm,
    bits_hbm,
    cot_hbm,
    wr_hbm,
    ws_hbm,
    we_hbm,
    ig_ref,
    ib_ref,
    og_ref,
    ob_ref,
    hwt_ref,
    hb_ref,
    info_ref,
    mask_ref,
    heads_ref,
    hwg_ref,
    hbg_ref,
    igs,
    ibs,
    ogs,
    obs,
    rs_ref,
    rc_ref,
    info_out,
    sums_out,
    merged_hbm,
    u1_hbm,
    zc_hbm,
    za_hbm,
    zb_hbm,
    r1_hbm,
    wr_all,
    ws_all,
    we_all,
    wr,
    ws,
    we,
    u0,
    u1,
    a_ref,
    b_ref,
    e_ref,
    cat,
    r2,
    za,
    zb,
    zc,
    merged,
    bits,
    cot,
    edge,
    halo,
    live_halo,
    msg,
    msg_c,
    first_msg,
    stat,
    stat_c,
    part_sum,
    send_sem,
    recv_sem,
    edge_send,
    edge_recv,
    w_load,
    w_send,
    w_recv,
    w_out,
    in_sem,
    bit_sem,
    out_sem,
):
    link = Exchange(size, send_sem, recv_sem, edge_send, edge_recv)
    section, me = link.section, link.me
    pixels, channels = u0.shape
    inner = a_ref.shape[1]
    half = channels // 2
    rows, width = bits_hbm.shape[1], bits_hbm.shape[2]
    f32, bf16 = jnp.float32, jnp.bfloat16

    load_u = pltpu.make_async_copy(u_hbm, u0, in_sem.at[0])
    load_cot = pltpu.make_async_copy(cot_hbm.at[section], cot, in_sem.at[1])

    def load_bits(chunk):
        return pltpu.make_async_copy(
            bits_hbm.at[section, chunk], bits.at[chunk % 2], bit_sem.at[chunk % 2]
        )

    link.greet()
    load_u.start()

    weights = ((wr_hbm, wr, wr_all), (ws_hbm, ws, ws_all), (we_hbm, we, we_all))

    def local_load(kind):
        source, target, _ = weights[kind]
        return pltpu.make_async_copy(source, target.at[section], w_load.at[kind])

    def pushed(kind):
        source, target, _ = weights[kind]
        return pltpu.make_async_remote_copy(
            src_ref=source,
            dst_ref=target.at[section],
            send_sem=w_send.at[kind],
            recv_sem=w_recv.at[kind],
            device_id=(1 - section, me),
            device_id_type=MESH,
        )

    vectors = ((ig_ref, igs), (ib_ref, ibs), (og_ref, ogs), (ob_ref, obs))

    def pushed_vector(kind):
        source, target = vectors[kind]
        return pltpu.make_async_remote_copy(
            src_ref=source,
            dst_ref=target.at[section],
            send_sem=w_send.at[3 + kind],
            recv_sem=w_recv.at[3 + kind],
            device_id=(1 - section, me),
            device_id_type=MESH,
        )

    def save_weight(kind, layer):
        _, target, saved = weights[kind]
        return pltpu.make_async_copy(target.at[layer], saved.at[layer], w_out.at[kind, layer])

    local_load(0).start()
    load_cot.start()
    load_bits(0).start()
    load_bits(1).start()
    link.met()
    for kind in range(4):
        pushed_vector(kind).start()
    pushed(0).start()
    for source, target in vectors:
        target[section] = source[...]

    def need_weight(kind, layer):
        pl.when(section == layer)(local_load(kind).wait)
        pl.when(section != layer)(pushed(kind).wait_recv)
        save_weight(kind, layer).start()

    own = pl.ds(width, pixels)
    live_edges = (info_ref.at[pl.ds(0, width)], info_ref.at[pl.ds(pixels - width, width)])

    def drop_chunk(chunk):
        load_bits(chunk).wait()
        start = pl.multiple_of(chunk * width, 16)
        target = cot[chunk].astype(f32) * mask_ref[chunk : chunk + 1]
        task = lax.broadcasted_iota(jnp.int32, target.shape, 0) // HEAD_OUT
        parts = [jnp.where(task == k, target, 0.0).astype(bf16) for k in range(TASKS)]

        @pl.loop(0, channels // TILE)
        def _(tile):
            cols = pl.ds(pl.multiple_of(tile * TILE, TILE), TILE)
            table = hwt_ref[:, cols]
            signed = magnitude = weighted = None
            for part in parts:
                value = lax.dot_general(part, table, ACROSS, preferred_element_type=f32)
                square = value * value
                whole = square + SOFT * SOFT
                inverse = lax.rsqrt(whole)
                if signed is None:
                    signed, magnitude, weighted = value, whole * inverse, square * inverse
                else:
                    signed = signed + value
                    magnitude = magnitude + whole * inverse
                    weighted = weighted + square * inverse
            level = bits[chunk % 2, :, cols].astype(f32)
            reach = 0.25 / SHARP
            inside = reach * (signed / magnitude) + (
                reach * (1.0 - 1.0 / LEVELS) - (2.0 * reach / LEVELS) * level
            )
            value = 0.5 * signed + (0.5 * jnp.tanh(inside)) * weighted
            merged[pl.ds(start, width), cols] = value.astype(bf16)

        if chunk + 2 < rows:
            load_bits(chunk + 2).start()

    live_all = info_ref[:, 0:1]
    count_here = jnp.sum(live_all, axis=0, keepdims=True)
    share = 1.0 / count_here

    def column_stats(values):
        mean = jnp.sum(values * live_all, axis=0, keepdims=True) * share
        apart = values - mean
        return mean, jnp.sum(live_all * apart * apart, axis=0, keepdims=True)

    def counts(step):
        return first_msg[step, 2:3, 0:1]

    def combine(slots):
        number = counts(0)
        mean = slots[0, 0:1] * counts(0)
        spread = slots[0, 1:2]
        for step in range(1, size):
            number = number + counts(step)
            mean = mean + slots[step, 0:1] * counts(step)
            spread = spread + slots[step, 1:2]
        mean = mean / number
        for step in range(size):
            apart = slots[step, 0:1] - mean
            spread = spread + counts(step) * apart * apart
        return mean, lax.rsqrt(spread / number + EPS), number

    load_u.wait()
    load_cot.wait()
    first_msg[0, 2:3] = jnp.broadcast_to(count_here, (1, inner))
    first_msg[0, 3:4] = jnp.zeros((1, inner), f32)
    zc_out = za_out = zb_out = r1_out = None
    u1_out = pltpu.make_async_copy(u1, u1_hbm, out_sem.at[0])
    for layer in range(2):
        x_ref = (u0, u1)[layer]
        need_weight(0, layer)
        if layer == 0:
            local_load(1).start()
            local_load(2).start()
        slots = first_msg if layer == 0 else msg.at[0]

        @pl.loop(0, inner // 256)
        def _(tile):
            cols = pl.ds(pl.multiple_of(tile * 256, 256), 256)
            values = jnp.dot(x_ref[...], wr[layer, :, cols], preferred_element_type=f32)
            a_ref[:, cols] = values
            mean, spread = column_stats(values)
            slots[0, 0:1, cols] = mean
            slots[0, 1:2, cols] = spread

        if layer == 1:
            for copy in (za_out, zb_out, r1_out, zc_out):
                copy.wait()
            u1_out.start()
        sends = link.copies(3 * layer, slots)
        for copy in sends:
            copy.start()
        centre = slots[0, 0:1]
        edge[0] = (a_ref[0:width] - centre).astype(bf16)
        edge[1] = (a_ref[pixels - width : pixels] - centre).astype(bf16)
        a_edges = (edge.at[0], edge.at[1])
        a_halo = halo.at[2 * layer]
        link.start_edges(2 * layer, *a_edges, a_halo)
        if layer == 0:
            link.start_edges(4, *live_edges, live_halo)
            pushed(1).start()
            for kind in range(4):
                pushed_vector(kind).wait()
        if layer == 0:
            drop_chunk(0)
        drop_chunk(1 + 3 * layer)
        for copy in sends:
            copy.wait()
        if layer == 0:
            pushed(2).start()
        mean, inverse, number = combine(slots)
        stat[layer, 0:1], stat[layer, 1:2] = mean, inverse
        rs_ref[layer, 0:1] = inverse
        rs_ref[layer, 2:3] = jnp.broadcast_to(number, (1, inner))

        def first_act(row, values, inside):
            normed = (values - stat[layer, 0:1]) * stat[layer, 1:2]
            affine = normed * igs[layer, 0:1] + ibs[layer, 0:1]
            act = affine * sigmoid(affine)
            if inside is not None:
                act = jnp.where(inside, act, 0.0)
            here = pl.ds(pl.multiple_of(row * width, 16), width)
            masks = info_ref[0:width]
            cat[here, 0:inner] = (pltpu.roll(act, 1, 0) * masks[:, 1:2]).astype(bf16)
            cat[here, inner : 2 * inner] = act.astype(bf16)
            cat[here, 2 * inner : 3 * inner] = (
                pltpu.roll(act, width - 1, 0) * masks[:, 2:3]
            ).astype(bf16)
            return normed

        @pl.loop(0, rows)
        def _(row):
            here = pl.ds(pl.multiple_of(row * width, 16), width)
            za[here] = first_act(row + 1, a_ref[here], None).astype(bf16)

        link.wait_edges(2 * layer, *a_edges, a_halo)
        first_act(0, a_halo[0].astype(f32) + slots[1, 0:1], me > 0)
        first_act(rows + 1, a_halo[1].astype(f32) + slots[size - 1, 0:1], me < size - 1)

        za_out = pltpu.make_async_copy(za, za_hbm.at[layer], out_sem.at[1])
        r1_out = pltpu.make_async_copy(
            cat.at[:, pl.ds(inner, inner)], r1_hbm.at[layer], out_sem.at[2]
        )
        za_out.start()
        r1_out.start()
        need_weight(1, layer)
        slots = msg.at[1 + 2 * layer]

        @pl.loop(0, inner // 256)
        def _(tile):
            cols = pl.ds(pl.multiple_of(tile * 256, 256), 256)
            values = None
            for tap in range(3):
                table = ws[layer, 3 * tap : 3 * tap + 3, :, cols].reshape(3 * inner, 256)
                value = jnp.dot(
                    cat[tap * width : tap * width + pixels], table, preferred_element_type=f32
                )
                values = value if values is None else values + value
            b_ref[:, cols] = values
            mean, spread = column_stats(values)
            slots[0, 0:1, cols] = mean
            slots[0, 1:2, cols] = spread

        sends = link.copies(3 * layer + 1, slots)
        for copy in sends:
            copy.start()
        drop_chunk(2 + 3 * layer)
        for copy in sends:
            copy.wait()
        mean, inverse, _ = combine(slots)
        stat[layer, 2:3], stat[layer, 3:4] = mean, inverse
        rs_ref[layer, 1:2] = inverse

        @pl.loop(0, rows)
        def _(row):
            here = pl.ds(pl.multiple_of(row * width, 16), width)
            normed = (b_ref[here] - stat[layer, 2:3]) * stat[layer, 3:4]
            zb[pl.ds(pl.multiple_of((row + 1) * width, 16), width)] = normed.astype(bf16)
            affine = normed * igs[layer, 1:2] + ibs[layer, 1:2]
            r2[here] = (affine * sigmoid(affine)).astype(bf16)

        b_edges = (zb.at[pl.ds(width, width)], zb.at[pl.ds(pixels, width)])
        b_halo = halo.at[2 * layer + 1]
        link.start_edges(2 * layer + 1, *b_edges, b_halo)
        need_weight(2, layer)
        sends = []
        for side in range(2):
            slots = msg_c.at[layer, side]

            @pl.loop(0, half // 256)
            def _(tile):
                cols = pl.ds(pl.multiple_of(side * half + tile * 256, 256), 256)
                at = pl.ds(pl.multiple_of(tile * 256, 256), 256)
                values = jnp.dot(r2[...], we[layer, :, cols], preferred_element_type=f32)
                e_ref[:, cols] = values
                mean, spread = column_stats(values)
                slots[0, 0:1, at] = mean
                slots[0, 1:2, at] = spread

            sends += link.copies((2 if side == 0 else 7) + 3 * layer, slots)
            for copy in sends[-(size - 1) :]:
                copy.start()
        drop_chunk(3 + 3 * layer)
        if layer == 0:
            link.wait_edges(4, *live_edges, live_halo)
            info_out[own] = info_ref[...]
            info_out[0:width] = live_halo[0]
            info_out[pixels + width : pixels + 2 * width] = live_halo[1]
        if layer == 1:
            drop_chunk(7)
        link.wait_edges(2 * layer + 1, *b_edges, b_halo)
        for side, row in ((0, 0), (1, rows + 1)):
            zb[row * width : (row + 1) * width] = b_halo[side]
        zb_out = pltpu.make_async_copy(zb, zb_hbm.at[layer], out_sem.at[3])
        zb_out.start()
        for copy in sends:
            copy.wait()
        for side in range(2):
            cols = slice(side * half, (side + 1) * half)
            mean, inverse, _ = combine(msg_c.at[layer, side])
            stat_c[0:1, cols], stat_c[1:2, cols] = mean, inverse
            rc_ref[layer, :, cols] = inverse
        out_ref = (u1, u0)[layer]
        if layer == 1:
            part_sum[...] = jnp.zeros_like(part_sum)

        def last_act(chunk):
            tile, row = chunk // rows, chunk % rows
            here = pl.ds(pl.multiple_of(row * width, 16), width)
            cols = pl.ds(pl.multiple_of(tile * TILE, TILE), TILE)
            normed = (e_ref[here, cols] - stat_c[0:1, cols]) * stat_c[1:2, cols]
            zc[here, cols] = normed.astype(bf16)
            total = normed * ogs[layer, :, cols] + obs[layer, :, cols] + x_ref[here, cols].astype(f32)
            if layer == 0:
                out_ref[here, cols] = (total * sigmoid(total)).astype(bf16)
            else:
                act, slope = silu_parts(total)
                out_ref[here, cols] = act.astype(bf16)
                dt = merged[here, cols].astype(f32) * slope
                merged[here, cols] = dt.astype(bf16)
                part_sum[0, :, cols] += folded(dt)
                part_sum[1, :, cols] += folded(dt * normed)

        turns = rows * (channels // TILE)
        if layer == 0:
            pl.loop(0, turns)(last_act)
        else:
            sends = []
            for side in range(2):
                pl.loop(side * (turns // 2), (side + 1) * (turns // 2))(last_act)
                slots = msg_c.at[2, side]
                cols = slice(side * half, (side + 1) * half)
                slots[0, 0:1] = jnp.sum(part_sum[0, :, cols], axis=0, keepdims=True)
                slots[0, 1:2] = jnp.sum(part_sum[1, :, cols], axis=0, keepdims=True)
                sends += link.copies((6, 8)[side], slots)
                for copy in sends[-(size - 1) :]:
                    copy.start()
        zc_out = pltpu.make_async_copy(zc, zc_hbm.at[layer], out_sem.at[5])
        zc_out.start()

    pltpu.make_async_copy(merged, merged_hbm, out_sem.at[4]).start()

    bias_sum = None
    for row in range(rows):
        lines = pl.ds(row * width, width)
        heads_ref[row] = (
            lax.dot_general(hwt_ref[...], u0[lines], BESIDE, preferred_element_type=f32)
            + hb_ref[...].T
        )
        target = cot[row].astype(f32) * mask_ref[row : row + 1]
        lanes = jnp.sum(target, axis=1, keepdims=True)
        bias_sum = lanes if bias_sum is None else bias_sum + lanes
        part = jnp.dot(target.astype(bf16), u0[lines], preferred_element_type=f32)
        if row == 0:
            hwg_ref[...] = part
        else:
            hwg_ref[...] += part
    hbg_ref[...] = bias_sum

    for copy in sends:
        copy.wait()
    for side in range(2):
        found = msg_c[2, side, 0]
        for step in range(1, size):
            found = found + msg_c[2, side, step]
        sums_out[:, side * half : (side + 1) * half] = found
    for copy in (za_out, zb_out, r1_out, zc_out, u1_out):
        copy.wait()
    pltpu.make_async_copy(merged, merged_hbm, out_sem.at[4]).wait()
    for kind in range(3):
        pushed(kind).wait_send()
        for layer in range(2):
            save_weight(kind, layer).wait()


def forward(u, bits, cot, wr, ws, we, ig, ib, og, ob, hwt, hb, info, mask):
    size = lax.axis_size("dp")
    pixels, channels = u.shape
    inner = wr.shape[1]
    _, rows, head_cols, width = cot.shape
    f32, bf16 = jnp.float32, jnp.bfloat16
    padded = pixels + 2 * width
    anywhere = pl.BlockSpec(memory_space=pl.ANY)
    vmem = pl.BlockSpec(memory_space=pltpu.VMEM)

    def out(kind, *shape):
        return jax.ShapeDtypeStruct(shape, kind)

    return pl.pallas_call(
        functools.partial(forward_kernel, size),
        out_shape=[
            out(f32, rows, head_cols, width),
            out(f32, head_cols, channels),
            out(f32, head_cols, 1),
            out(f32, 2, 2, inner),
            out(f32, 2, 2, inner),
            out(f32, 2, 1, channels),
            out(f32, 2, 1, channels),
            out(f32, 2, 8, inner),
            out(f32, 2, 1, channels),
            out(f32, padded, 128),
            out(f32, 2, channels),
            out(bf16, pixels, channels),
            out(bf16, pixels, channels),
            out(bf16, 2, pixels, channels),
            out(bf16, 2, pixels, inner),
            out(bf16, 2, padded, inner),
            out(bf16, 2, padded, inner),
            out(bf16, 2, channels, inner),
            out(bf16, 2, 9, inner, inner),
            out(bf16, 2, inner, channels),
        ],
        in_specs=[anywhere] * 6 + [vmem] * 8,
        out_specs=[vmem] * 11 + [anywhere] * 9,
        scratch_shapes=[
            pltpu.VMEM((2, channels, inner), bf16),
            pltpu.VMEM((2, 9, inner, inner), bf16),
            pltpu.VMEM((2, inner, channels), bf16),
            pltpu.VMEM((pixels, channels), bf16),
            pltpu.VMEM((pixels, channels), bf16),
            pltpu.VMEM((pixels, inner), f32),
            pltpu.VMEM((pixels, inner), f32),
            pltpu.VMEM((pixels, channels), f32),
            pltpu.VMEM((padded, 3 * inner), bf16),
            pltpu.VMEM((pixels, inner), bf16),
            pltpu.VMEM((pixels, inner), bf16),
            pltpu.VMEM((padded, inner), bf16),
            pltpu.VMEM((pixels, channels), bf16),
            pltpu.VMEM((pixels, channels), bf16),
            pltpu.VMEM((2, width, channels), jnp.int32),
            pltpu.VMEM((rows, head_cols, width), bf16),
            pltpu.VMEM((2, width, inner), bf16),
            pltpu.VMEM((4, 2, width, inner), bf16),
            pltpu.VMEM((2, width, 128), f32),
            pltpu.VMEM((4, size, 2, inner), f32),
            pltpu.VMEM((3, 2, size, 2, channels // 2), f32),
            pltpu.VMEM((size, 4, inner), f32),
            pltpu.VMEM((2, 8, inner), f32),
            pltpu.VMEM((2, channels), f32),
            pltpu.VMEM((2, 8, channels), f32),
            pltpu.SemaphoreType.DMA((11, size)),
            pltpu.SemaphoreType.DMA((11, size)),
            pltpu.SemaphoreType.DMA((5, 2)),
            pltpu.SemaphoreType.DMA((5, 2)),
            pltpu.SemaphoreType.DMA((3,)),
            pltpu.SemaphoreType.DMA((7,)),
            pltpu.SemaphoreType.DMA((7,)),
            pltpu.SemaphoreType.DMA((3, 2)),
            pltpu.SemaphoreType.DMA((2,)),
            pltpu.SemaphoreType.DMA((2,)),
            pltpu.SemaphoreType.DMA((6,)),
        ],
        compiler_params=pltpu.CompilerParams(
            collective_id=1, has_side_effects=True, vmem_limit_bytes=LIMIT
        ),
    )(u, bits, cot, wr, ws, we, ig, ib, og, ob, hwt, hb, info, mask)


def backward_kernel(
    size,
    reducer,
    u0_hbm,
    u1_hbm,
    merged_hbm,
    zc_hbm,
    za_hbm,
    zb_hbm,
    r1_hbm,
    wr_all,
    ws_all,
    we_all,
    igs,
    ibs,
    ogs,
    obs,
    rs_ref,
    rc_ref,
    hwg_ref,
    hbg_ref,
    info_ref,
    sums_ref,
    grad_hbm,
    expand_hbm,
    spatial_hbm,
    reduce_hbm,
    small_hbm,
    wr,
    ws,
    we,
    u_ref,
    d_ref,
    zc,
    za,
    zb,
    r1,
    r2,
    wide,
    dz_ref,
    da,
    small,
    edge,
    halo,
    msg,
    msg_c,
    part_sum,
    sums,
    sums_c,
    send_sem,
    recv_sem,
    edge_send,
    edge_recv,
    in_sem,
    out_sem,
    *scratch,
):
    reducer.bind((expand_hbm, spatial_hbm, reduce_hbm, small_hbm), scratch)
    link = Exchange(size, send_sem, recv_sem, edge_send, edge_recv)
    section, me = link.section, link.me
    pixels, channels = d_ref.shape
    inner = da.shape[1]
    width = halo.shape[2]
    rows = pixels // width
    across = channels // TILE
    f32, bf16 = jnp.float32, jnp.bfloat16
    own = pl.ds(width, pixels)
    de, cat = wide.at[pl.ds(0, pixels)], wide.at[:, pl.ds(0, 3 * inner)]

    def loads(layer):
        return {
            "zc": pltpu.make_async_copy(zc_hbm.at[layer], zc, in_sem.at[0]),
            "za": pltpu.make_async_copy(za_hbm.at[layer], za, in_sem.at[1]),
            "zb": pltpu.make_async_copy(zb_hbm.at[layer], zb, in_sem.at[2]),
            "r1": pltpu.make_async_copy(r1_hbm.at[layer], r1, in_sem.at[3]),
            "wr": pltpu.make_async_copy(wr_all.at[layer], wr, in_sem.at[4]),
            "ws": pltpu.make_async_copy(ws_all.at[layer], ws, in_sem.at[5]),
            "we": pltpu.make_async_copy(we_all.at[layer], we, in_sem.at[6]),
            "u": pltpu.make_async_copy((u0_hbm, u1_hbm)[layer], u_ref.at[layer], in_sem.at[7 + layer]),
        }

    load_d = pltpu.make_async_copy(merged_hbm, d_ref, in_sem.at[9])
    first, second = loads(1), loads(0)
    load_d.start()
    first["zc"].start()
    link.greet()
    live_all = info_ref[own, 0:1]

    def put_tile(unit, make):
        @pl.loop(0, 2)
        def _(side):
            cols = pl.ds(pl.multiple_of(side * 256, 256), 256)
            value = make(side).astype(bf16)
            inside = (slice(None),) * len(reducer.shape)
            for part in range(reducer.per_tile):
                lines = value[part * reducer.lines : (part + 1) * reducer.lines]
                at = (reducer.slot(unit + part),) + inside + (cols,)
                reducer.ring[at] = lines.reshape((2,) + reducer.shape[:-1] + (256,))

    def column_sums(values):
        return jnp.sum(values, axis=0, keepdims=True)

    def total_of(slots):
        found = slots[0]
        for step in range(1, size):
            found = found + slots[step]
        return found

    def expand_tiles(layer):
        def put(tile, unit):
            def make(side):
                cols = pl.ds(pl.multiple_of(tile * TILE + side * 256, 256), 256)
                return lax.dot_general(r2[...], de[:, cols], ACROSS, preferred_element_type=f32)

            put_tile(unit, make)

        reducer.burst(3 * (1 - layer), across, put)

    def spatial_tiles(layer):
        def put(tap, unit):
            shift, side_step = tap // 3, tap % 3

            def make(side):
                at = pl.ds(pl.multiple_of(shift * width, 16), pixels)
                cols = pl.ds(pl.multiple_of(side_step * inner + side * 256, 256), 256)
                return lax.dot_general(r1[at], cat[own, cols], ACROSS, preferred_element_type=f32)

            put_tile(unit, make)

        reducer.burst(3 * (1 - layer) + 1, 9, put)

    def reduce_tiles(layer):
        def put(tile, unit):
            def make(side):
                cols = pl.ds(pl.multiple_of(side * 256, 256), 256)
                lines = pl.ds(pl.multiple_of(tile * TILE, TILE), TILE)
                return lax.dot_general(
                    u_ref[layer, :, lines], da[:, cols], ACROSS, preferred_element_type=f32
                )

            put_tile(unit, make)

        reducer.burst(3 * (1 - layer) + 2, across, put, functools.partial(small_unit, layer))

    def small_unit(layer, unit):
        half = channels // 2
        head_cols = hwg_ref.shape[0]
        small[...] = jnp.zeros_like(small)
        for k in range(2):
            at = layer * half + k * TILE
            small[k * head_cols : (k + 1) * head_cols] = hwg_ref[:, at : at + TILE]
        row = 2 * head_cols
        small[row : row + 1, 0:head_cols] = hbg_ref[...].T
        only = (me == 0).astype(f32)
        small[row + 8 : row + 9] = sums[0, 1:2] * only
        small[row + 9 : row + 10] = sums[1, 1:2] * only
        small[row + 10 : row + 11] = sums[0, 0:1] * only
        small[row + 11 : row + 12] = sums[1, 0:1] * only
        for k in range(across):
            cols = slice(k * TILE, (k + 1) * TILE)
            small[row + 12 + k : row + 13 + k] = sums_c[1:2, cols] * only
            small[row + 12 + across + k : row + 13 + across + k] = sums_c[0:1, cols] * only
        slot = reducer.slot(unit)
        blank = jnp.zeros(reducer.shape, bf16)
        reducer.ring[slot, 0] = small[0 : reducer.half].astype(bf16).reshape(reducer.shape)
        reducer.ring[slot, 1] = blank

    load_d.wait()
    for layer in (1, 0):
        now = (second, first)[layer]
        now["zc"].wait()
        if layer == 1:
            for name in ("we", "zb", "ws", "za", "r1", "wr", "u"):
                first[name].start()
            second["u"].start()
        if layer == 0:
            now["u"].wait()
            first["u"].wait()
        if layer == 0:
            part_sum[...] = jnp.zeros_like(part_sum)

        def dt_chunk(chunk):
            tile, row = chunk // rows, chunk % rows
            here = pl.ds(pl.multiple_of(row * width, 16), width)
            cols = pl.ds(pl.multiple_of(tile * TILE, TILE), TILE)
            normed = zc[here, cols].astype(f32)
            total = (
                normed * ogs[layer, :, cols]
                + obs[layer, :, cols]
                + u_ref[layer, here, cols].astype(f32)
            )
            _, slope = silu_parts(total)
            dt = d_ref[here, cols].astype(f32) * slope
            d_ref[here, cols] = dt.astype(bf16)
            part_sum[0, :, cols] += folded(dt)
            part_sum[1, :, cols] += folded(dt * normed)

        if layer == 1:
            sums_c[...] = sums_ref[...]
        else:
            sends = []
            for part in range(4):
                pl.loop(part * (rows * across // 4), (part + 1) * (rows * across // 4))(dt_chunk)
                if part % 2 == 1:
                    slots = msg_c.at[part // 2]
                    cols = slice(part // 2 * (channels // 2), (part // 2 + 1) * (channels // 2))
                    slots[0, 0:1] = column_sums(part_sum[0, :, cols])
                    slots[0, 1:2] = column_sums(part_sum[1, :, cols])
                    sends += link.copies((0, 3)[part // 2], slots)
                    for copy in sends[-(size - 1) :]:
                        copy.start()
                reducer.pump()
            reduce_tiles(1)
            for copy in sends:
                copy.wait()
            for side in range(2):
                cols = slice(side * (channels // 2), (side + 1) * (channels // 2))
                sums_c[:, cols] = total_of(msg_c.at[side])
        number = rs_ref[layer, 2:3, 0:1]
        share = 1.0 / number

        def de_chunk(chunk):
            row, tile = chunk // across, chunk % across
            here = pl.ds(pl.multiple_of(row * width, 16), width)
            cols = pl.ds(pl.multiple_of(tile * TILE, TILE), TILE)
            live = info_ref[pl.ds(pl.multiple_of((row + 1) * width, 16), width), 0:1]
            normed = zc[here, cols].astype(f32)
            away = (sums_c[0:1, cols] + normed * sums_c[1:2, cols]) * share
            scale = rc_ref[layer, :, cols] * ogs[layer, :, cols]
            value = scale * (d_ref[here, cols].astype(f32) - live * away)
            de[here, cols] = value.astype(bf16)

        for part in range(4):
            pl.loop(part * (rows * across // 4), (part + 1) * (rows * across // 4))(de_chunk)
            if layer == 0:
                reducer.pump()
        now["we"].wait()
        now["zb"].wait()
        slots = msg.at[2 * layer]

        for tile in range(inner // 256):
            cols = pl.ds(tile * 256, 256)
            dr2 = lax.dot_general(de[...], we[cols], BESIDE, preferred_element_type=f32)
            normed = zb[own, cols].astype(f32)
            act, slope = silu_parts(normed * igs[layer, 1:2, cols] + ibs[layer, 1:2, cols])
            r2[:, cols] = act.astype(bf16)
            dz = dr2 * slope
            dz_ref[:, cols] = dz
            slots[0, 0:1, cols] = column_sums(dz)
            slots[0, 1:2, cols] = column_sums(dz * normed)
            if layer == 0:
                reducer.pump()

        if layer == 1:
            link.met()
        sends = link.copies(3 * layer + 1, slots)
        for copy in sends:
            copy.start()
        edge[0] = dz_ref[0:width].astype(bf16)
        edge[1] = dz_ref[pixels - width : pixels].astype(bf16)
        edges = (edge.at[0], edge.at[1])
        landing = halo.at[layer]
        link.start_edges(layer, *edges, landing)
        if layer == 1:
            second["zc"].start()
            second["we"].start()
        expand_tiles(layer)
        for copy in sends:
            copy.wait()
        sums[1] = total_of(slots)

        def db_row(row, dz, inside):
            here = pl.ds(pl.multiple_of(row * width, 16), width)
            live = info_ref[here, 0:1]
            normed = zb[here].astype(f32)
            away = (sums[1, 0:1] + normed * sums[1, 1:2]) * share
            value = (rs_ref[layer, 1:2] * igs[layer, 1:2]) * (dz - live * away)
            if inside is not None:
                value = jnp.where(inside, value, 0.0)
            masks = info_ref[pl.ds(width, width), :]
            cat[here, 0:inner] = (pltpu.roll(value, width - 1, 0) * masks[:, 2:3]).astype(bf16)
            cat[here, inner : 2 * inner] = value.astype(bf16)
            cat[here, 2 * inner : 3 * inner] = (
                pltpu.roll(value, 1, 0) * masks[:, 1:2]
            ).astype(bf16)

        def own_db(row):
            db_row(row + 1, dz_ref[pl.ds(pl.multiple_of(row * width, 16), width)], None)

        pl.loop(0, rows // 2)(own_db)
        reducer.pump()
        pl.loop(rows // 2, rows)(own_db)
        reducer.pump()

        link.wait_edges(layer, *edges, landing)
        db_row(0, landing[0].astype(f32), me > 0)
        db_row(rows + 1, landing[1].astype(f32), me < size - 1)
        reducer.pump()

        if layer == 1:
            second["zb"].start()
        now["ws"].wait()
        now["za"].wait()
        slots = msg.at[2 * layer + 1]

        for tile in range(inner // 256):
            cols = pl.ds(tile * 256, 256)
            dr1 = None
            for tap in range(9):
                start = (2 - tap // 3) * width
                block = cat[start : start + pixels, (tap % 3) * inner : (tap % 3 + 1) * inner]
                value = lax.dot_general(block, ws[tap, cols], BESIDE, preferred_element_type=f32)
                dr1 = value if dr1 is None else dr1 + value
                if tap == 4:
                    reducer.pump()
            normed = za[:, cols].astype(f32)
            _, slope = silu_parts(normed * igs[layer, 0:1, cols] + ibs[layer, 0:1, cols])
            dz = dr1 * slope
            dz_ref[:, cols] = dz
            slots[0, 0:1, cols] = column_sums(dz)
            slots[0, 1:2, cols] = column_sums(dz * normed)
            reducer.pump()

        sends = link.copies(3 * layer + 2, slots)
        for copy in sends:
            copy.start()
        if layer == 1:
            second["ws"].start()
        now["r1"].wait()
        spatial_tiles(layer)
        for copy in sends:
            copy.wait()
        sums[0] = total_of(slots)
        if layer == 1:
            second["r1"].start()

        @pl.loop(0, rows)
        def _(row):
            here = pl.ds(pl.multiple_of(row * width, 16), width)
            live = info_ref[pl.ds(pl.multiple_of((row + 1) * width, 16), width), 0:1]
            away = (sums[0, 0:1] + za[here].astype(f32) * sums[0, 1:2]) * share
            value = (rs_ref[layer, 0:1] * igs[layer, 0:1]) * (dz_ref[here] - live * away)
            da[here] = value.astype(bf16)

        if layer == 1:
            second["za"].start()
        now["wr"].wait()
        reducer.pump()

        def du_tile(tile):
            cols = pl.ds(pl.multiple_of(tile * 256, 256), 256)
            du = lax.dot_general(da[...], wr[cols], BESIDE, preferred_element_type=f32)
            d_ref[:, cols] = (du + d_ref[:, cols].astype(f32)).astype(bf16)

        if layer == 0:
            reduce_tiles(0)
        for part in range(4):
            pl.loop(part * (channels // 1024), (part + 1) * (channels // 1024))(du_tile)
            reducer.pump()
        if layer == 1:
            second["wr"].start()
    out = pltpu.make_async_copy(d_ref, grad_hbm, out_sem)
    out.start()
    reducer.drain()
    out.wait()


def backward(u0, u1, merged, zc, za, zb, r1, wr, ws, we, igs, ibs, ogs, obs, rs, rc, hwg, hbg, info, sums):
    size = lax.axis_size("dp")
    pixels, channels = u0.shape
    inner = za.shape[2]
    padded = zb.shape[1]
    width = (padded - pixels) // 2
    f32, bf16 = jnp.float32, jnp.bfloat16
    anywhere = pl.BlockSpec(memory_space=pl.ANY)
    vmem = pl.BlockSpec(memory_space=pltpu.VMEM)
    taps = ws.shape[1]
    reducer = Reducer(size, channels // TILE, taps)
    totals = reducer.totals(channels // TILE, taps)
    return pl.pallas_call(
        functools.partial(backward_kernel, size, reducer),
        out_shape=[
            jax.ShapeDtypeStruct((pixels, channels), bf16),
        ]
        + [jax.ShapeDtypeStruct(shape, bf16) for shape in totals],
        in_specs=[anywhere] * 10 + [vmem] * 10,
        out_specs=[anywhere] * 5,
        scratch_shapes=[
            pltpu.VMEM((channels, inner), bf16),
            pltpu.VMEM((9, inner, inner), bf16),
            pltpu.VMEM((inner, channels), bf16),
            pltpu.VMEM((2, pixels, channels), bf16),
            pltpu.VMEM((pixels, channels), bf16),
            pltpu.VMEM((pixels, channels), bf16),
            pltpu.VMEM((pixels, inner), bf16),
            pltpu.VMEM((padded, inner), bf16),
            pltpu.VMEM((padded, inner), bf16),
            pltpu.VMEM((pixels, inner), bf16),
            pltpu.VMEM((padded, channels), bf16),
            pltpu.VMEM((pixels, inner), f32),
            pltpu.VMEM((pixels, inner), bf16),
            pltpu.VMEM((reducer.half, TILE), f32),
            pltpu.VMEM((2, width, inner), bf16),
            pltpu.VMEM((2, 2, width, inner), bf16),
            pltpu.VMEM((4, size, 2, inner), f32),
            pltpu.VMEM((2, size, 2, channels // 2), f32),
            pltpu.VMEM((2, 8, channels), f32),
            pltpu.VMEM((2, 2, inner), f32),
            pltpu.VMEM((2, channels), f32),
            pltpu.SemaphoreType.DMA((6, size)),
            pltpu.SemaphoreType.DMA((6, size)),
            pltpu.SemaphoreType.DMA((2, 2)),
            pltpu.SemaphoreType.DMA((2, 2)),
            pltpu.SemaphoreType.DMA((10,)),
            pltpu.SemaphoreType.DMA,
        ]
        + reducer.scratch(),
        compiler_params=pltpu.CompilerParams(
            collective_id=2, has_side_effects=True, vmem_limit_bytes=63 * 2**20
        ),
    )(u0, u1, merged, zc, za, zb, r1, wr, ws, we, igs, ibs, ogs, obs, rs, rc, hwg, hbg, info, sums)


def pixel_info(pixel_mask, starts):
    width = pixel_mask.shape[1]
    columns = jnp.arange(width, dtype=jnp.int32)
    crop = jnp.sum((columns[:, None] >= starts[None, :]).astype(jnp.int32), axis=1)
    outside = jnp.full((1,), -1, jnp.int32)
    left = jnp.concatenate([outside, crop[:-1]]) == crop
    right = jnp.concatenate([crop[1:], outside]) == crop
    lane = jnp.arange(128, dtype=jnp.int32)
    first = jnp.where(lane == 0, pixel_mask[:, :, None], 0)
    links = jnp.where(lane == 1, left[:, None].astype(jnp.int32), 0)
    links = links + jnp.where(lane == 2, right[:, None].astype(jnp.int32), 0)
    return (first + links[None]).astype(jnp.float32).reshape(-1, 128)


def finish_kernel(
    head_cols,
    expand_in,
    spatial_in,
    reduce_in,
    small_in,
    grad_in,
    expand,
    spatial,
    reduce,
    gains,
    biases,
    outer,
    outer_b,
    head_w,
    head_b,
    grad,
):
    expand[...] = expand_in[...].astype(jnp.float32)
    spatial[...] = spatial_in[...].astype(jnp.float32)
    reduce[...] = reduce_in[...].astype(jnp.float32)
    grad[...] = grad_in[...]

    @pl.when(pl.program_id(0) == 0)
    def _():
        small = small_in[...].astype(jnp.float32)
        across = outer.shape[1] // TILE
        for k in range(2):
            head_w[:, k * TILE : (k + 1) * TILE] = small[k * head_cols : (k + 1) * head_cols]
        row, cut = 2 * head_cols, head_cols // 2
        one, other = small[row : row + 1, :cut], small[row : row + 1, cut:head_cols]
        head_b[...] = jnp.where(lax.axis_index("section") == 0, one, other)
        row += 8
        gains[...] = small[row : row + 2]
        biases[...] = small[row + 2 : row + 4]
        for k in range(across):
            cols = slice(k * TILE, (k + 1) * TILE)
            outer[:, cols] = small[row + 4 + k : row + 5 + k]
            outer_b[:, cols] = small[row + 4 + across + k : row + 5 + across + k]


def finish(expand, spatial, reduce, small, grad, head_cols):
    steps = 2
    channels = expand.shape[1]

    def rows(x, kind):
        block = pl.BlockSpec((x.shape[0] // steps, x.shape[1]), lambda i: (i, 0))
        return block, jax.ShapeDtypeStruct(x.shape, kind)

    def whole(*shape):
        return pl.BlockSpec(shape, lambda i: (0, 0)), jax.ShapeDtypeStruct(shape, jnp.float32)

    ins = [rows(x, x.dtype)[0] for x in (expand, spatial, reduce)]
    ins += [pl.BlockSpec((128, TILE), lambda i: (0, 0)), rows(grad, grad.dtype)[0]]
    outs = [rows(x, jnp.float32) for x in (expand, spatial, reduce)]
    outs += [whole(2, TILE), whole(2, TILE), whole(1, channels), whole(1, channels)]
    outs += [whole(head_cols, 2 * TILE), whole(1, head_cols // 2), rows(grad, grad.dtype)]
    return pl.pallas_call(
        functools.partial(finish_kernel, head_cols),
        grid=(steps,),
        in_specs=ins,
        out_specs=[block for block, _ in outs],
        out_shape=[shape for _, shape in outs],
        compiler_params=pltpu.CompilerParams(vmem_limit_bytes=LIMIT),
    )(expand, spatial, reduce, small, grad)


def pick(array, index):
    return lax.dynamic_index_in_dim(array, index, 0, keepdims=False)


def local(
    canvases,
    crop_starts,
    pixel_mask,
    drop_bits,
    reduce_weight,
    spatial_weight,
    expand_weight,
    inner_gain,
    inner_bias,
    outer_gain,
    outer_bias,
    head_weight,
    head_bias,
    head_cotangent,
):
    section = lax.axis_index("section")
    first = section == 0
    rows, width, channels = canvases.shape[1:]
    head_cols = head_weight.shape[1]
    pixels = rows * width
    flat = canvases.reshape(pixels, channels)
    mask = pick(pixel_mask, section)
    info = pixel_info(mask, pick(crop_starts, section))
    heads, hwg, hbg, igs, ibs, ogs, obs, rs, rc, info, sums, merged, u1, zc, za, zb, r1, wr, ws, we = forward(
        flat,
        drop_bits,
        jnp.swapaxes(head_cotangent, 2, 3),
        reduce_weight[0],
        spatial_weight[0],
        expand_weight[0],
        inner_gain[0],
        inner_bias[0],
        outer_gain,
        outer_bias,
        head_weight.T,
        head_bias[None],
        info,
        mask.astype(jnp.float32),
    )
    grad, expand_total, spatial_total, reduce_total, small = backward(
        flat, u1, merged, zc, za, zb, r1, wr, ws, we, igs, ibs, ogs, obs, rs, rc, hwg, hbg, info, sums
    )
    expand, spatial, reduce, gains, biases, outer, outer_b, head_w, head_b, grad = finish(
        expand_total.reshape(TILE, channels),
        spatial_total.reshape(-1, TILE),
        reduce_total.reshape(channels, TILE),
        small.reshape(-1, TILE),
        grad,
        head_cols,
    )
    return (
        jnp.swapaxes(heads, 1, 2)[None],
        grad.reshape(1, rows, width, channels),
        reduce[None],
        spatial.reshape(1, -1, TILE, TILE),
        expand[None],
        gains[None],
        biases[None],
        outer,
        outer_b,
        head_w.T,
        head_b.reshape(-1),
    )


def solution(mesh):
    placed = (
        P("section", "dp", None, None),
        P(),
        P(None, "dp", None),
        P(None, "dp", None, None),
        P("section", None, None),
        P("section", None, None, None),
        P("section", None, None),
        P("section", None, None),
        P("section", None, None),
        P("section", None),
        P("section", None),
        P(),
        P(),
        P(None, "dp", None, None),
    )
    return jax.shard_map(
        local,
        mesh=mesh,
        in_specs=placed,
        out_specs=(
            P("section", "dp", None, None),
            P("section", "dp", None, None),
            P("section", None, None),
            P("section", None, None, None),
            P("section", None, None),
            P("section", None, None),
            P("section", None, None),
            P("section", None),
            P("section", None),
            P("section", None),
            P("section"),
        ),
        check_vma=False,
    )
```
